512 devices in a mesh: slab: 128 (over z, y, core), sub: 4 (over x).
Axes of the slice: x: 4, y: 8, z: 8, core: 2. Of those that a mesh axis runs over, the one named last changes fastest.
Arguments:
- positions: float32 [3, 2097152], P(None, ('slab', 'sub')), may hold values from -5 to 5
- motion: float32 [6, 2097152], P(None, ('slab', 'sub')), may hold values from -3 to 3
- radius: float32 [2097152], P(('slab', 'sub')), may hold values from 0.4 to 0.8
- liquid: float32 [2097152], P(('slab', 'sub')), may hold values from 0.05 to 0.4
- new_owner: int32 [16384], P(('slab', 'sub')), may hold values from 0 to 4095, as said below
- ghost_rows: int32 [3, 262144], P(None, ('slab', 'sub')), may hold values from 0 to 4095
- partner_tiles: int32 [2, 16384], P(None, ('slab', 'sub')), may hold values from 0 to 55
- live_pairs: int32 [16384], P(('slab', 'sub')), may hold values from 0 to 2
Outputs:
- contact_force: float32 [3, 2097152], P(None, ('slab', 'sub'))
- contact_torque: float32 [3, 2097152], P(None, ('slab', 'sub'))
- motion_next: float32 [6, 2097152], P(None, ('slab', 'sub'))
The draws below stay inside these ranges and needn't reach their ends.
Inputs may be any that keep to these rules, and one draw needn't show every extreme that they name: `new_owner`: within each sub column the entries form a permutation of the 32 * 128 block places; every block stays on its slab or moves to the slab just before or just after; at most 4 blocks of one device go to each neighbouring slab, and in every draw some device sends exactly 4 blocks to the next slab. `ghost_rows`: local particle indices after migration. `partner_tiles`: indices of candidate tiles of the same device.
All inputs are finite; a program needn't handle non-finite values.
Results may differ from the reference program's by a relative error of at most 0.0003.
Values sent between devices are 32-bit elements; how exact they have to be, the bound alone decides.
No kernel may reach another device: no remote copies, remote signals or barrier semaphores. Data moves between devices by JAX's collectives and lax.ppermute only.
A program may use at most 64 MiB of HBM per device.

```python
import math
import jax
import jax.numpy as jnp
from jax import lax

NB = 32
GHOST = 512
K = 2
CAP = 4
ROWS = 2097152
CAND_TILES = 56
N_SLAB = 128
N_SUB = 4


def draw_new_owner(key, part):
    key_moves, key_chosen, key_orders = jax.random.split(key, 3)
    moves = jax.random.randint(key_moves, (N_SUB, N_SLAB - 1), CAP // 2, CAP + 1).astype(jnp.int32)
    chosen = jax.random.randint(key_chosen, (N_SUB, 1), 0, N_SLAB - 1).astype(jnp.int32)
    moves = jnp.where(jnp.arange(N_SLAB - 1, dtype=jnp.int32)[None, :] == chosen, CAP, moves).astype(jnp.int32)
    empty_col = jnp.zeros((N_SUB, 1), jnp.int32)
    to_prev = jnp.concatenate([empty_col, moves], 1)
    to_next = jnp.concatenate([moves, empty_col], 1)
    order_keys = jax.random.split(key_orders, N_SUB * N_SLAB)
    orders = jax.vmap(lambda subkey: jax.random.permutation(subkey, NB))(order_keys)
    orders = orders.reshape(N_SUB, N_SLAB, NB).astype(jnp.int32)
    ranks = jnp.argsort(orders, axis=2).astype(jnp.int32)
    slab_ids = jnp.arange(N_SLAB, dtype=jnp.int32)[None, :, None]
    slot_ids = jnp.arange(NB, dtype=jnp.int32)[None, None, :]
    prev_count = to_prev[:, :, None]
    next_count = to_next[:, :, None]
    heading_prev = ranks < prev_count
    heading_next = (ranks >= prev_count) & (ranks < prev_count + next_count)
    prev_orders = jnp.concatenate([orders[:, :1], orders[:, :-1]], 1)
    prev_offset = jnp.concatenate([empty_col, to_prev[:, :-1]], 1)[:, :, None]
    slot_prev = jnp.take_along_axis(prev_orders, jnp.clip(prev_offset + ranks, 0, NB - 1), axis=2)
    next_orders = jnp.concatenate([orders[:, 1:], orders[:, -1:]], 1)
    slot_next = jnp.take_along_axis(next_orders, jnp.clip(ranks - prev_count, 0, NB - 1), axis=2)
    stay = slab_ids * NB + slot_ids
    target = jnp.where(heading_prev, (slab_ids - 1) * NB + slot_prev, jnp.where(heading_next, (slab_ids + 1) * NB + slot_next, stay))
    return target.transpose(1, 0, 2).reshape(-1).astype(jnp.int32)


def with_ends(entries, key, smallest, high):
    index_at = [jax.random.randint(jax.random.fold_in(key, axis), (), 0, length) for axis, length in enumerate(entries.shape)]
    main_axis = entries.shape.index(max(entries.shape))
    neighbour = index_at[:main_axis] + [(index_at[main_axis] + 1) % entries.shape[main_axis]] + index_at[main_axis + 1:]
    return entries.at[tuple(index_at)].set(smallest).at[tuple(neighbour)].set(high)


def block_levels(stream_key, extent, pieces, smallest, largest):
    factor_of = 1.0
    for dim, shards_of in pieces:
        steps = jax.random.uniform(jax.random.fold_in(jax.random.fold_in(stream_key, 6), dim), (shards_of,), jnp.float32, smallest / len(pieces), largest / len(pieces))
        factor_of = factor_of * jnp.repeat(jnp.exp(steps), extent[dim] // shards_of).reshape((-1,) + (1,) * (len(extent) - 1 - dim))
    return factor_of


def gaussian(key, extent, scale, bound, pieces=(), held_as=jnp.bfloat16):
    values = jax.random.normal(key, extent, jnp.float32) * scale
    if len(pieces) > 0:
        values = block_levels(key, extent, pieces, -0.22, 0.18) * values
    return jnp.clip(values, min=-bound, max=bound).astype(held_as)


def setup_inputs(seed: int = 0) -> dict:
    arg_keys = jax.random.split(jax.random.key(seed), 9)
    positions = gaussian(arg_keys[0], (3, ROWS), 1.0, 5.0, ((1, 512),), jnp.float32)
    motion = gaussian(arg_keys[1], (6, ROWS), 0.5, 3.0, ((1, 512),), jnp.float32)
    radius = jnp.clip(jnp.exp(math.log(0.8) - 0.6931472 * jax.random.uniform(arg_keys[2], (ROWS,), jnp.float32) ** block_levels(arg_keys[2], (ROWS,), ((0, 512),), -0.2, 0.2)), 0.4, 0.8)
    liquid = jnp.clip(jnp.exp(math.log(0.4) - 2.0794415 * jax.random.uniform(arg_keys[3], (ROWS,), jnp.float32) ** block_levels(arg_keys[3], (ROWS,), ((0, 512),), -0.2, 0.2)), 0.05, 0.4)
    new_owner = draw_new_owner(jax.random.fold_in(arg_keys[8], 71), 0)
    ghost_rows = with_ends(jax.random.randint(arg_keys[5], (3, GHOST * N_SLAB * N_SUB), 0, NB * 128), jax.random.fold_in(arg_keys[5], 1), 0, (NB * 128) - 1).astype(jnp.int32)
    partner_tiles = with_ends(jax.random.randint(arg_keys[6], (K, NB * N_SLAB * N_SUB), 0, CAND_TILES), jax.random.fold_in(arg_keys[6], 1), 0, CAND_TILES - 1).astype(jnp.int32)
    live_pairs = with_ends(jax.random.randint(arg_keys[7], (NB * N_SLAB * N_SUB,), 0, K + 1), jax.random.fold_in(arg_keys[7], 1), 0, K).astype(jnp.int32)
    return {"positions": positions, "motion": motion, "radius": radius, "liquid": liquid, "new_owner": new_owner, "ghost_rows": ghost_rows, "partner_tiles": partner_tiles, "live_pairs": live_pairs}


min_distance = 0.2
stiffness = 1.0
normal_damp = 0.5
shear_damp = 0.3
surface_tension = 2.0
rupture_scale = 1.0
time_step = 0.005

def cross_product(first, second):
    return jnp.stack([first[1] * second[2] - first[2] * second[1], first[2] * second[0] - first[0] * second[2], first[0] * second[1] - first[1] * second[0]])

def contact(center, others, live_mask):
    offset = others[0:3, None, :] - center[0:3, :, None]
    length = jnp.sqrt(lax.optimization_barrier(jnp.sum(offset * offset, axis=0)))
    normal = offset / jnp.maximum(length, min_distance)
    radius_own = center[9][:, None]
    radius_far = others[9][None, :]
    liquid_own = center[10][:, None]
    liquid_far = others[10][None, :]
    intersection = jnp.maximum(radius_own + radius_far - length, 0.0)
    reduced = radius_own * radius_far / (radius_own + radius_far)
    spread = jnp.sqrt(reduced * intersection)
    spins = radius_own[None] * center[6:9, :, None] + radius_far[None] * others[6:9, None, :]
    relative = others[3:6, None, :] - center[3:6, :, None] - cross_product(spins, normal)
    approach = lax.optimization_barrier(jnp.sum(relative * normal, axis=0))
    sliding = relative - approach[None] * normal
    pressure = stiffness * spread * intersection - normal_damp * spread * approach
    separation = jnp.maximum(length - radius_own - radius_far, 0.0)
    bridge_fill = jnp.maximum(1.0 - separation / (rupture_scale * (liquid_own + liquid_far)), 0.0)
    bridge = surface_tension * reduced * jnp.sqrt(liquid_own * liquid_far) * bridge_fill * bridge_fill
    shear = shear_damp * spread[None] * sliding * live_mask[None, None, :]
    pair_force = ((bridge - pressure) * live_mask[None, :])[None] * normal + shear
    pair_turn = cross_product(normal, shear)
    on_center = jnp.concatenate([lax.optimization_barrier(jnp.sum(pair_force, axis=2)), center[9][None, :] * lax.optimization_barrier(jnp.sum(pair_turn, axis=2))], 0)
    on_others = jnp.concatenate([-lax.optimization_barrier(jnp.sum(pair_force, axis=1)), others[9][None, :] * lax.optimization_barrier(jnp.sum(pair_turn, axis=1))], 0)
    return (on_center, on_others)

def device_forces(candidates, tiles, live_count):
    width = candidates.shape[1]
    partners = tiles.shape[0]
    local_tiles = tiles.shape[1]
    tile_view = candidates.reshape(11, width // 128, 128)
    turns = min(local_tiles, 16)
    group = local_tiles // turns

    def one_turn(turn, carry):
        own_sum, react_sum = carry
        first = (turn * group).astype(jnp.int32)
        center = lax.dynamic_slice_in_dim(tile_view, first, group, 1)
        partner_ids = lax.dynamic_slice_in_dim(tiles, first, group, 1).T.astype(jnp.int32)
        counts = lax.dynamic_slice_in_dim(live_count, first, group, 0)
        others = jnp.take(tile_view, partner_ids.reshape(-1), axis=1).reshape(11, group, partners * 128)
        live_mask = (jnp.arange(partners, dtype=jnp.int32)[None, :] < counts[:, None]).astype(jnp.float32)
        live_mask = jnp.repeat(live_mask, 128, axis=1)
        on_center, on_others = jax.vmap(contact, in_axes=(1, 1, 0))(center, others, live_mask)
        slots = first + jnp.arange(group, dtype=jnp.int32)
        own_sum = own_sum.at[:, slots].add(on_center.transpose(1, 0, 2))
        spread_back = on_others.reshape(group, 6, partners, 128).transpose(1, 0, 2, 3).reshape(6, group * partners, 128)
        react_sum = react_sum.at[:, partner_ids.reshape(-1)].add(spread_back)
        return (own_sum, react_sum)
    start = (jnp.zeros((6, local_tiles, 128), jnp.float32), jnp.zeros((6, width // 128, 128), jnp.float32))
    own_sum, react_sum = lax.fori_loop(0, turns, one_turn, start)
    return (own_sum.reshape(6, local_tiles * 128), react_sum.reshape(6, width))

def reference(positions, motion, radius, liquid, new_owner, ghost_rows, partner_tiles, live_pairs):
    slabs = N_SLAB
    subs = N_SUB
    per_dev = NB * 128
    states = jnp.concatenate([positions, motion, radius[None], liquid[None]], 0)
    blocks = states.reshape(11, slabs, subs, NB, 128).transpose(1, 2, 3, 0, 4)
    target = new_owner.reshape(slabs, subs, NB).astype(jnp.int32)
    sub_ids = jnp.arange(subs, dtype=jnp.int32)[None, :, None]
    moved = jnp.zeros_like(blocks).at[target // NB, sub_ids, target % NB].set(blocks)
    migrated = moved.transpose(0, 1, 3, 2, 4).reshape(slabs, subs, 11, per_dev)
    rows = ghost_rows.reshape(3, slabs, subs, GHOST).astype(jnp.int32)

    def pick_set(which):
        index = jnp.broadcast_to(rows[which][:, :, None, :], (slabs, subs, 11, GHOST))
        return jnp.take_along_axis(migrated, index, axis=3)
    ghosts_zero = pick_set(0)
    ghosts_one = pick_set(1)
    ghosts_two = pick_set(2)
    blank = jnp.zeros((1, subs, 11, GHOST), jnp.float32)
    from_prev = jnp.concatenate([blank, ghosts_one[:-1]], 0)
    from_next = jnp.concatenate([ghosts_zero[1:], blank], 0)
    shared = ghosts_two.transpose(0, 2, 1, 3).reshape(slabs, 11, subs * GHOST)
    shared = jnp.broadcast_to(shared[:, None], (slabs, subs, 11, subs * GHOST))
    candidates = jnp.concatenate([migrated, from_prev, from_next, shared], 3)
    width = candidates.shape[3]
    tiles = partner_tiles.reshape(K, slabs * subs, NB).transpose(1, 0, 2).astype(jnp.int32)
    live_count = live_pairs.reshape(slabs * subs, NB).astype(jnp.int32)
    own_sum, react_sum = lax.map(lambda item: device_forces(item[0], item[1], item[2]), (candidates.reshape(slabs * subs, 11, width), tiles, live_count))
    own_sum = own_sum.reshape(slabs, subs, 6, per_dev)
    react_sum = react_sum.reshape(slabs, subs, 6, width)
    totals = own_sum + react_sum[..., :per_dev]
    back_prev = react_sum[..., per_dev:per_dev + GHOST]
    back_next = react_sum[..., per_dev + GHOST:per_dev + 2 * GHOST]
    back_sub = react_sum[..., per_dev + 2 * GHOST:]
    blank_six = jnp.zeros((1, subs, 6, GHOST), jnp.float32)
    return_zero = jnp.concatenate([blank_six, back_next[:-1]], 0)
    return_one = jnp.concatenate([back_prev[1:], blank_six], 0)
    return_two = back_sub.reshape(slabs, subs, 6, subs, GHOST).sum(axis=1).transpose(0, 2, 1, 3)

    def add_back(acc, index, values):
        return acc.at[:, index].add(values)
    flat = totals.reshape(slabs * subs, 6, per_dev)
    for which, values in ((0, return_zero), (1, return_one), (2, return_two)):
        flat = jax.vmap(add_back)(flat, rows[which].reshape(slabs * subs, GHOST), values.reshape(slabs * subs, 6, GHOST))
    totals = flat.reshape(slabs, subs, 6, per_dev)
    radii = migrated[:, :, 9]
    mass = radii ** 3
    inertia = 0.4 * radii ** 5
    velocity = migrated[:, :, 3:6] + time_step * totals[:, :, 0:3] / mass[:, :, None]
    spin_next = migrated[:, :, 6:9] + time_step * totals[:, :, 3:6] / inertia[:, :, None]

    def flatten(array):
        return array.transpose(2, 0, 1, 3).reshape(array.shape[2], slabs * subs * per_dev)
    return (flatten(totals[:, :, 0:3]), flatten(totals[:, :, 3:6]), flatten(jnp.concatenate([velocity, spin_next], 2)))
```

```python
import functools

import jax
import jax.numpy as jnp
from jax import lax
from jax.experimental import pallas as pl
from jax.experimental.pallas import tpu as pltpu
from jax.sharding import PartitionSpec as P

min_distance = 0.2
stiffness = 1.0
normal_damp = 0.5
shear_damp = 0.3
surface_tension = 2.0
rupture_scale = 1.0
time_step = 0.005

LANES = 128
ROWS = 16
CAP = 4
FEATS = 16
MATS = 5

f32 = jnp.float32
bf16 = jnp.bfloat16
VMEM = pl.BlockSpec(memory_space=pltpu.VMEM)
SMEM = pl.BlockSpec(memory_space=pltpu.SMEM)
PARAMS = pltpu.CompilerParams(vmem_limit_bytes=40 * 1024 * 1024)


def split(value, parts):
    out = []
    for _ in range(parts - 1):
        high = value.astype(bf16)
        out.append(high)
        value = value - high.astype(f32)
    out.append(value.astype(bf16))
    return out


def dot_nn(left, right):
    return lax.dot_general(left, right, (((1,), (0,)), ((), ())), preferred_element_type=f32)


def dot_nt(left, right):
    return lax.dot_general(left, right, (((1,), (1,)), ((), ())), preferred_element_type=f32)


def pack_kernel(owner, positions, motion, radius, liquid, state, ahead, behind):
    here = lax.axis_index("slab")
    blocks = state.shape[0]
    ahead[...] = jnp.zeros_like(ahead)
    behind[...] = jnp.zeros_like(behind)
    count_ahead = jnp.int32(0)
    count_behind = jnp.int32(0)
    for block in range(blocks):
        columns = slice(block * LANES, (block + 1) * LANES)
        place = owner[block]
        state[block, 0:3, :] = positions[:, columns]
        state[block, 3:9, :] = motion[:, columns]
        state[block, 9:10, :] = radius[block : block + 1, :]
        state[block, 10:11, :] = liquid[block : block + 1, :]
        state[block, 11:16, :] = jnp.full((5, LANES), (place + 1).astype(f32), f32)
        slab = place // blocks
        goes_ahead = slab == here + 1
        goes_behind = slab == here - 1

        @pl.when(goes_ahead)
        def _():
            ahead[count_ahead] = state[block]

        @pl.when(goes_behind)
        def _():
            behind[count_behind] = state[block]

        count_ahead = jnp.minimum(count_ahead + goes_ahead.astype(jnp.int32), CAP - 1)
        count_behind = jnp.minimum(count_behind + goes_behind.astype(jnp.int32), CAP - 1)


def place_kernel(owner, state, low, high, rows, migrated, ghosts0, ghosts1, ghosts2):
    here = lax.axis_index("slab")
    blocks = state.shape[0]
    for block in range(blocks):
        place = owner[block]

        @pl.when(place // blocks == here)
        def _():
            migrated[place % blocks] = state[block]

    base = (here * blocks + 1).astype(f32)
    arrived = [low[slot] for slot in range(CAP)] + [high[slot] for slot in range(CAP)]
    tags = [jnp.broadcast_to(block[11:12, :], (ROWS, LANES)) - base for block in arrived]
    for slot in range(blocks):
        current = migrated[slot]
        for block, tag in zip(arrived, tags):
            current = jnp.where(tag == float(slot), block, current)
        migrated[slot] = current

    flat = migrated[...].reshape(blocks * ROWS, LANES)
    left = jnp.concatenate(split(flat, 3), axis=1)
    lane_ids = lax.broadcasted_iota(jnp.int32, (LANES, LANES), 0)
    for which, ghosts in enumerate((ghosts0, ghosts1, ghosts2)):
        for tile in range(ghosts.shape[0]):
            index = rows[which : which + 1, tile * LANES : (tile + 1) * LANES]
            hot = jnp.where(lane_ids == index % LANES, 1.0, 0.0).astype(bf16)
            picked = dot_nn(left, jnp.concatenate([hot, hot, hot], axis=0))
            source = jnp.broadcast_to(index // LANES, (ROWS, LANES))
            total = jnp.zeros((ROWS, LANES), f32)
            for block in range(blocks):
                total = jnp.where(source == block, picked[block * ROWS : (block + 1) * ROWS], total)
            ghosts[tile] = total


def cross(first, second):
    return [
        first[1] * second[2] - first[2] * second[1],
        first[2] * second[0] - first[0] * second[2],
        first[0] * second[1] - first[1] * second[0],
    ]


def recip(value):
    guess = pl.reciprocal(value, approx=True)
    return guess * (2.0 - value * guess)


def prepare(tile, scaled, feats, slot):
    rows = [tile[row : row + 1, :] for row in range(11)]
    place, velocity, spin = rows[0:3], rows[3:6], rows[6:9]
    radius, liquid = rows[9], rows[10]
    turn = [radius * part for part in spin]
    bond = radius * jnp.sqrt(surface_tension * liquid)
    one = jnp.ones((1, LANES), f32)
    zero = jnp.zeros((1, LANES), f32)
    scaled[slot] = jnp.concatenate(
        place + velocity + turn + [radius, liquid, bond, zero, zero, zero, zero], axis=0
    )
    features = jnp.concatenate(
        place + [one] + velocity + turn + cross(turn, place) + cross(place, velocity), axis=0
    )
    feats[slot] = jnp.concatenate(split(features, 3), axis=0)


def add_pair(first, second, scaled, feats, sums, coefs):
    near = scaled[first].T
    far = scaled[second]
    far_rows = [far[row : row + 1, :] for row in range(12)]
    step = 16
    for start in range(0, LANES, step):
        center = near[start : start + step]
        col = [center[:, row : row + 1] for row in range(12)]
        offset = [far_rows[row] - col[row] for row in range(3)]
        moving = [far_rows[row] - col[row] for row in range(3, 6)]
        turning = [far_rows[row] + col[row] for row in range(6, 9)]
        square = offset[0] * offset[0] + offset[1] * offset[1] + offset[2] * offset[2]
        along = offset[0] * moving[0] + offset[1] * moving[1] + offset[2] * moving[2]
        twist = offset[0] * turning[0] + offset[1] * turning[1] + offset[2] * turning[2]
        root = lax.rsqrt(jnp.maximum(square, 1e-30))
        length = square * root
        inverse = jnp.minimum(root, 1.0 / min_distance)
        radii = far_rows[9] + col[9]
        gap = length - radii
        overlap = jnp.maximum(-gap, 0.0)
        apart = jnp.maximum(gap, 0.0)
        over_radii = recip(radii)
        inner = far_rows[9] * col[9] * over_radii * overlap
        spread = inner * lax.rsqrt(jnp.maximum(inner, 1e-30))
        fill = jnp.maximum(1.0 - apart * recip(rupture_scale * (far_rows[10] + col[10])), 0.0)
        bridge = far_rows[11] * col[11] * over_radii * (fill * fill)
        approach = along * inverse
        shear = shear_damp * spread
        push = stiffness * overlap - (normal_damp - shear_damp) * approach
        shear_inv = shear * inverse
        shear_inv2 = shear_inv * inverse
        mats = [
            (bridge - spread * push) * inverse,
            shear,
            shear_inv,
            shear_inv2 * square,
            shear_inv2 * twist,
        ]
        for index, mat in enumerate(mats):
            high, low = split(mat, 2)
            coefs[index * LANES + start : index * LANES + start + step, 0:LANES] = high
            coefs[index * LANES + start : index * LANES + start + step, LANES:] = low
    far_feats = feats[second]
    own = dot_nt(jnp.concatenate([far_feats, far_feats], axis=1), coefs[...])
    own = own[0:FEATS] + own[FEATS : 2 * FEATS] + own[2 * FEATS :]
    near_feats = feats[first]
    own_base = pl.multiple_of(first * (MATS * FEATS), 16)
    far_base = pl.multiple_of(second * (MATS * FEATS), 16)
    for index in range(MATS):
        sums[pl.ds(own_base + index * FEATS, FEATS), :] += own[:, index * LANES : (index + 1) * LANES]
    for index in range(MATS):
        back = dot_nn(near_feats, coefs[index * LANES : (index + 1) * LANES, :])
        back = back[:, 0:LANES] + back[:, LANES:]
        back = back[0:FEATS] + back[FEATS : 2 * FEATS] + back[2 * FEATS :]
        if index == MATS - 1:
            back = -back
        sums[pl.ds(far_base + index * FEATS, FEATS), :] += back


def finish(group, sums, scaled):
    span = MATS * FEATS

    def total(mat, feat):
        return sums[pl.ds(group * 8 * span + mat * FEATS + feat, 8, stride=span), :]

    def own(row):
        return scaled[pl.ds(group * 8, 8), row, :]

    place = [own(row) for row in range(3)]
    velocity = [own(row) for row in range(3, 6)]
    turn = [own(row) for row in range(6, 9)]
    radius = own(9)
    s_place = [total(0, feat) for feat in range(3)]
    s_one = total(0, 3)
    c_one = total(1, 3)
    c_velocity = [total(1, feat) for feat in range(4, 7)]
    n_place = [total(2, feat) for feat in range(3)]
    n_one = total(2, 3)
    n_velocity = [total(2, feat) for feat in range(4, 7)]
    n_turn = [total(2, feat) for feat in range(7, 10)]
    n_turn_place = [total(2, feat) for feat in range(10, 13)]
    n_place_velocity = [total(2, feat) for feat in range(13, 16)]
    k_one = total(3, 3)
    k_turn = [total(3, feat) for feat in range(7, 10)]
    g_place = [total(4, feat) for feat in range(3)]
    g_one = total(4, 3)
    turn_place = cross(turn, place)
    place_velocity = cross(place, velocity)
    first = cross(turn, n_place)
    second = cross(n_turn, place)
    third = cross(n_place, velocity)
    fourth = cross(place, n_velocity)
    force = [
        (s_place[x] - place[x] * s_one)
        + (c_velocity[x] - velocity[x] * c_one)
        - (first[x] - turn_place[x] * n_one + n_turn_place[x] - second[x])
        for x in range(3)
    ]
    torque = [
        radius
        * (
            (n_place_velocity[x] - third[x] - fourth[x] + place_velocity[x] * n_one)
            - (turn[x] * k_one + k_turn[x])
            + (g_place[x] - place[x] * g_one)
        )
        for x in range(3)
    ]
    return force + torque


def pair_kernel(remote, partners, live, state, *rest):
    blocks = state.shape[0]
    if remote:
        buffers, rest = rest[:6], rest[6:]
        totals, returns = rest[0], rest[1:7]
        scaled, feats, sums, coefs, todo = rest[7:]
    else:
        totals, scaled, feats, sums, coefs, todo = rest
    tiles = scaled.shape[0]
    sums[...] = jnp.zeros_like(sums)
    for tile in range(blocks):
        prepare(state[tile], scaled, feats, tile)
    if remote:
        size = buffers[0].shape[0]
        for which, buffer in enumerate(buffers):
            for tile in range(size):
                prepare(buffer[tile], scaled, feats, blocks + which * size + tile)
        sub = lax.axis_index("sub")
        subs = lax.axis_size("sub")
    count = jnp.int32(0)
    for tile in range(blocks):
        for which in range(partners.shape[0]):
            partner = partners[which, tile]
            slot = partner
            if remote:
                shared = (partner - blocks) // size - 2
                shift = lax.rem(sub - shared + 2 * subs, subs)
                slot = jnp.where(shared >= 0, partner + (shift - shared) * size, partner)
                wanted = (which < live[tile]) & (partner >= blocks)
            else:
                wanted = (which < live[tile]) & (partner < blocks)
            todo[count] = tile * 64 + slot
            count = count + wanted.astype(jnp.int32)

    def one_pair(index, carry):
        entry = todo[index]
        add_pair(entry // 64, entry % 64, scaled, feats, sums, coefs)
        return carry

    lax.fori_loop(0, count, one_pair, 0)
    for group in range(tiles // 8):
        for row, value in enumerate(finish(group, sums, scaled)):
            if group < blocks // 8:
                totals[pl.ds(group * 64 + row, 8, stride=8), :] = value
            else:
                which = (group - blocks // 8) * 2
                for part in range(2):
                    returns[which + part][:, row, :] = value[part * size : (part + 1) * size]


def final_kernel(
    state, totals_near, totals_far, rows, ret0, ret1, sub0, sub1, sub2, sub3, force, torque, kicked
):
    blocks = state.shape[0]
    size = ret0.shape[0]
    lane_ids = lax.broadcasted_iota(jnp.int32, (LANES, LANES), 0)
    hots = []
    lefts = []
    for which in range(3):
        for tile in range(size):
            index = rows[which : which + 1, tile * LANES : (tile + 1) * LANES]
            hots.append(jnp.where(lane_ids == index % LANES, 1.0, 0.0).astype(bf16))
            if which == 0:
                value = ret0[tile]
            elif which == 1:
                value = ret1[tile]
            else:
                value = sub0[tile] + sub1[tile] + sub2[tile] + sub3[tile]
            high = value.astype(bf16).astype(f32)
            both = jnp.concatenate([high, value - high], axis=0)
            source = jnp.broadcast_to(index // LANES, (ROWS, LANES))
            lefts.append(
                jnp.concatenate(
                    [
                        jnp.where(source == block, both, 0.0).astype(bf16)
                        for block in range(blocks)
                    ],
                    axis=0,
                )
            )
    added = dot_nt(jnp.concatenate(lefts, axis=1), jnp.concatenate(hots, axis=1))
    row_ids = lax.broadcasted_iota(jnp.int32, (8, LANES), 0)
    for block in range(blocks):
        columns = slice(block * LANES, (block + 1) * LANES)
        extra = added[block * ROWS : block * ROWS + 8] + added[block * ROWS + 8 : block * ROWS + 16]
        part = slice(block * 8, block * 8 + 8)
        total = totals_near[part, :] + totals_far[part, :] + extra
        radius = state[block, 9:10, :]
        mass = radius * radius * radius
        inertia = 0.4 * mass * radius * radius
        weight = jnp.where(row_ids < 3, time_step / mass, time_step / inertia)
        force[:, columns] = total[0:3]
        torque[:, columns] = total[3:6]
        kicked[:, columns] = state[block, 3:9, :] + (total * weight)[0:6]


def shape(*dims, dtype=f32):
    return jax.ShapeDtypeStruct(dims, dtype)


def pair_scratch(tiles, pairs):
    return [
        pltpu.VMEM((tiles, ROWS, LANES), f32),
        pltpu.VMEM((tiles, 3 * FEATS, LANES), bf16),
        pltpu.VMEM((tiles * MATS * FEATS, LANES), f32),
        pltpu.VMEM((MATS * LANES, 2 * LANES), bf16),
        pltpu.SMEM((pairs + 1,), jnp.int32),
    ]


def body(positions, motion, radius, liquid, new_owner, ghost_rows, partner_tiles, live_pairs):
    per_dev = positions.shape[1]
    blocks = per_dev // LANES
    size = ghost_rows.shape[1] // LANES
    pairs = partner_tiles.shape[0] * blocks
    slabs = lax.axis_size("slab")
    subs = lax.axis_size("sub")
    up = [(i, i + 1) for i in range(slabs - 1)]
    down = [(i + 1, i) for i in range(slabs - 1)]
    around = [[(i, (i + d) % subs) for i in range(subs)] for d in range(subs)]
    against = [[(i, (i - d) % subs) for i in range(subs)] for d in range(subs)]

    state, ahead, behind = pl.pallas_call(
        pack_kernel,
        out_shape=(
            shape(blocks, ROWS, LANES),
            shape(CAP, ROWS, LANES),
            shape(CAP, ROWS, LANES),
        ),
        in_specs=[SMEM] + [VMEM] * 4,
        out_specs=(VMEM,) * 3,
        compiler_params=PARAMS,
        name="pack",
    )(
        new_owner,
        positions,
        motion,
        radius.reshape(blocks, LANES),
        liquid.reshape(blocks, LANES),
    )
    low = lax.ppermute(ahead, "slab", up)
    high = lax.ppermute(behind, "slab", down)
    migrated, ghosts0, ghosts1, ghosts2 = pl.pallas_call(
        place_kernel,
        out_shape=(shape(blocks, ROWS, LANES),) + (shape(size, ROWS, LANES),) * 3,
        in_specs=[SMEM] + [VMEM] * 4,
        out_specs=(VMEM,) * 4,
        compiler_params=PARAMS,
        name="place",
    )(new_owner, state, low, high, ghost_rows)
    before = lax.ppermute(ghosts1, "slab", up)
    after = lax.ppermute(ghosts0, "slab", down)
    shared = [ghosts2] + [lax.ppermute(ghosts2, "sub", around[d]) for d in range(1, subs)]
    totals_near = pl.pallas_call(
        functools.partial(pair_kernel, False),
        out_shape=shape(blocks * 8, LANES),
        in_specs=[SMEM, SMEM, VMEM],
        out_specs=VMEM,
        scratch_shapes=pair_scratch(blocks, pairs),
        compiler_params=PARAMS,
        cost_estimate=pl.CostEstimate(flops=60000000, bytes_accessed=400000, transcendentals=0),
        name="near_pairs",
    )(partner_tiles, live_pairs, migrated)
    far = pl.pallas_call(
        functools.partial(pair_kernel, True),
        out_shape=(shape(blocks * 8, LANES),) + (shape(size, 8, LANES),) * 6,
        in_specs=[SMEM, SMEM] + [VMEM] * 7,
        out_specs=(VMEM,) * 7,
        scratch_shapes=pair_scratch(blocks + 6 * size, pairs),
        compiler_params=PARAMS,
        cost_estimate=pl.CostEstimate(flops=60000000, bytes_accessed=400000, transcendentals=0),
        name="far_pairs",
    )(partner_tiles, live_pairs, migrated, before, after, *shared)
    totals_far, back_before, back_after = far[0], far[1], far[2]
    back_shared = far[3:]
    return0 = lax.ppermute(back_after, "slab", up)
    return1 = lax.ppermute(back_before, "slab", down)
    returned = [back_shared[0]] + [
        lax.ppermute(back_shared[d], "sub", against[d]) for d in range(1, subs)
    ]
    return tuple(
        pl.pallas_call(
            final_kernel,
            out_shape=(shape(3, per_dev), shape(3, per_dev), shape(6, per_dev)),
            in_specs=[VMEM] * 10,
            out_specs=(VMEM,) * 3,
            compiler_params=PARAMS,
            name="final",
        )(migrated, totals_near, totals_far, ghost_rows, return0, return1, *returned)
    )


def solution(mesh):
    return jax.shard_map(
        body,
        mesh=mesh,
        in_specs=(
            P(None, ("slab", "sub")),
            P(None, ("slab", "sub")),
            P(("slab", "sub")),
            P(("slab", "sub")),
            P(("slab", "sub")),
            P(None, ("slab", "sub")),
            P(None, ("slab", "sub")),
            P(("slab", "sub")),
        ),
        out_specs=(P(None, ("slab", "sub")), P(None, ("slab", "sub")), P(None, ("slab", "sub"))),
        check_vma=False,
    )
```

```python
import functools

import jax
import jax.numpy as jnp
from jax import lax
from jax.experimental import pallas as pl
from jax.experimental.pallas import tpu as pltpu
from jax.sharding import PartitionSpec as P

min_distance = 0.2
stiffness = 1.0
normal_damp = 0.5
shear_damp = 0.3
surface_tension = 2.0
rupture_scale = 1.0
time_step = 0.005

LANES = 128
ROWS = 16
CAP = 4
FEATS = 16
MATS = 5
PAIR_ROWS = 12
GROUP = 4

f32 = jnp.float32
bf16 = jnp.bfloat16
VMEM = pl.BlockSpec(memory_space=pltpu.VMEM)
SMEM = pl.BlockSpec(memory_space=pltpu.SMEM)
HBM = pl.BlockSpec(memory_space=pltpu.HBM)
PARAMS = pltpu.CompilerParams(vmem_limit_bytes=40 * 1024 * 1024)


def split(value, parts):
    out = []
    for _ in range(parts - 1):
        high = value.astype(bf16)
        out.append(high)
        value = value - high.astype(f32)
    out.append(value.astype(bf16))
    return out


def dot_nn(left, right):
    return lax.dot_general(left, right, (((1,), (0,)), ((), ())), preferred_element_type=f32)


def dot_nt(left, right):
    return lax.dot_general(left, right, (((1,), (1,)), ((), ())), preferred_element_type=f32)


def pack_kernel(
    owner, positions, motion, radius, liquid, state, ahead, behind, place, speed, size, wet, sems
):
    copies = [
        pltpu.make_async_copy(source, target, sems.at[index])
        for index, (source, target) in enumerate(
            [(positions, place), (motion, speed), (radius, size), (liquid, wet)]
        )
    ]
    for copy in copies:
        copy.start()
    here = lax.axis_index("slab")
    blocks = state.shape[0]
    ahead[...] = jnp.zeros_like(ahead)
    behind[...] = jnp.zeros_like(behind)
    for copy in copies:
        copy.wait()
    count_ahead = jnp.int32(0)
    count_behind = jnp.int32(0)
    for block in range(blocks):
        columns = slice(block * LANES, (block + 1) * LANES)
        target = owner[block]
        state[block, 0:3, :] = place[:, columns]
        state[block, 3:9, :] = speed[:, columns]
        state[block, 9:10, :] = size[block : block + 1, :]
        state[block, 10:11, :] = wet[block : block + 1, :]
        state[block, 11:16, :] = jnp.full((5, LANES), (target + 1).astype(f32), f32)
        slab = target // blocks
        goes_ahead = slab == here + 1
        goes_behind = slab == here - 1

        @pl.when(goes_ahead)
        def _():
            ahead[count_ahead] = state[block]

        @pl.when(goes_behind)
        def _():
            behind[count_behind] = state[block]

        count_ahead = jnp.minimum(count_ahead + goes_ahead.astype(jnp.int32), CAP - 1)
        count_behind = jnp.minimum(count_behind + goes_behind.astype(jnp.int32), CAP - 1)


def place_kernel(owner, state, low, high, rows, partners, live, to_prev, to_next, to_sub):
    here = lax.axis_index("slab")
    blocks = state.shape[0]
    for block in range(blocks):
        target = owner[block]

        @pl.when(target // blocks == here)
        def _():
            to_sub[target % blocks] = state[block]

    base = (here * blocks + 1).astype(f32)
    arrived = [low[slot] for slot in range(CAP)] + [high[slot] for slot in range(CAP)]
    tags = [jnp.broadcast_to(block[11:12, :], (ROWS, LANES)) - base for block in arrived]
    for slot in range(blocks):
        current = to_sub[slot]
        for block, tag in zip(arrived, tags):
            current = jnp.where(tag == float(slot), block, current)
        to_sub[slot] = current
        to_prev[slot] = current
        to_next[slot] = current

    flat = to_sub[0:blocks].reshape(blocks * ROWS, LANES)
    left = jnp.concatenate(split(flat, 3), axis=1)
    lane_ids = lax.broadcasted_iota(jnp.int32, (LANES, LANES), 0)
    code = jnp.concatenate(
        [
            jnp.where(live[...] > which, partners[which : which + 1, :], -1).astype(f32)
            for which in range(partners.shape[0])
        ],
        axis=0,
    )
    for which, message in enumerate((to_prev, to_next, to_sub)):
        for tile in range(message.shape[0] - blocks):
            index = rows[which : which + 1, tile * LANES : (tile + 1) * LANES]
            hot = jnp.where(lane_ids == index % LANES, 1.0, 0.0).astype(bf16)
            picked = dot_nn(left, jnp.concatenate([hot, hot, hot], axis=0))
            source = jnp.broadcast_to(index // LANES, (ROWS, LANES))
            total = jnp.zeros((ROWS, LANES), f32)
            for block in range(blocks):
                total = jnp.where(source == block, picked[block * ROWS : (block + 1) * ROWS], total)
            message[blocks + tile] = total
        message[blocks, 11 : 11 + partners.shape[0], 0:blocks] = code


def cross(first, second):
    return [
        first[1] * second[2] - first[2] * second[1],
        first[2] * second[0] - first[0] * second[2],
        first[0] * second[1] - first[1] * second[0],
    ]


def recip(value):
    guess = pl.reciprocal(value, approx=True)
    return guess * (2.0 - value * guess)


def scale(tile):
    radius, liquid = tile[9:10, :], tile[10:11, :]
    bond = radius * jnp.sqrt(surface_tension * liquid)
    zero = jnp.zeros((4, LANES), f32)
    return jnp.concatenate([tile[0:6, :], radius * tile[6:9, :], radius, liquid, bond, zero], axis=0)


def features(scaled):
    rows = [scaled[row : row + 1, :] for row in range(9)]
    place, velocity, turn = rows[0:3], rows[3:6], rows[6:9]
    one = jnp.ones((1, LANES), f32)
    values = jnp.concatenate(
        place + [one] + velocity + turn + cross(turn, place) + cross(place, velocity), axis=0
    )
    return jnp.concatenate(split(values, 3), axis=0)


def fill_spread(spread):
    rows = lax.broadcasted_iota(jnp.int32, (3 * ROWS, LANES), 0) % ROWS
    for row in range(PAIR_ROWS):
        spread[:, row * LANES : (row + 1) * LANES] = jnp.where(rows == row, 1.0, 0.0).astype(bf16)


def pair_scalars(near, far, spread, coefs):
    parts = jnp.concatenate(split(near, 3), axis=0)
    columns = lax.dot_general(
        parts, spread[...], (((0,), (0,)), ((), ())), preferred_element_type=f32
    )
    far_rows = [far[row : row + 1, :] for row in range(PAIR_ROWS)]
    step = 16
    for start in range(0, LANES, step):
        col = [
            columns[start : start + step, row * LANES : (row + 1) * LANES]
            for row in range(PAIR_ROWS)
        ]
        offset = [far_rows[row] - col[row] for row in range(3)]
        moving = [far_rows[row] - col[row] for row in range(3, 6)]
        turning = [far_rows[row] + col[row] for row in range(6, 9)]
        square = offset[0] * offset[0] + offset[1] * offset[1] + offset[2] * offset[2]
        along = offset[0] * moving[0] + offset[1] * moving[1] + offset[2] * moving[2]
        twist = offset[0] * turning[0] + offset[1] * turning[1] + offset[2] * turning[2]
        root = lax.rsqrt(jnp.maximum(square, 1e-30))
        length = square * root
        inverse = jnp.minimum(root, 1.0 / min_distance)
        radii = far_rows[9] + col[9]
        gap = length - radii
        overlap = jnp.maximum(-gap, 0.0)
        apart = jnp.maximum(gap, 0.0)
        over_radii = recip(radii)
        inner = far_rows[9] * col[9] * over_radii * overlap
        spread = inner * lax.rsqrt(jnp.maximum(inner, 1e-30))
        fill = jnp.maximum(1.0 - apart * recip(rupture_scale * (far_rows[10] + col[10])), 0.0)
        bridge = far_rows[11] * col[11] * over_radii * (fill * fill)
        approach = along * inverse
        shear = shear_damp * spread
        push = stiffness * overlap - (normal_damp - shear_damp) * approach
        shear_inv = shear * inverse
        shear_inv2 = shear_inv * inverse
        mats = [
            (bridge - spread * push) * inverse,
            shear,
            shear_inv,
            shear_inv2 * square,
            shear_inv2 * twist,
        ]
        for index, mat in enumerate(mats):
            high, low = split(mat, 2)
            coefs[index * LANES + start : index * LANES + start + step, 0:LANES] = high
            coefs[index * LANES + start : index * LANES + start + step, LANES:] = low


def add_own(first, far_feats, sums, coefs):
    own = dot_nt(jnp.concatenate([far_feats, far_feats], axis=1), coefs[...])
    own = own[0:FEATS] + own[FEATS : 2 * FEATS] + own[2 * FEATS :]
    base = pl.multiple_of(first * (MATS * FEATS), 16)
    for index in range(MATS):
        sums[pl.ds(base + index * FEATS, FEATS), :] += own[:, index * LANES : (index + 1) * LANES]


def add_back(second, near_feats, sums, coefs):
    base = pl.multiple_of(second * (MATS * FEATS), 16)
    for index in range(MATS):
        back = dot_nn(near_feats, coefs[index * LANES : (index + 1) * LANES, :])
        back = back[:, 0:LANES] + back[:, LANES:]
        back = back[0:FEATS] + back[FEATS : 2 * FEATS] + back[2 * FEATS :]
        if index == MATS - 1:
            back = -back
        sums[pl.ds(base + index * FEATS, FEATS), :] += back


def finish(group, sums, scaled):
    span = MATS * FEATS

    def total(mat, feat):
        return sums[pl.ds(group * 8 * span + mat * FEATS + feat, 8, stride=span), :]

    def own(row):
        return scaled[pl.ds(group * 8, 8), row, :]

    place = [own(row) for row in range(3)]
    velocity = [own(row) for row in range(3, 6)]
    turn = [own(row) for row in range(6, 9)]
    radius = own(9)
    s_place = [total(0, feat) for feat in range(3)]
    s_one = total(0, 3)
    c_one = total(1, 3)
    c_velocity = [total(1, feat) for feat in range(4, 7)]
    n_place = [total(2, feat) for feat in range(3)]
    n_one = total(2, 3)
    n_velocity = [total(2, feat) for feat in range(4, 7)]
    n_turn = [total(2, feat) for feat in range(7, 10)]
    n_turn_place = [total(2, feat) for feat in range(10, 13)]
    n_place_velocity = [total(2, feat) for feat in range(13, 16)]
    k_one = total(3, 3)
    k_turn = [total(3, feat) for feat in range(7, 10)]
    g_place = [total(4, feat) for feat in range(3)]
    g_one = total(4, 3)
    turn_place = cross(turn, place)
    place_velocity = cross(place, velocity)
    first = cross(turn, n_place)
    second = cross(n_turn, place)
    third = cross(n_place, velocity)
    fourth = cross(place, n_velocity)
    force = [
        (s_place[x] - place[x] * s_one)
        + (c_velocity[x] - velocity[x] * c_one)
        - (first[x] - turn_place[x] * n_one + n_turn_place[x] - second[x])
        for x in range(3)
    ]
    torque = [
        radius
        * (
            (n_place_velocity[x] - third[x] - fourth[x] + place_velocity[x] * n_one)
            - (turn[x] * k_one + k_turn[x])
            + (g_place[x] - place[x] * g_one)
        )
        for x in range(3)
    ]
    return force + torque


def near_kernel(
    partners, live, to_prev, to_next, to_sub, totals, scaled, feats, sums, spread, todo, *coefs
):
    own_tiles = to_sub.shape[0]
    size = own_tiles - partners.shape[1]
    blocks = own_tiles - size
    fill_spread(spread)
    sums[...] = jnp.zeros_like(sums)
    for tile in range(own_tiles):
        scaled[tile] = scale(to_sub[tile])
        feats[tile] = features(scaled[tile])
    for tile in range(size):
        scaled[own_tiles + tile] = scale(to_prev[blocks + tile])
        scaled[own_tiles + size + tile] = scale(to_next[blocks + tile])
    spare = scaled.shape[0] - 1
    for tile in range(own_tiles + 2 * size, spare + 1):
        scaled[tile] = jnp.ones((ROWS, LANES), f32)
    feats[spare] = features(scaled[spare])
    shared = blocks + (2 + lax.axis_index("sub")) * size
    count = jnp.int32(0)
    for tile in range(blocks):
        for which in range(partners.shape[0]):
            partner = partners[which, tile]
            mine = (partner >= shared) & (partner < shared + size)
            wanted = (which < live[tile]) & ((partner < blocks) | mine)
            slot = jnp.where(mine, partner - shared + blocks, partner)
            todo[count] = tile * 64 + slot
            count = count + wanted.astype(jnp.int32)

    for extra in range(GROUP):
        todo[count + extra] = spare * 64 + spare

    def some_pairs(index, carry):
        entries = [todo[index * GROUP + lane] for lane in range(GROUP)]
        entries = [(entry // 64, entry % 64) for entry in entries]
        for (first, second), coef in zip(entries, coefs):
            pair_scalars(scaled[first], scaled[second], spread, coef)
        for (first, second), coef in zip(entries, coefs):
            add_own(first, feats[second], sums, coef)
            add_back(second, feats[first], sums, coef)
        return carry

    lax.fori_loop(0, (count + GROUP - 1) // GROUP, some_pairs, 0)
    for group in range(scaled.shape[0] // 8):
        for row, value in enumerate(finish(group, sums, scaled)):
            totals[pl.ds(group * 64 + row, 8, stride=8), :] = value


def far_kernel(shared, partners, live, before, scaled, *rest):
    messages, rest = rest[:-8 - GROUP], rest[-8 - GROUP :]
    totals, sums, spread, picked, codes, heard, todo, sem = rest[:8]
    coefs = rest[8:]
    spare = scaled.shape[0] - 1
    fill_spread(spread)
    blocks = partners.shape[1]
    choices = partners.shape[0]
    size = messages[0].shape[0] - blocks
    for number, message in enumerate(messages):
        codes[number * choices : (number + 1) * choices, :] = message[
            blocks, 11 : 11 + choices, :
        ].astype(jnp.int32)
    copy = pltpu.make_async_copy(codes, heard, sem)
    copy.start()
    sums[...] = jnp.zeros_like(sums)
    copy.wait()
    sub = lax.axis_index("sub")
    subs = lax.axis_size("sub")
    count = jnp.int32(0)
    for number, message in enumerate(messages):
        if shared:
            sender = lax.rem(sub + subs - 1 - number, subs)
            theirs = blocks + (2 + sender) * size
            ours = blocks + (2 + sub) * size
            ghost = blocks
        else:
            theirs = blocks + number * size
            ours = blocks + (1 - number) * size
            ghost = blocks + (1 + number) * size

        start = count
        for tile in range(blocks):
            for which in range(choices):
                shift = partners[which, tile] - theirs
                wanted = (which < live[tile]) & (shift >= 0) & (shift < size)
                todo[count] = tile * 64 + blocks + shift
                count = count + wanted.astype(jnp.int32)
                shift = heard[number * choices + which, tile] - ours
                wanted = (shift >= 0) & (shift < size)
                todo[count] = (ghost + shift) * 64 + tile
                count = count + wanted.astype(jnp.int32)

        def pick(index, carry):
            picked[index] = scale(message[todo[index] % 64])
            return carry

        lax.fori_loop(start, count, pick, 0)
    for extra in range(GROUP):
        todo[count + extra] = spare * 64
        picked[count + extra] = scaled[spare]

    def some_pairs(index, carry):
        first = index * GROUP
        mine = [todo[first + lane] // 64 for lane in range(GROUP)]
        near = [picked[first + lane] for lane in range(GROUP)]
        for lane, coef in enumerate(coefs):
            pair_scalars(near[lane], scaled[mine[lane]], spread, coef)
        for lane, coef in enumerate(coefs):
            add_back(mine[lane], features(near[lane]), sums, coef)
        return carry

    lax.fori_loop(0, (count + GROUP - 1) // GROUP, some_pairs, 0)
    for group in range(scaled.shape[0] // 8):
        for row, value in enumerate(finish(group, sums, scaled)):
            part = pl.ds(group * 64 + row, 8, stride=8)
            totals[part, :] = before[part, :] + value


def final_kernel(state, totals, rows, force, torque, kicked):
    size = rows.shape[1] // LANES
    blocks = state.shape[0] - size
    lane_ids = lax.broadcasted_iota(jnp.int32, (LANES, LANES), 0)
    hots = []
    lefts = []
    for which in range(3):
        for tile in range(size):
            index = rows[which : which + 1, tile * LANES : (tile + 1) * LANES]
            hots.append(jnp.where(lane_ids == index % LANES, 1.0, 0.0).astype(bf16))
            ghost = blocks + (which + 1) % 3 * size + tile
            value = totals[ghost * 8 : ghost * 8 + 8, :]
            high = value.astype(bf16).astype(f32)
            both = jnp.concatenate([high, value - high], axis=0)
            source = jnp.broadcast_to(index // LANES, (ROWS, LANES))
            lefts.append(
                jnp.concatenate(
                    [
                        jnp.where(source == block, both, 0.0).astype(bf16)
                        for block in range(blocks)
                    ],
                    axis=0,
                )
            )
    added = dot_nt(jnp.concatenate(lefts, axis=1), jnp.concatenate(hots, axis=1))
    row_ids = lax.broadcasted_iota(jnp.int32, (8, LANES), 0)
    for block in range(blocks):
        columns = slice(block * LANES, (block + 1) * LANES)
        extra = added[block * ROWS : block * ROWS + 8] + added[block * ROWS + 8 : block * ROWS + 16]
        total = totals[block * 8 : block * 8 + 8, :] + extra
        radius = state[block, 9:10, :]
        mass = radius * radius * radius
        inertia = 0.4 * mass * radius * radius
        weight = jnp.where(row_ids < 3, time_step / mass, time_step / inertia)
        force[:, columns] = total[0:3]
        torque[:, columns] = total[3:6]
        kicked[:, columns] = state[block, 3:9, :] + (total * weight)[0:6]


def shape(*dims, dtype=f32):
    return jax.ShapeDtypeStruct(dims, dtype)


def body(positions, motion, radius, liquid, new_owner, ghost_rows, partner_tiles, live_pairs):
    per_dev = positions.shape[1]
    blocks = per_dev // LANES
    size = ghost_rows.shape[1] // LANES
    choices = partner_tiles.shape[0]
    tiles = -(-(blocks + 3 * size) // 8) * 8
    slabs = lax.axis_size("slab")
    subs = lax.axis_size("sub")
    up = [(i, i + 1) for i in range(slabs - 1)]
    down = [(i + 1, i) for i in range(slabs - 1)]
    around = [[(i, (i + d) % subs) for i in range(subs)] for d in range(subs)]
    sums = pltpu.VMEM((tiles * MATS * FEATS, LANES), f32)
    spread = pltpu.VMEM((3 * ROWS, PAIR_ROWS * LANES), bf16)
    coefs = [pltpu.VMEM((MATS * LANES, 2 * LANES), bf16)] * GROUP
    cost = pl.CostEstimate(flops=60000000, bytes_accessed=400000, transcendentals=0)

    state, ahead, behind = pl.pallas_call(
        pack_kernel,
        out_shape=(
            shape(blocks, ROWS, LANES),
            shape(CAP, ROWS, LANES),
            shape(CAP, ROWS, LANES),
        ),
        in_specs=[SMEM] + [HBM] * 4,
        out_specs=(VMEM,) * 3,
        scratch_shapes=[
            pltpu.VMEM((3, per_dev), f32),
            pltpu.VMEM((6, per_dev), f32),
            pltpu.VMEM((blocks, LANES), f32),
            pltpu.VMEM((blocks, LANES), f32),
            pltpu.SemaphoreType.DMA((4,)),
        ],
        compiler_params=PARAMS,
        name="pack",
    )(
        new_owner,
        positions,
        motion,
        radius.reshape(blocks, LANES),
        liquid.reshape(blocks, LANES),
    )
    low = lax.ppermute(ahead, "slab", up)
    high = lax.ppermute(behind, "slab", down)
    to_prev, to_next, to_sub = pl.pallas_call(
        place_kernel,
        out_shape=(shape(blocks + size, ROWS, LANES),) * 3,
        in_specs=[SMEM] + [VMEM] * 6,
        out_specs=(VMEM,) * 3,
        compiler_params=PARAMS,
        name="place",
    )(new_owner, state, low, high, ghost_rows, partner_tiles, live_pairs.reshape(1, blocks))
    around_sub = [lax.ppermute(to_sub, "sub", around[d]) for d in range(1, subs)]
    from_prev = lax.ppermute(to_next, "slab", up)
    from_next = lax.ppermute(to_prev, "slab", down)
    totals, scaled = pl.pallas_call(
        near_kernel,
        out_shape=(shape(tiles * 8, LANES), shape(tiles, ROWS, LANES)),
        in_specs=[SMEM, SMEM] + [VMEM] * 3,
        out_specs=(VMEM, VMEM),
        scratch_shapes=[
            pltpu.VMEM((tiles, 3 * FEATS, LANES), bf16),
            sums,
            spread,
            pltpu.SMEM((choices * blocks + GROUP,), jnp.int32),
        ]
        + coefs,
        compiler_params=PARAMS,
        cost_estimate=cost,
        name="near_pairs",
    )(partner_tiles, live_pairs, to_prev, to_next, to_sub)
    for shared, messages in ((False, [from_prev, from_next]), (True, around_sub)):
        room = choices * blocks * (1 + len(messages))
        totals = pl.pallas_call(
            functools.partial(far_kernel, shared),
            out_shape=shape(tiles * 8, LANES),
            in_specs=[SMEM, SMEM] + [VMEM] * (2 + len(messages)),
            out_specs=VMEM,
            scratch_shapes=[
                sums,
                spread,
                pltpu.VMEM((room + GROUP, ROWS, LANES), f32),
                pltpu.VMEM((8, LANES), jnp.int32),
                pltpu.SMEM((8, LANES), jnp.int32),
                pltpu.SMEM((room + GROUP,), jnp.int32),
                pltpu.SemaphoreType.DMA(()),
            ]
            + coefs,
            compiler_params=PARAMS,
            cost_estimate=cost,
            name="sub_pairs" if shared else "slab_pairs",
        )(partner_tiles, live_pairs, totals, scaled, *messages)
    return tuple(
        pl.pallas_call(
            final_kernel,
            out_shape=(shape(3, per_dev), shape(3, per_dev), shape(6, per_dev)),
            in_specs=[VMEM] * 3,
            out_specs=(VMEM,) * 3,
            compiler_params=PARAMS,
            name="final",
        )(to_sub, totals, ghost_rows)
    )


def solution(mesh):
    return jax.shard_map(
        body,
        mesh=mesh,
        in_specs=(
            P(None, ("slab", "sub")),
            P(None, ("slab", "sub")),
            P(("slab", "sub")),
            P(("slab", "sub")),
            P(("slab", "sub")),
            P(None, ("slab", "sub")),
            P(None, ("slab", "sub")),
            P(("slab", "sub")),
        ),
        out_specs=(P(None, ("slab", "sub")), P(None, ("slab", "sub")), P(None, ("slab", "sub"))),
        check_vma=False,
    )
```

```python
import jax
import jax.numpy as jnp
from jax import lax
from jax.experimental import pallas as pl
from jax.experimental.pallas import tpu as pltpu
from jax.sharding import PartitionSpec as P

min_distance = 0.2
stiffness = 1.0
normal_damp = 0.5
shear_damp = 0.3
surface_tension = 2.0
rupture_scale = 1.0
time_step = 0.005

LANES = 128
ROWS = 16
CAP = 4
FEATS = 16
MATS = 5
WIDE_ROWS = (0, 1, 2, 9, 10, 11)
GROUP = 4
CHOICES = 2
GHOST_TILES = 4

f32 = jnp.float32
bf16 = jnp.bfloat16
VMEM = pl.BlockSpec(memory_space=pltpu.VMEM)
HBM = pl.BlockSpec(memory_space=pltpu.HBM)
PARAMS = pltpu.CompilerParams(vmem_limit_bytes=40 * 1024 * 1024)


def split(value, parts):
    out = []
    for _ in range(parts - 1):
        high = value.astype(bf16)
        out.append(high)
        value = value - high.astype(f32)
    out.append(value.astype(bf16))
    return out


def dot_nn(left, right):
    return lax.dot_general(left, right, (((1,), (0,)), ((), ())), preferred_element_type=f32)


def dot_nt(left, right):
    return lax.dot_general(left, right, (((1,), (1,)), ((), ())), preferred_element_type=f32)


def partners_of(here):
    odd = lax.rem(here, 2)
    return odd, here + 1 - 2 * odd, here - 1 + 2 * odd


def pack_kernel(*refs):
    sources, (state, swap_a, swap_b), (moving, sems) = refs[:8], refs[8:11], refs[-2:]
    goal, place, speed, size, wet, rows, partners, live = refs[11:-2]
    copies = [
        pltpu.make_async_copy(source, target, sems.at[index])
        for index, (source, target) in enumerate(zip(sources, refs[11:-2]))
    ]
    for copy in copies:
        copy.start()
    here = lax.axis_index("slab")
    _, slab_a, slab_b = partners_of(here)
    blocks = state.shape[0] - 1
    swap_a[...] = jnp.zeros_like(swap_a)
    swap_b[...] = jnp.zeros_like(swap_b)
    for copy in copies:
        copy.wait()
    count_a = jnp.int32(0)
    count_b = jnp.int32(0)
    for block in range(blocks):
        columns = slice(block * LANES, (block + 1) * LANES)
        target = goal[block]
        moving[block, 0:3, :] = place[:, columns]
        moving[block, 3:9, :] = speed[:, columns]
        moving[block, 9:10, :] = size[block : block + 1, :]
        moving[block, 10:11, :] = wet[block : block + 1, :]
        moving[block, 11:16, :] = jnp.full((5, LANES), (target + 1).astype(f32), f32)
        slab = target // blocks
        goes_a = slab == slab_a
        goes_b = slab == slab_b

        @pl.when(slab == here)
        def _():
            state[target % blocks] = moving[block]

        @pl.when(goes_a)
        def _():
            swap_a[count_a] = moving[block]

        @pl.when(goes_b)
        def _():
            swap_b[count_b] = moving[block]

        count_a = jnp.minimum(count_a + goes_a.astype(jnp.int32), CAP - 1)
        count_b = jnp.minimum(count_b + goes_b.astype(jnp.int32), CAP - 1)
    state[blocks] = jnp.zeros((ROWS, LANES), f32)
    tiles = rows.shape[1] // LANES
    for which in range(3):
        for tile in range(tiles):
            state[blocks, which * tiles + tile : which * tiles + tile + 1, :] = rows[
                which : which + 1, tile * LANES : (tile + 1) * LANES
            ].astype(f32)
    for which in range(partners.shape[0]):
        state[blocks, 12 + which : 13 + which, 0:blocks] = jnp.where(
            live[...] > which, partners[which : which + 1, :], -1
        ).astype(f32)


def ghost_index(extra, which, tile, tiles, odd):
    rows = [extra[other * tiles + tile : other * tiles + tile + 1, :] for other in range(3)]
    row = rows[2] if which == 2 else jnp.where(odd == which, rows[1], rows[0])
    return row.astype(jnp.int32)


def place_kernel(state, low, high, to_a, to_b, to_sub):
    here = lax.axis_index("slab")
    odd, _, _ = partners_of(here)
    blocks = state.shape[0] - 1
    size = to_sub.shape[0] - blocks
    extra = state[blocks]
    base = (here * blocks + 1).astype(f32)
    arrived = [low[slot] for slot in range(CAP)] + [high[slot] for slot in range(CAP)]
    tags = [jnp.broadcast_to(block[11:12, :], (ROWS, LANES)) - base for block in arrived]
    for slot in range(blocks):
        current = state[slot]
        for block, tag in zip(arrived, tags):
            current = jnp.where(tag == float(slot), block, current)
        to_sub[slot] = current
        to_a[slot] = current
        to_b[slot] = current

    flat = to_sub[0:blocks].reshape(blocks * ROWS, LANES)
    left = jnp.concatenate(split(flat, 3), axis=1)
    lane_ids = lax.broadcasted_iota(jnp.int32, (LANES, LANES), 0)
    for which, message in enumerate((to_a, to_b, to_sub)):
        for tile in range(message.shape[0] - blocks):
            index = ghost_index(extra, which, tile, size, odd)
            hot = jnp.where(lane_ids == index % LANES, 1.0, 0.0).astype(bf16)
            picked = dot_nn(left, jnp.concatenate([hot, hot, hot], axis=0))
            source = jnp.broadcast_to(index // LANES, (ROWS, LANES))
            total = jnp.zeros((ROWS, LANES), f32)
            for block in range(blocks):
                total = jnp.where(source == block, picked[block * ROWS : (block + 1) * ROWS], total)
            message[blocks + tile] = total
        message[blocks, 11:13, :] = extra[12:14, :]


def cross(first, second):
    return [
        first[1] * second[2] - first[2] * second[1],
        first[2] * second[0] - first[0] * second[2],
        first[0] * second[1] - first[1] * second[0],
    ]


def recip(value):
    guess = pl.reciprocal(value, approx=True)
    return guess * (2.0 - value * guess)


def dot_rows(first, second):
    return first[0] * second[0] + first[1] * second[1] + first[2] * second[2]


def scale(tile):
    radius, liquid = tile[9:10, :], tile[10:11, :]
    turn = radius * tile[6:9, :]
    bond = radius * jnp.sqrt(surface_tension * liquid)
    place = [tile[row : row + 1, :] for row in range(3)]
    along = dot_rows(place, [tile[row : row + 1, :] for row in range(3, 6)])
    twist = dot_rows(place, [turn[row : row + 1, :] for row in range(3)])
    one = jnp.ones((1, LANES), f32)
    return jnp.concatenate(
        [tile[0:6, :], turn, radius, rupture_scale * liquid, bond, along, one, twist, 0.0 * one],
        axis=0,
    )


def mirror(scaled):
    place, velocity, turn = scaled[0:3, :], scaled[3:6, :], scaled[6:9, :]
    along, one, twist, zero = [scaled[row : row + 1, :] for row in range(12, 16)]
    blank = jnp.broadcast_to(zero, (6, LANES))
    damp = normal_damp - shear_damp
    moving = jnp.concatenate([-velocity, -place, blank, one, along, zero, zero], axis=0)
    turning = jnp.concatenate(
        [-turn, blank[0:3], place, blank[0:3], zero, twist, -one, zero], axis=0
    )
    return jnp.concatenate([damp * moving, turning], axis=0)


def six(value, order):
    parts = split(value, 3)
    return jnp.concatenate([parts[index] for index in order], axis=0)


def features(scaled):
    rows = [scaled[row : row + 1, :] for row in range(9)]
    place, velocity, turn = rows[0:3], rows[3:6], rows[6:9]
    one = jnp.ones((1, LANES), f32)
    values = jnp.concatenate(
        place + [one] + velocity + turn + cross(turn, place) + cross(place, velocity), axis=0
    )
    return jnp.concatenate(split(values, 3), axis=0)


def fill_spread(spread):
    rows = lax.broadcasted_iota(jnp.int32, (6 * ROWS, LANES), 0)
    part = rows // ROWS
    first = (part == 0) | (part == 3) | (part == 5)
    for block, row in enumerate(WIDE_ROWS):
        hot = first & (rows % ROWS == row)
        spread[:, block * LANES : (block + 1) * LANES] = jnp.where(hot, 1.0, 0.0).astype(bf16)


def pair_scalars(near, far, far_mirror, spread, coefs):
    moving = six(far_mirror[0:ROWS], (0, 1, 2, 0, 1, 0))
    turning = six(far_mirror[ROWS:], (0, 1, 2, 0, 1, 0))
    columns = lax.dot_general(
        six(near, (0, 0, 0, 1, 1, 2)),
        jnp.concatenate([spread[...], moving, turning], axis=1),
        (((0,), (0,)), ((), ())),
        preferred_element_type=f32,
    )
    far_rows = [far[row : row + 1, :] for row in WIDE_ROWS]
    step = 16
    for start in range(0, LANES, step):
        col = [
            columns[start : start + step, block * LANES : (block + 1) * LANES] for block in range(8)
        ]
        offset = [far_rows[row] - col[row] for row in range(3)]
        along, twist = col[6], col[7]
        square = dot_rows(offset, offset)
        root = lax.rsqrt(jnp.maximum(square, 1e-30))
        inverse = jnp.minimum(root, 1.0 / min_distance)
        gap = square * root - (far_rows[3] + col[3])
        apart = jnp.maximum(gap, 0.0)
        overlap = apart - gap
        over_radii = recip(far_rows[3] + col[3])
        inner = far_rows[3] * col[3] * over_radii * overlap
        spread_pair = inner * lax.rsqrt(jnp.maximum(inner, 1e-30))
        fill = jnp.maximum(1.0 - apart * recip(far_rows[4] + col[4]), 0.0)
        bridge = far_rows[5] * col[5] * over_radii * (fill * fill)
        inverse1 = spread_pair * inverse
        inverse2 = inverse1 * inverse
        mats = [
            (bridge - spread_pair * (overlap - along * inverse)) * inverse,
            spread_pair,
            inverse1,
            inverse2 * square,
            inverse2 * twist,
        ]
        for index, mat in enumerate(mats):
            high, low = split(mat, 2)
            coefs[index * LANES + start : index * LANES + start + step, 0:LANES] = high
            coefs[index * LANES + start : index * LANES + start + step, LANES:] = low


def add_own(first, far_feats, sums, coefs):
    own = dot_nt(jnp.concatenate([far_feats, far_feats], axis=1), coefs[...])
    own = own[0:FEATS] + own[FEATS : 2 * FEATS] + own[2 * FEATS :]
    base = pl.multiple_of(first * (MATS * FEATS), 16)
    for index in range(MATS):
        sums[pl.ds(base + index * FEATS, FEATS), :] += own[:, index * LANES : (index + 1) * LANES]


def add_back(second, near_feats, sums, coefs):
    base = pl.multiple_of(second * (MATS * FEATS), 16)
    for index in range(MATS):
        back = dot_nn(near_feats, coefs[index * LANES : (index + 1) * LANES, :])
        back = back[:, 0:LANES] + back[:, LANES:]
        back = back[0:FEATS] + back[FEATS : 2 * FEATS] + back[2 * FEATS :]
        if index == MATS - 1:
            back = -back
        sums[pl.ds(base + index * FEATS, FEATS), :] += back


def finish(group, sums, scaled):
    span = MATS * FEATS

    def total(mat, feat):
        return sums[pl.ds(group * 8 * span + mat * FEATS + feat, 8, stride=span), :]

    def own(row):
        return scaled[pl.ds(group * 8, 8), row, :]

    place = [own(row) for row in range(3)]
    velocity = [own(row) for row in range(3, 6)]
    turn = [own(row) for row in range(6, 9)]
    radius = own(9)
    s_place = [total(0, feat) for feat in range(3)]
    s_one = total(0, 3)
    c_one = total(1, 3)
    c_velocity = [total(1, feat) for feat in range(4, 7)]
    n_place = [total(2, feat) for feat in range(3)]
    n_one = total(2, 3)
    n_velocity = [total(2, feat) for feat in range(4, 7)]
    n_turn = [total(2, feat) for feat in range(7, 10)]
    n_turn_place = [total(2, feat) for feat in range(10, 13)]
    n_place_velocity = [total(2, feat) for feat in range(13, 16)]
    k_one = total(3, 3)
    k_turn = [total(3, feat) for feat in range(7, 10)]
    g_place = [total(4, feat) for feat in range(3)]
    g_one = total(4, 3)
    turn_place = cross(turn, place)
    place_velocity = cross(place, velocity)
    first = cross(turn, n_place)
    second = cross(n_turn, place)
    third = cross(n_place, velocity)
    fourth = cross(place, n_velocity)
    force = [
        (s_place[x] - place[x] * s_one)
        + shear_damp
        * (
            (c_velocity[x] - velocity[x] * c_one)
            - (first[x] - turn_place[x] * n_one + n_turn_place[x] - second[x])
        )
        for x in range(3)
    ]
    torque = [
        shear_damp
        * radius
        * (
            (n_place_velocity[x] - third[x] - fourth[x] + place_velocity[x] * n_one)
            - (turn[x] * k_one + k_turn[x])
            + (g_place[x] - place[x] * g_one)
        )
        for x in range(3)
    ]
    return force + torque


def run_pairs(count, todo, coefs, load, scalars, add):
    def some_pairs(index, carry):
        items = [load(index * GROUP + lane) for lane in range(GROUP)]
        for lane in range(GROUP + 1):
            if lane < GROUP:
                scalars(items[lane], coefs[lane])
            if lane > 0:
                add(items[lane - 1], coefs[lane - 1])
        return carry

    lax.fori_loop(0, (count + GROUP - 1) // GROUP, some_pairs, 0)


def list_far(count, message, heard, number, theirs, ours, ghost, blocks, picked, todo):
    size = message.shape[0] - blocks
    start = count
    for tile in range(blocks):
        for which in range(CHOICES):
            shift = heard[which, tile] - theirs
            wanted = (shift >= 0) & (shift < size)
            todo[count] = tile * 64 + blocks + shift
            count = count + wanted.astype(jnp.int32)
            shift = heard[(number + 1) * CHOICES + which, tile] - ours
            wanted = (shift >= 0) & (shift < size)
            todo[count] = (ghost + shift) * 64 + tile
            count = count + wanted.astype(jnp.int32)

    def pick(index, carry):
        picked[index] = scale(message[todo[index] % 64])
        return carry

    lax.fori_loop(start, count, pick, 0)
    return count


def hear(messages, blocks, codes, heard, sem):
    for number, message in enumerate(messages):
        codes[number * CHOICES : (number + 1) * CHOICES, :] = message[
            blocks, 11 : 11 + CHOICES, :
        ].astype(jnp.int32)
    copy = pltpu.make_async_copy(codes, heard, sem)
    copy.start()
    return copy


def far_pairs(messages, places, tiles, sums, spread, picked, heard, todo, coefs):
    spare = tiles.shape[0] - 1
    blocks = messages[0].shape[0] - GHOST_TILES
    count = jnp.int32(0)
    for number, (message, (theirs, ours, ghost)) in enumerate(zip(messages, places)):
        count = list_far(count, message, heard, number, theirs, ours, ghost, blocks, picked, todo)
    for extra in range(GROUP):
        todo[count + extra] = spare * 64
        picked[count + extra] = tiles[spare, 0:ROWS]

    def load(index):
        return todo[index] // 64, picked[index]

    def scalars(item, coef):
        mine, near = item
        pair_scalars(near, tiles[mine, 0:ROWS], tiles[mine, ROWS:], spread, coef)

    def add(item, coef):
        add_back(item[0], features(item[1]), sums, coef)

    run_pairs(count, todo, coefs, load, scalars, add)


def slab_kernel(to_a, to_b, to_sub, from_a, from_b, totals, tiles, feats, sums, spread, *rest):
    picked, codes, heard, todo, sem = rest[:5]
    coefs = rest[5:]
    own_tiles = to_sub.shape[0]
    size = GHOST_TILES
    blocks = own_tiles - size
    copy = hear([to_sub, from_a, from_b], blocks, codes, heard, sem)
    spare = tiles.shape[0] - 1

    def enter(slot, tile):
        rows = scale(tile)
        tiles[slot, 0:ROWS] = rows
        tiles[slot, ROWS:] = mirror(rows)
        return rows

    fill_spread(spread)
    sums[...] = jnp.zeros_like(sums)
    for tile in range(own_tiles):
        feats[tile] = features(enter(tile, to_sub[tile]))
    for tile in range(size):
        enter(own_tiles + tile, to_a[blocks + tile])
        enter(own_tiles + size + tile, to_b[blocks + tile])
    for tile in range(own_tiles + 2 * size, spare + 1):
        feats[spare] = features(enter(tile, jnp.ones((ROWS, LANES), f32)))
    copy.wait()
    shared = blocks + (2 + lax.axis_index("sub")) * size
    count = jnp.int32(0)
    for tile in range(blocks):
        for which in range(CHOICES):
            partner = heard[which, tile]
            mine = (partner >= shared) & (partner < shared + size)
            wanted = ((partner >= 0) & (partner < blocks)) | mine
            slot = jnp.where(mine, partner - shared + blocks, partner)
            todo[count] = tile * 64 + slot
            count = count + wanted.astype(jnp.int32)
    for extra in range(GROUP):
        todo[count + extra] = spare * 64 + spare

    def load(index):
        return todo[index] // 64, todo[index] % 64

    def scalars(item, coef):
        first, second = item
        pair_scalars(tiles[first, 0:ROWS], tiles[second, 0:ROWS], tiles[second, ROWS:], spread, coef)

    def add(item, coef):
        first, second = item
        add_own(first, feats[second], sums, coef)
        add_back(second, feats[first], sums, coef)

    run_pairs(count, todo, coefs, load, scalars, add)
    odd, _, _ = partners_of(lax.axis_index("slab"))
    low, high = blocks + odd * size, blocks + (1 - odd) * size
    places = [(high, low, own_tiles), (low, high, own_tiles + size)]
    far_pairs([from_a, from_b], places, tiles, sums, spread, picked, heard, todo, coefs)
    for group in range(tiles.shape[0] // 8):
        for row, value in enumerate(finish(group, sums, tiles)):
            totals[pl.ds(group * 64 + row, 8, stride=8), :] = value


def sub_kernel(before, tiles, state, extra, *rest):
    messages = rest[: -11 - GROUP]
    force, torque, kicked, totals, sums, spread, picked, codes, heard, todo, sem = rest[
        -11 - GROUP : -GROUP
    ]
    coefs = rest[-GROUP:]
    size = GHOST_TILES
    blocks = state.shape[0] - size
    copy = hear([state, *messages], blocks, codes, heard, sem)
    fill_spread(spread)
    sums[...] = jnp.zeros_like(sums)
    copy.wait()
    sub = lax.axis_index("sub")
    ours = blocks + (2 + sub) * size
    places = [
        (blocks + (2 + lax.bitwise_xor(sub, number + 1)) * size, ours, blocks)
        for number in range(len(messages))
    ]
    far_pairs(messages, places, tiles, sums, spread, picked, heard, todo, coefs)
    for group in range(tiles.shape[0] // 8):
        for row, value in enumerate(finish(group, sums, tiles)):
            part = pl.ds(group * 64 + row, 8, stride=8)
            totals[part, :] = before[part, :] + value
    settle(state, totals, extra[blocks], force, torque, kicked)


def settle(state, totals, extra, force, torque, kicked):
    odd, _, _ = partners_of(lax.axis_index("slab"))
    size = GHOST_TILES
    blocks = state.shape[0] - size
    lane_ids = lax.broadcasted_iota(jnp.int32, (LANES, LANES), 0)
    hots = []
    lefts = []
    for which in range(3):
        for tile in range(size):
            index = ghost_index(extra, which, tile, size, odd)
            hots.append(jnp.where(lane_ids == index % LANES, 1.0, 0.0).astype(bf16))
            ghost = blocks + (which + 1) % 3 * size + tile
            value = totals[ghost * 8 : ghost * 8 + 8, :]
            high = value.astype(bf16).astype(f32)
            both = jnp.concatenate([high, value - high], axis=0)
            source = jnp.broadcast_to(index // LANES, (ROWS, LANES))
            lefts.append(
                jnp.concatenate(
                    [
                        jnp.where(source == block, both, 0.0).astype(bf16)
                        for block in range(blocks)
                    ],
                    axis=0,
                )
            )
    added = dot_nt(jnp.concatenate(lefts, axis=1), jnp.concatenate(hots, axis=1))
    row_ids = lax.broadcasted_iota(jnp.int32, (8, LANES), 0)
    for block in range(blocks):
        columns = slice(block * LANES, (block + 1) * LANES)
        extra = added[block * ROWS : block * ROWS + 8] + added[block * ROWS + 8 : block * ROWS + 16]
        total = totals[block * 8 : block * 8 + 8, :] + extra
        radius = state[block, 9:10, :]
        mass = radius * radius * radius
        inertia = 0.4 * mass * radius * radius
        weight = jnp.where(row_ids < 3, time_step / mass, time_step / inertia)
        force[:, columns] = total[0:3]
        torque[:, columns] = total[3:6]
        kicked[:, columns] = state[block, 3:9, :] + (total * weight)[0:6]


def shape(*dims, dtype=f32):
    return jax.ShapeDtypeStruct(dims, dtype)


def body(positions, motion, radius, liquid, new_owner, ghost_rows, partner_tiles, live_pairs):
    per_dev = positions.shape[1]
    blocks = per_dev // LANES
    size = ghost_rows.shape[1] // LANES
    choices = partner_tiles.shape[0]
    tiles = -(-(blocks + 3 * size + 1) // 8) * 8
    slabs = lax.axis_size("slab")
    subs = lax.axis_size("sub")
    inside = [(i, i ^ 1) for i in range(slabs) if i ^ 1 < slabs]
    across = [(i, (i - 1 ^ 1) + 1) for i in range(1, slabs) if (i - 1 ^ 1) + 1 < slabs]

    state, swap_a, swap_b = pl.pallas_call(
        pack_kernel,
        out_shape=(
            shape(blocks + 1, ROWS, LANES),
            shape(CAP, ROWS, LANES),
            shape(CAP, ROWS, LANES),
        ),
        in_specs=[HBM] * 8,
        out_specs=(VMEM,) * 3,
        scratch_shapes=[
            pltpu.SMEM((blocks,), jnp.int32),
            pltpu.VMEM((3, per_dev), f32),
            pltpu.VMEM((6, per_dev), f32),
            pltpu.VMEM((blocks, LANES), f32),
            pltpu.VMEM((blocks, LANES), f32),
            pltpu.VMEM(ghost_rows.shape, jnp.int32),
            pltpu.VMEM(partner_tiles.shape, jnp.int32),
            pltpu.VMEM((1, blocks), jnp.int32),
            pltpu.VMEM((blocks, ROWS, LANES), f32),
            pltpu.SemaphoreType.DMA((8,)),
        ],
        compiler_params=pltpu.CompilerParams(vmem_limit_bytes=60 * 1024 * 1024),
        name="pack",
    )(
        new_owner,
        positions,
        motion,
        radius.reshape(blocks, LANES),
        liquid.reshape(blocks, LANES),
        ghost_rows,
        partner_tiles,
        live_pairs.reshape(1, blocks),
    )
    low = lax.ppermute(swap_a, "slab", inside)
    high = lax.ppermute(swap_b, "slab", across)
    to_a, to_b, to_sub = pl.pallas_call(
        place_kernel,
        out_shape=(shape(blocks + size, ROWS, LANES),) * 3,
        in_specs=[VMEM] * 3,
        out_specs=(VMEM,) * 3,
        compiler_params=PARAMS,
        name="place",
    )(state, low, high)
    from_a = lax.ppermute(to_a, "slab", inside)
    from_b = lax.ppermute(to_b, "slab", across)
    from_sub = [
        lax.ppermute(to_sub, "sub", [(i, i ^ d) for i in range(subs)]) for d in range(1, subs)
    ]

    def work(messages):
        room = choices * blocks * (1 + messages) + GROUP
        return [
            pltpu.VMEM((tiles * MATS * FEATS, LANES), f32),
            pltpu.VMEM((6 * ROWS, len(WIDE_ROWS) * LANES), bf16),
            pltpu.VMEM((room, ROWS, LANES), f32),
            pltpu.VMEM((8, LANES), jnp.int32),
            pltpu.SMEM((8, LANES), jnp.int32),
            pltpu.SMEM((room,), jnp.int32),
            pltpu.SemaphoreType.DMA(()),
        ] + [pltpu.VMEM((MATS * LANES, 2 * LANES), bf16)] * GROUP

    totals, table = pl.pallas_call(
        slab_kernel,
        out_shape=(shape(tiles * 8, LANES), shape(tiles, 3 * ROWS, LANES)),
        in_specs=[VMEM] * 5,
        out_specs=(VMEM, VMEM),
        scratch_shapes=[pltpu.VMEM((tiles, 3 * FEATS, LANES), bf16)] + work(2),
        compiler_params=PARAMS,
        cost_estimate=pl.CostEstimate(flops=90000000, bytes_accessed=400000, transcendentals=0),
        name="slab_pairs",
    )(to_a, to_b, to_sub, from_a, from_b)
    return tuple(
        pl.pallas_call(
            sub_kernel,
            out_shape=(shape(3, per_dev), shape(3, per_dev), shape(6, per_dev)),
            in_specs=[VMEM] * (4 + len(from_sub)),
            out_specs=(VMEM,) * 3,
            scratch_shapes=[pltpu.VMEM((tiles * 8, LANES), f32)] + work(len(from_sub)),
            compiler_params=PARAMS,
            name="sub_pairs",
        )(totals, table, to_sub, state, *from_sub)
    )


def solution(mesh):
    return jax.shard_map(
        body,
        mesh=mesh,
        in_specs=(
            P(None, ("slab", "sub")),
            P(None, ("slab", "sub")),
            P(("slab", "sub")),
            P(("slab", "sub")),
            P(("slab", "sub")),
            P(None, ("slab", "sub")),
            P(None, ("slab", "sub")),
            P(("slab", "sub")),
        ),
        out_specs=(P(None, ("slab", "sub")), P(None, ("slab", "sub")), P(None, ("slab", "sub"))),
        check_vma=False,
    )
```

```python
import jax
import jax.numpy as jnp
from jax import lax
from jax.experimental import pallas as pl
from jax.experimental.pallas import tpu as pltpu
from jax.sharding import PartitionSpec as P

min_distance = 0.2
stiffness = 1.0
normal_damp = 0.5
shear_damp = 0.3
surface_tension = 2.0
rupture_scale = 1.0
time_step = 0.005

LANES = 128
ROWS = 16
CAP = 4
FEATS = 16
MATS = 5
WIDE_ROWS = (0, 1, 2, 9, 10, 11)
GROUP = 4
CHOICES = 2
GHOST_TILES = 4

f32 = jnp.float32
bf16 = jnp.bfloat16
VMEM = pl.BlockSpec(memory_space=pltpu.VMEM)
HBM = pl.BlockSpec(memory_space=pltpu.HBM)
PARAMS = pltpu.CompilerParams(vmem_limit_bytes=40 * 1024 * 1024)


def split(value, parts):
    out = []
    for _ in range(parts - 1):
        high = value.astype(bf16)
        out.append(high)
        value = value - high.astype(f32)
    out.append(value.astype(bf16))
    return out


def dot_nn(left, right):
    return lax.dot_general(left, right, (((1,), (0,)), ((), ())), preferred_element_type=f32)


def dot_nt(left, right):
    return lax.dot_general(left, right, (((1,), (1,)), ((), ())), preferred_element_type=f32)


def partners_of(here):
    odd = lax.rem(here, 2)
    return odd, here + 1 - 2 * odd, here - 1 + 2 * odd


def pack_kernel(*refs):
    sources, (state, swap_a, swap_b), (moving, sems) = refs[:8], refs[8:11], refs[-2:]
    goal, place, speed, size, wet, rows, partners, live = refs[11:-2]
    copies = [
        pltpu.make_async_copy(source, target, sems.at[index])
        for index, (source, target) in enumerate(zip(sources, refs[11:-2]))
    ]
    for copy in copies:
        copy.start()
    here = lax.axis_index("slab")
    _, slab_a, slab_b = partners_of(here)
    blocks = state.shape[0] - 1
    swap_a[...] = jnp.zeros_like(swap_a)
    swap_b[...] = jnp.zeros_like(swap_b)
    for copy in copies:
        copy.wait()
    count_a = jnp.int32(0)
    count_b = jnp.int32(0)
    for block in range(blocks):
        columns = slice(block * LANES, (block + 1) * LANES)
        target = goal[block]
        moving[block, 0:3, :] = place[:, columns]
        moving[block, 3:9, :] = speed[:, columns]
        moving[block, 9:10, :] = size[block : block + 1, :]
        moving[block, 10:11, :] = wet[block : block + 1, :]
        moving[block, 11:16, :] = jnp.full((5, LANES), (target + 1).astype(f32), f32)
        slab = target // blocks
        goes_a = slab == slab_a
        goes_b = slab == slab_b

        @pl.when(slab == here)
        def _():
            state[target % blocks] = moving[block]

        @pl.when(goes_a)
        def _():
            swap_a[count_a] = moving[block]

        @pl.when(goes_b)
        def _():
            swap_b[count_b] = moving[block]

        count_a = jnp.minimum(count_a + goes_a.astype(jnp.int32), CAP - 1)
        count_b = jnp.minimum(count_b + goes_b.astype(jnp.int32), CAP - 1)
    state[blocks] = jnp.zeros((ROWS, LANES), f32)
    tiles = rows.shape[1] // LANES
    for which in range(3):
        for tile in range(tiles):
            state[blocks, which * tiles + tile : which * tiles + tile + 1, :] = rows[
                which : which + 1, tile * LANES : (tile + 1) * LANES
            ].astype(f32)
    for which in range(partners.shape[0]):
        state[blocks, 12 + which : 13 + which, 0:blocks] = jnp.where(
            live[...] > which, partners[which : which + 1, :], -1
        ).astype(f32)


def ghost_index(extra, which, tile, tiles, odd):
    rows = [extra[other * tiles + tile : other * tiles + tile + 1, :] for other in range(3)]
    row = rows[2] if which == 2 else jnp.where(odd == which, rows[1], rows[0])
    return row.astype(jnp.int32)


def place_kernel(state, low, high, to_a, to_b, to_sub):
    here = lax.axis_index("slab")
    odd, _, _ = partners_of(here)
    blocks = state.shape[0] - 1
    size = to_sub.shape[0] - blocks
    extra = state[blocks]
    base = (here * blocks + 1).astype(f32)
    arrived = [low[slot] for slot in range(CAP)] + [high[slot] for slot in range(CAP)]
    tags = [jnp.broadcast_to(block[11:12, :], (ROWS, LANES)) - base for block in arrived]
    for slot in range(blocks):
        current = state[slot]
        for block, tag in zip(arrived, tags):
            current = jnp.where(tag == float(slot), block, current)
        to_sub[slot] = current
        to_a[slot] = current
        to_b[slot] = current

    flat = to_sub[0:blocks].reshape(blocks * ROWS, LANES)
    left = jnp.concatenate(split(flat, 3), axis=1)
    lane_ids = lax.broadcasted_iota(jnp.int32, (LANES, LANES), 0)
    for which, message in enumerate((to_a, to_b, to_sub)):
        for tile in range(message.shape[0] - blocks):
            index = ghost_index(extra, which, tile, size, odd)
            hot = jnp.where(lane_ids == index % LANES, 1.0, 0.0).astype(bf16)
            picked = dot_nn(left, jnp.concatenate([hot, hot, hot], axis=0))
            source = jnp.broadcast_to(index // LANES, (ROWS, LANES))
            total = jnp.zeros((ROWS, LANES), f32)
            for block in range(blocks):
                total = jnp.where(source == block, picked[block * ROWS : (block + 1) * ROWS], total)
            message[blocks + tile] = total
        message[blocks, 11:13, :] = extra[12:14, :]


def cross(first, second):
    return [
        first[1] * second[2] - first[2] * second[1],
        first[2] * second[0] - first[0] * second[2],
        first[0] * second[1] - first[1] * second[0],
    ]


def recip(value):
    guess = pl.reciprocal(value, approx=True)
    return guess * (2.0 - value * guess)


def dot_rows(first, second):
    return first[0] * second[0] + first[1] * second[1] + first[2] * second[2]


def scale(tile):
    radius, liquid = tile[9:10, :], tile[10:11, :]
    turn = radius * tile[6:9, :]
    bond = radius * jnp.sqrt(surface_tension * liquid)
    place = [tile[row : row + 1, :] for row in range(3)]
    along = dot_rows(place, [tile[row : row + 1, :] for row in range(3, 6)])
    twist = dot_rows(place, [turn[row : row + 1, :] for row in range(3)])
    one = jnp.ones((1, LANES), f32)
    return jnp.concatenate(
        [tile[0:6, :], turn, radius, rupture_scale * liquid, bond, along, one, twist, 0.0 * one],
        axis=0,
    )


def mirror(scaled):
    place, velocity, turn = scaled[0:3, :], scaled[3:6, :], scaled[6:9, :]
    along, one, twist, zero = [scaled[row : row + 1, :] for row in range(12, 16)]
    blank = jnp.broadcast_to(zero, (6, LANES))
    damp = normal_damp - shear_damp
    moving = jnp.concatenate([-velocity, -place, blank, one, along, zero, zero], axis=0)
    turning = jnp.concatenate(
        [-turn, blank[0:3], place, blank[0:3], zero, twist, -one, zero], axis=0
    )
    return jnp.concatenate([damp * moving, turning], axis=0)


def six(value, order):
    parts = split(value, 3)
    return jnp.concatenate([parts[index] for index in order], axis=0)


def features(scaled):
    rows = [scaled[row : row + 1, :] for row in range(9)]
    place, velocity, turn = rows[0:3], rows[3:6], rows[6:9]
    one = jnp.ones((1, LANES), f32)
    values = jnp.concatenate(
        place + [one] + velocity + turn + cross(turn, place) + cross(place, velocity), axis=0
    )
    return jnp.concatenate(split(values, 3), axis=0)


def fill_spread(spread):
    rows = lax.broadcasted_iota(jnp.int32, (6 * ROWS, LANES), 0)
    part = rows // ROWS
    first = (part == 0) | (part == 3) | (part == 5)
    for block, row in enumerate(WIDE_ROWS):
        hot = first & (rows % ROWS == row)
        spread[:, block * LANES : (block + 1) * LANES] = jnp.where(hot, 1.0, 0.0).astype(bf16)


def pair_scalars(near, far, far_mirror, spread, coefs):
    moving = six(far_mirror[0:ROWS], (0, 1, 2, 0, 1, 0))
    turning = six(far_mirror[ROWS:], (0, 1, 2, 0, 1, 0))
    columns = lax.dot_general(
        six(near, (0, 0, 0, 1, 1, 2)),
        jnp.concatenate([spread[...], moving, turning], axis=1),
        (((0,), (0,)), ((), ())),
        preferred_element_type=f32,
    )
    far_rows = [far[row : row + 1, :] for row in WIDE_ROWS]
    step = 16
    for start in range(0, LANES, step):
        col = [
            columns[start : start + step, block * LANES : (block + 1) * LANES] for block in range(8)
        ]
        offset = [far_rows[row] - col[row] for row in range(3)]
        along, twist = col[6], col[7]
        square = dot_rows(offset, offset)
        root = lax.rsqrt(jnp.maximum(square, 1e-30))
        inverse = jnp.minimum(root, 1.0 / min_distance)
        gap = square * root - (far_rows[3] + col[3])
        apart = jnp.maximum(gap, 0.0)
        overlap = apart - gap
        over_radii = recip(far_rows[3] + col[3])
        inner = far_rows[3] * col[3] * over_radii * overlap
        spread_pair = inner * lax.rsqrt(jnp.maximum(inner, 1e-30))
        fill = jnp.maximum(1.0 - apart * recip(far_rows[4] + col[4]), 0.0)
        bridge = far_rows[5] * col[5] * over_radii * (fill * fill)
        inverse1 = spread_pair * inverse
        inverse2 = inverse1 * inverse
        mats = [
            (bridge - spread_pair * (overlap - along * inverse)) * inverse,
            spread_pair,
            inverse1,
            inverse2 * square,
            inverse2 * twist,
        ]
        for index, mat in enumerate(mats):
            high, low = split(mat, 2)
            coefs[index * LANES + start : index * LANES + start + step, 0:LANES] = high
            coefs[index * LANES + start : index * LANES + start + step, LANES:] = low


def add_own(first, far_feats, sums, coefs):
    own = dot_nt(jnp.concatenate([far_feats, far_feats], axis=1), coefs[...])
    own = own[0:FEATS] + own[FEATS : 2 * FEATS] + own[2 * FEATS :]
    base = pl.multiple_of(first * (MATS * FEATS), 16)
    for index in range(MATS):
        sums[pl.ds(base + index * FEATS, FEATS), :] += own[:, index * LANES : (index + 1) * LANES]


def add_back(second, near_feats, sums, coefs):
    base = pl.multiple_of(second * (MATS * FEATS), 16)
    for index in range(MATS):
        back = dot_nn(near_feats, coefs[index * LANES : (index + 1) * LANES, :])
        back = back[:, 0:LANES] + back[:, LANES:]
        back = back[0:FEATS] + back[FEATS : 2 * FEATS] + back[2 * FEATS :]
        if index == MATS - 1:
            back = -back
        sums[pl.ds(base + index * FEATS, FEATS), :] += back


def finish(group, sums, scaled):
    span = MATS * FEATS

    def total(mat, feat):
        return sums[pl.ds(group * 8 * span + mat * FEATS + feat, 8, stride=span), :]

    def own(row):
        return scaled[pl.ds(group * 8, 8), row, :]

    place = [own(row) for row in range(3)]
    velocity = [own(row) for row in range(3, 6)]
    turn = [own(row) for row in range(6, 9)]
    radius = own(9)
    s_place = [total(0, feat) for feat in range(3)]
    s_one = total(0, 3)
    c_one = total(1, 3)
    c_velocity = [total(1, feat) for feat in range(4, 7)]
    n_place = [total(2, feat) for feat in range(3)]
    n_one = total(2, 3)
    n_velocity = [total(2, feat) for feat in range(4, 7)]
    n_turn = [total(2, feat) for feat in range(7, 10)]
    n_turn_place = [total(2, feat) for feat in range(10, 13)]
    n_place_velocity = [total(2, feat) for feat in range(13, 16)]
    k_one = total(3, 3)
    k_turn = [total(3, feat) for feat in range(7, 10)]
    g_place = [total(4, feat) for feat in range(3)]
    g_one = total(4, 3)
    turn_place = cross(turn, place)
    place_velocity = cross(place, velocity)
    first = cross(turn, n_place)
    second = cross(n_turn, place)
    third = cross(n_place, velocity)
    fourth = cross(place, n_velocity)
    force = [
        (s_place[x] - place[x] * s_one)
        + shear_damp
        * (
            (c_velocity[x] - velocity[x] * c_one)
            - (first[x] - turn_place[x] * n_one + n_turn_place[x] - second[x])
        )
        for x in range(3)
    ]
    torque = [
        shear_damp
        * radius
        * (
            (n_place_velocity[x] - third[x] - fourth[x] + place_velocity[x] * n_one)
            - (turn[x] * k_one + k_turn[x])
            + (g_place[x] - place[x] * g_one)
        )
        for x in range(3)
    ]
    return force + torque


def run_pairs(count, todo, coefs, load, scalars, add):
    def some_pairs(index, carry):
        items = [load(index * GROUP + lane) for lane in range(GROUP)]
        for lane in range(GROUP + 1):
            if lane < GROUP:
                scalars(items[lane], coefs[lane])
            if lane > 0:
                add(items[lane - 1], coefs[lane - 1])
        return carry

    lax.fori_loop(0, (count + GROUP - 1) // GROUP, some_pairs, 0)


def list_far(count, message, heard, number, theirs, ours, ghost, blocks, picked, todo):
    size = message.shape[0] - blocks
    start = count
    for tile in range(blocks):
        for which in range(CHOICES):
            shift = heard[which, tile] - theirs
            wanted = (shift >= 0) & (shift < size)
            todo[count] = tile * 64 + blocks + shift
            count = count + wanted.astype(jnp.int32)
            shift = heard[(number + 1) * CHOICES + which, tile] - ours
            wanted = (shift >= 0) & (shift < size)
            todo[count] = (ghost + shift) * 64 + tile
            count = count + wanted.astype(jnp.int32)

    def pick(index, carry):
        picked[index] = scale(message[todo[index] % 64])
        return carry

    lax.fori_loop(start, count, pick, 0)
    return count


def hear(messages, blocks, codes, heard, sem):
    for number, message in enumerate(messages):
        codes[number * CHOICES : (number + 1) * CHOICES, :] = message[
            blocks, 11 : 11 + CHOICES, :
        ].astype(jnp.int32)
    copy = pltpu.make_async_copy(codes, heard, sem)
    copy.start()
    return copy


def far_pairs(messages, places, tiles, sums, spread, picked, heard, todo, coefs):
    spare = tiles.shape[0] - 1
    blocks = messages[0].shape[0] - GHOST_TILES
    count = jnp.int32(0)
    for number, (message, (theirs, ours, ghost)) in enumerate(zip(messages, places)):
        count = list_far(count, message, heard, number, theirs, ours, ghost, blocks, picked, todo)
    for extra in range(GROUP):
        todo[count + extra] = spare * 64
        picked[count + extra] = tiles[spare, 0:ROWS]

    def load(index):
        return todo[index] // 64, picked[index]

    def scalars(item, coef):
        mine, near = item
        pair_scalars(near, tiles[mine, 0:ROWS], tiles[mine, ROWS:], spread, coef)

    def add(item, coef):
        add_back(item[0], features(item[1]), sums, coef)

    run_pairs(count, todo, coefs, load, scalars, add)


def slab_kernel(to_a, to_b, to_sub, from_a, from_b, totals, tiles, feats, sums, spread, *rest):
    picked, codes, heard, todo, sem = rest[:5]
    coefs = rest[5:]
    own_tiles = to_sub.shape[0]
    size = GHOST_TILES
    blocks = own_tiles - size
    copy = hear([to_sub, from_a, from_b], blocks, codes, heard, sem)
    spare = tiles.shape[0] - 1

    def enter(slot, tile):
        rows = scale(tile)
        tiles[slot, 0:ROWS] = rows
        tiles[slot, ROWS:] = mirror(rows)
        return rows

    fill_spread(spread)
    sums[...] = jnp.zeros_like(sums)
    for tile in range(own_tiles):
        feats[tile] = features(enter(tile, to_sub[tile]))
    for tile in range(size):
        enter(own_tiles + tile, to_a[blocks + tile])
        enter(own_tiles + size + tile, to_b[blocks + tile])
    for tile in range(own_tiles + 2 * size, spare + 1):
        feats[spare] = features(enter(tile, jnp.ones((ROWS, LANES), f32)))
    copy.wait()
    shared = blocks + (2 + lax.axis_index("sub")) * size
    count = jnp.int32(0)
    for tile in range(blocks):
        for which in range(CHOICES):
            partner = heard[which, tile]
            mine = (partner >= shared) & (partner < shared + size)
            wanted = ((partner >= 0) & (partner < blocks)) | mine
            slot = jnp.where(mine, partner - shared + blocks, partner)
            todo[count] = tile * 64 + slot
            count = count + wanted.astype(jnp.int32)
    for extra in range(GROUP):
        todo[count + extra] = spare * 64 + spare

    def load(index):
        return todo[index] // 64, todo[index] % 64

    def scalars(item, coef):
        first, second = item
        pair_scalars(tiles[first, 0:ROWS], tiles[second, 0:ROWS], tiles[second, ROWS:], spread, coef)

    def add(item, coef):
        first, second = item
        add_own(first, feats[second], sums, coef)
        add_back(second, feats[first], sums, coef)

    run_pairs(count, todo, coefs, load, scalars, add)
    odd, _, _ = partners_of(lax.axis_index("slab"))
    low, high = blocks + odd * size, blocks + (1 - odd) * size
    places = [(high, low, own_tiles), (low, high, own_tiles + size)]
    far_pairs([from_a, from_b], places, tiles, sums, spread, picked, heard, todo, coefs)
    for group in range(tiles.shape[0] // 8):
        for row, value in enumerate(finish(group, sums, tiles)):
            totals[pl.ds(group * 64 + row, 8, stride=8), :] = value


def sub_kernel(before, tiles, state, extra, *rest):
    sub = lax.axis_index("sub")
    part = state.shape[0]
    messages = [
        rest[0].at[pl.ds(lax.bitwise_xor(sub, number + 1) * part, part)] for number in range(3)
    ]
    force, torque, kicked, totals, sums, spread, picked, codes, heard, todo, sem = rest[
        -11 - GROUP : -GROUP
    ]
    coefs = rest[-GROUP:]
    size = GHOST_TILES
    blocks = state.shape[0] - size
    copy = hear([state, *messages], blocks, codes, heard, sem)
    fill_spread(spread)
    sums[...] = jnp.zeros_like(sums)
    copy.wait()
    ours = blocks + (2 + sub) * size
    places = [
        (blocks + (2 + lax.bitwise_xor(sub, number + 1)) * size, ours, blocks)
        for number in range(len(messages))
    ]
    far_pairs(messages, places, tiles, sums, spread, picked, heard, todo, coefs)
    for group in range(tiles.shape[0] // 8):
        for row, value in enumerate(finish(group, sums, tiles)):
            part = pl.ds(group * 64 + row, 8, stride=8)
            totals[part, :] = before[part, :] + value
    settle(state, totals, extra[blocks], force, torque, kicked)


def settle(state, totals, extra, force, torque, kicked):
    odd, _, _ = partners_of(lax.axis_index("slab"))
    size = GHOST_TILES
    blocks = state.shape[0] - size
    lane_ids = lax.broadcasted_iota(jnp.int32, (LANES, LANES), 0)
    hots = []
    lefts = []
    for which in range(3):
        for tile in range(size):
            index = ghost_index(extra, which, tile, size, odd)
            hots.append(jnp.where(lane_ids == index % LANES, 1.0, 0.0).astype(bf16))
            ghost = blocks + (which + 1) % 3 * size + tile
            value = totals[ghost * 8 : ghost * 8 + 8, :]
            high = value.astype(bf16).astype(f32)
            both = jnp.concatenate([high, value - high], axis=0)
            source = jnp.broadcast_to(index // LANES, (ROWS, LANES))
            lefts.append(
                jnp.concatenate(
                    [
                        jnp.where(source == block, both, 0.0).astype(bf16)
                        for block in range(blocks)
                    ],
                    axis=0,
                )
            )
    added = dot_nt(jnp.concatenate(lefts, axis=1), jnp.concatenate(hots, axis=1))
    row_ids = lax.broadcasted_iota(jnp.int32, (8, LANES), 0)
    for block in range(blocks):
        columns = slice(block * LANES, (block + 1) * LANES)
        extra = added[block * ROWS : block * ROWS + 8] + added[block * ROWS + 8 : block * ROWS + 16]
        total = totals[block * 8 : block * 8 + 8, :] + extra
        radius = state[block, 9:10, :]
        mass = radius * radius * radius
        inertia = 0.4 * mass * radius * radius
        weight = jnp.where(row_ids < 3, time_step / mass, time_step / inertia)
        force[:, columns] = total[0:3]
        torque[:, columns] = total[3:6]
        kicked[:, columns] = state[block, 3:9, :] + (total * weight)[0:6]


def shape(*dims, dtype=f32):
    return jax.ShapeDtypeStruct(dims, dtype)


def body(positions, motion, radius, liquid, new_owner, ghost_rows, partner_tiles, live_pairs):
    per_dev = positions.shape[1]
    blocks = per_dev // LANES
    size = ghost_rows.shape[1] // LANES
    choices = partner_tiles.shape[0]
    tiles = -(-(blocks + 3 * size + 1) // 8) * 8
    slabs = lax.axis_size("slab")
    subs = lax.axis_size("sub")
    inside = [(i, i ^ 1) for i in range(slabs) if i ^ 1 < slabs]
    across = [(i, (i - 1 ^ 1) + 1) for i in range(1, slabs) if (i - 1 ^ 1) + 1 < slabs]

    state, swap_a, swap_b = pl.pallas_call(
        pack_kernel,
        out_shape=(
            shape(blocks + 1, ROWS, LANES),
            shape(CAP, ROWS, LANES),
            shape(CAP, ROWS, LANES),
        ),
        in_specs=[HBM] * 8,
        out_specs=(VMEM,) * 3,
        scratch_shapes=[
            pltpu.SMEM((blocks,), jnp.int32),
            pltpu.VMEM((3, per_dev), f32),
            pltpu.VMEM((6, per_dev), f32),
            pltpu.VMEM((blocks, LANES), f32),
            pltpu.VMEM((blocks, LANES), f32),
            pltpu.VMEM(ghost_rows.shape, jnp.int32),
            pltpu.VMEM(partner_tiles.shape, jnp.int32),
            pltpu.VMEM((1, blocks), jnp.int32),
            pltpu.VMEM((blocks, ROWS, LANES), f32),
            pltpu.SemaphoreType.DMA((8,)),
        ],
        compiler_params=pltpu.CompilerParams(vmem_limit_bytes=60 * 1024 * 1024),
        name="pack",
    )(
        new_owner,
        positions,
        motion,
        radius.reshape(blocks, LANES),
        liquid.reshape(blocks, LANES),
        ghost_rows,
        partner_tiles,
        live_pairs.reshape(1, blocks),
    )
    low = lax.ppermute(swap_a, "slab", inside)
    high = lax.ppermute(swap_b, "slab", across)
    to_a, to_b, to_sub = pl.pallas_call(
        place_kernel,
        out_shape=(shape(blocks + size, ROWS, LANES),) * 3,
        in_specs=[VMEM] * 3,
        out_specs=(VMEM,) * 3,
        compiler_params=PARAMS,
        name="place",
    )(state, low, high)
    from_a = lax.ppermute(to_a, "slab", inside)
    from_b = lax.ppermute(to_b, "slab", across)
    from_sub = [lax.all_gather(to_sub, "sub", axis=0, tiled=True)]

    def work(messages):
        room = choices * blocks * (1 + messages) + GROUP
        return [
            pltpu.VMEM((tiles * MATS * FEATS, LANES), f32),
            pltpu.VMEM((6 * ROWS, len(WIDE_ROWS) * LANES), bf16),
            pltpu.VMEM((room, ROWS, LANES), f32),
            pltpu.VMEM((8, LANES), jnp.int32),
            pltpu.SMEM((8, LANES), jnp.int32),
            pltpu.SMEM((room,), jnp.int32),
            pltpu.SemaphoreType.DMA(()),
        ] + [pltpu.VMEM((MATS * LANES, 2 * LANES), bf16)] * GROUP

    totals, table = pl.pallas_call(
        slab_kernel,
        out_shape=(shape(tiles * 8, LANES), shape(tiles, 3 * ROWS, LANES)),
        in_specs=[VMEM] * 5,
        out_specs=(VMEM, VMEM),
        scratch_shapes=[pltpu.VMEM((tiles, 3 * FEATS, LANES), bf16)] + work(2),
        compiler_params=PARAMS,
        cost_estimate=pl.CostEstimate(flops=90000000, bytes_accessed=400000, transcendentals=0),
        name="slab_pairs",
    )(to_a, to_b, to_sub, from_a, from_b)
    return tuple(
        pl.pallas_call(
            sub_kernel,
            out_shape=(shape(3, per_dev), shape(3, per_dev), shape(6, per_dev)),
            in_specs=[VMEM] * (4 + len(from_sub)),
            out_specs=(VMEM,) * 3,
            scratch_shapes=[pltpu.VMEM((tiles * 8, LANES), f32)] + work(subs - 1),
            compiler_params=PARAMS,
            name="sub_pairs",
        )(totals, table, to_sub, state, *from_sub)
    )


def solution(mesh):
    return jax.shard_map(
        body,
        mesh=mesh,
        in_specs=(
            P(None, ("slab", "sub")),
            P(None, ("slab", "sub")),
            P(("slab", "sub")),
            P(("slab", "sub")),
            P(("slab", "sub")),
            P(None, ("slab", "sub")),
            P(None, ("slab", "sub")),
            P(("slab", "sub")),
        ),
        out_specs=(P(None, ("slab", "sub")), P(None, ("slab", "sub")), P(None, ("slab", "sub"))),
        check_vma=False,
    )
```

```python
import jax
import jax.numpy as jnp
from jax import lax
from jax.experimental import pallas as pl
from jax.experimental.pallas import tpu as pltpu
from jax.sharding import PartitionSpec as P

min_distance = 0.2
stiffness = 1.0
normal_damp = 0.5
shear_damp = 0.3
surface_tension = 2.0
rupture_scale = 1.0
time_step = 0.005

LANES = 128
ROWS = 16
CAP = 4
FEATS = 16
MATS = 5
WIDE_ROWS = (0, 1, 2, 9, 10, 11)
GROUP = 4
CHOICES = 2
GHOST_TILES = 4

f32 = jnp.float32
bf16 = jnp.bfloat16
VMEM = pl.BlockSpec(memory_space=pltpu.VMEM)
HBM = pl.BlockSpec(memory_space=pltpu.HBM)
PARAMS = pltpu.CompilerParams(vmem_limit_bytes=40 * 1024 * 1024)


def split(value, parts):
    out = []
    for _ in range(parts - 1):
        high = value.astype(bf16)
        out.append(high)
        value = value - high.astype(f32)
    out.append(value.astype(bf16))
    return out


def dot_nn(left, right):
    return lax.dot_general(left, right, (((1,), (0,)), ((), ())), preferred_element_type=f32)


def dot_nt(left, right):
    return lax.dot_general(left, right, (((1,), (1,)), ((), ())), preferred_element_type=f32)


def partners_of(here):
    odd = lax.rem(here, 2)
    return odd, here + 1 - 2 * odd, here - 1 + 2 * odd


def pack_kernel(*refs):
    sources, (state, swap_a, swap_b), (moving, sems) = refs[:9], refs[9:12], refs[-2:]
    goal, place, speed, size, wet, rows, partners, live, goals = refs[12:-2]
    copies = [
        pltpu.make_async_copy(source, target, sems.at[index])
        for index, (source, target) in enumerate(zip(sources, refs[12:-2]))
    ]
    for copy in copies:
        copy.start()
    here = lax.axis_index("slab")
    _, slab_a, slab_b = partners_of(here)
    blocks = state.shape[0] - 1
    swap_a[...] = jnp.zeros_like(swap_a)
    swap_b[...] = jnp.zeros_like(swap_b)
    for copy in copies:
        copy.wait()
    count_a = jnp.int32(0)
    count_b = jnp.int32(0)
    for block in range(blocks):
        columns = slice(block * LANES, (block + 1) * LANES)
        target = goal[block]
        moving[block, 0:3, :] = place[:, columns]
        moving[block, 3:9, :] = speed[:, columns]
        moving[block, 9:10, :] = size[block : block + 1, :]
        moving[block, 10:11, :] = wet[block : block + 1, :]
        moving[block, 11:16, :] = jnp.full((5, LANES), (target + 1).astype(f32), f32)
        slab = target // blocks
        goes_a = slab == slab_a
        goes_b = slab == slab_b

        @pl.when(slab == here)
        def _():
            state[target % blocks] = moving[block]

        @pl.when(goes_a)
        def _():
            swap_a[count_a] = moving[block]

        @pl.when(goes_b)
        def _():
            swap_b[count_b] = moving[block]

        count_a = jnp.minimum(count_a + goes_a.astype(jnp.int32), CAP - 1)
        count_b = jnp.minimum(count_b + goes_b.astype(jnp.int32), CAP - 1)
    state[blocks] = jnp.zeros((ROWS, LANES), f32)
    tiles = rows.shape[1] // LANES
    for which in range(3):
        for tile in range(tiles):
            state[blocks, which * tiles + tile : which * tiles + tile + 1, :] = rows[
                which : which + 1, tile * LANES : (tile + 1) * LANES
            ].astype(f32)
    for which in range(partners.shape[0]):
        state[blocks, 12 + which : 13 + which, 0:blocks] = jnp.where(
            live[...] > which, partners[which : which + 1, :], -1
        ).astype(f32)
    slots = lax.broadcasted_iota(jnp.int32, (LANES, blocks), 0)
    filled = jnp.where((goals[...] - here * blocks == slots) & (slots < blocks), 1.0, 0.0)
    counts = dot_nt(jnp.ones((8, blocks), bf16), filled.astype(bf16))
    state[blocks, 14:15, :] = counts[0:1, :]


def ghost_index(extra, which, tile, tiles, odd):
    rows = [extra[other * tiles + tile : other * tiles + tile + 1, :] for other in range(3)]
    row = rows[2] if which == 2 else jnp.where(odd == which, rows[1], rows[0])
    return row.astype(jnp.int32)


def place_kernel(state, low, high, _, to_a, to_b, to_sub):
    here = lax.axis_index("slab")
    odd, _, _ = partners_of(here)
    blocks = state.shape[0] - 1
    size = to_sub.shape[0] - blocks
    extra = state[blocks]
    base = (here * blocks + 1).astype(f32)
    arrived = [low[slot] for slot in range(CAP)] + [high[slot] for slot in range(CAP)]
    tags = [jnp.broadcast_to(block[11:12, :], (ROWS, LANES)) - base for block in arrived]
    for slot in range(blocks):
        current = state[slot]
        for block, tag in zip(arrived, tags):
            current = jnp.where(tag == float(slot), block, current)
        to_sub[slot] = current
        to_a[slot] = current
        to_b[slot] = current

    flat = to_sub[0:blocks].reshape(blocks * ROWS, LANES)
    left = jnp.concatenate(split(flat, 3), axis=1)
    lane_ids = lax.broadcasted_iota(jnp.int32, (LANES, LANES), 0)
    for which, message in enumerate((to_a, to_b, to_sub)):
        for tile in range(message.shape[0] - blocks):
            index = ghost_index(extra, which, tile, size, odd)
            hot = jnp.where(lane_ids == index % LANES, 1.0, 0.0).astype(bf16)
            picked = dot_nn(left, jnp.concatenate([hot, hot, hot], axis=0))
            source = jnp.broadcast_to(index // LANES, (ROWS, LANES))
            total = jnp.zeros((ROWS, LANES), f32)
            for block in range(blocks):
                total = jnp.where(source == block, picked[block * ROWS : (block + 1) * ROWS], total)
            message[blocks + tile] = total
        message[blocks, 11:14, :] = extra[12:15, :]


def cross(first, second):
    return [
        first[1] * second[2] - first[2] * second[1],
        first[2] * second[0] - first[0] * second[2],
        first[0] * second[1] - first[1] * second[0],
    ]


def recip(value):
    return pl.reciprocal(value, approx=True)


def dot_rows(first, second):
    return first[0] * second[0] + first[1] * second[1] + first[2] * second[2]


def scale(tile):
    radius, liquid = tile[9:10, :], tile[10:11, :]
    turn = radius * tile[6:9, :]
    bond = radius * jnp.sqrt(surface_tension * liquid)
    place = [tile[row : row + 1, :] for row in range(3)]
    along = dot_rows(place, [tile[row : row + 1, :] for row in range(3, 6)])
    twist = dot_rows(place, [turn[row : row + 1, :] for row in range(3)])
    one = jnp.ones((1, LANES), f32)
    return jnp.concatenate(
        [tile[0:6, :], turn, radius, rupture_scale * liquid, bond, along, one, twist, 0.0 * one],
        axis=0,
    )


def mirror(scaled):
    place, velocity, turn = scaled[0:3, :], scaled[3:6, :], scaled[6:9, :]
    along, one, twist, zero = [scaled[row : row + 1, :] for row in range(12, 16)]
    blank = jnp.broadcast_to(zero, (6, LANES))
    damp = normal_damp - shear_damp
    moving = jnp.concatenate([-velocity, -place, blank, one, along, zero, zero], axis=0)
    turning = jnp.concatenate(
        [-turn, blank[0:3], place, blank[0:3], zero, twist, -one, zero], axis=0
    )
    return jnp.concatenate([damp * moving, turning], axis=0)


def six(value, order):
    parts = split(value, 3)
    return jnp.concatenate([parts[index] for index in order], axis=0)


def features(scaled):
    rows = [scaled[row : row + 1, :] for row in range(9)]
    place, velocity, turn = rows[0:3], rows[3:6], rows[6:9]
    one = jnp.ones((1, LANES), f32)
    values = jnp.concatenate(
        place + [one] + velocity + turn + cross(turn, place) + cross(place, velocity), axis=0
    )
    return jnp.concatenate(split(values, 3), axis=0)


def fill_spread(spread):
    rows = lax.broadcasted_iota(jnp.int32, (6 * ROWS, LANES), 0)
    part = rows // ROWS
    first = (part == 0) | (part == 3) | (part == 5)
    for block, row in enumerate(WIDE_ROWS):
        hot = first & (rows % ROWS == row)
        spread[:, block * LANES : (block + 1) * LANES] = jnp.where(hot, 1.0, 0.0).astype(bf16)


def pair_scalars(near, far, far_mirror, spread, coefs):
    moving = six(far_mirror[0:ROWS], (0, 1, 2, 0, 1, 0))
    turning = six(far_mirror[ROWS:], (0, 1, 2, 0, 1, 0))
    columns = lax.dot_general(
        six(near, (0, 0, 0, 1, 1, 2)),
        jnp.concatenate([spread[...], moving, turning], axis=1),
        (((0,), (0,)), ((), ())),
        preferred_element_type=f32,
    )
    far_rows = [far[row : row + 1, :] for row in WIDE_ROWS]
    step = 16
    for start in range(0, LANES, step):
        col = [
            columns[start : start + step, block * LANES : (block + 1) * LANES] for block in range(8)
        ]
        offset = [far_rows[row] - col[row] for row in range(3)]
        along, twist = col[6], col[7]
        square = dot_rows(offset, offset)
        root = lax.rsqrt(jnp.maximum(square, 1e-30))
        inverse = jnp.minimum(root, 1.0 / min_distance)
        gap = square * root - (far_rows[3] + col[3])
        apart = jnp.maximum(gap, 0.0)
        overlap = apart - gap
        over_radii = recip(far_rows[3] + col[3])
        inner = far_rows[3] * col[3] * over_radii * overlap
        spread_pair = inner * lax.rsqrt(jnp.maximum(inner, 1e-30))
        fill = jnp.maximum(1.0 - apart * recip(far_rows[4] + col[4]), 0.0)
        bridge = far_rows[5] * col[5] * over_radii * (fill * fill)
        inverse1 = spread_pair * inverse
        inverse2 = inverse1 * inverse
        mats = [
            (bridge - spread_pair * (overlap - along * inverse)) * inverse,
            spread_pair,
            inverse1,
            inverse2 * square,
            inverse2 * twist,
        ]
        for index, mat in enumerate(mats):
            high, low = split(mat, 2)
            coefs[index * LANES + start : index * LANES + start + step, 0:LANES] = high
            coefs[index * LANES + start : index * LANES + start + step, LANES:] = low


def add_own(first, far_feats, sums, coefs):
    own = dot_nt(jnp.concatenate([far_feats, far_feats], axis=1), coefs[...])
    own = own[0:FEATS] + own[FEATS : 2 * FEATS] + own[2 * FEATS :]
    base = pl.multiple_of(first * (MATS * FEATS), 16)
    for index in range(MATS):
        sums[pl.ds(base + index * FEATS, FEATS), :] += own[:, index * LANES : (index + 1) * LANES]


def add_back(second, near_feats, sums, coefs):
    base = pl.multiple_of(second * (MATS * FEATS), 16)
    for index in range(MATS):
        back = dot_nn(near_feats, coefs[index * LANES : (index + 1) * LANES, :])
        back = back[:, 0:LANES] + back[:, LANES:]
        back = back[0:FEATS] + back[FEATS : 2 * FEATS] + back[2 * FEATS :]
        if index == MATS - 1:
            back = -back
        sums[pl.ds(base + index * FEATS, FEATS), :] += back


def finish(group, sums, scaled):
    span = MATS * FEATS

    def total(mat, feat):
        return sums[pl.ds(group * 8 * span + mat * FEATS + feat, 8, stride=span), :]

    def own(row):
        return scaled[pl.ds(group * 8, 8), row, :]

    place = [own(row) for row in range(3)]
    velocity = [own(row) for row in range(3, 6)]
    turn = [own(row) for row in range(6, 9)]
    radius = own(9)
    s_place = [total(0, feat) for feat in range(3)]
    s_one = total(0, 3)
    c_one = total(1, 3)
    c_velocity = [total(1, feat) for feat in range(4, 7)]
    n_place = [total(2, feat) for feat in range(3)]
    n_one = total(2, 3)
    n_velocity = [total(2, feat) for feat in range(4, 7)]
    n_turn = [total(2, feat) for feat in range(7, 10)]
    n_turn_place = [total(2, feat) for feat in range(10, 13)]
    n_place_velocity = [total(2, feat) for feat in range(13, 16)]
    k_one = total(3, 3)
    k_turn = [total(3, feat) for feat in range(7, 10)]
    g_place = [total(4, feat) for feat in range(3)]
    g_one = total(4, 3)
    turn_place = cross(turn, place)
    place_velocity = cross(place, velocity)
    first = cross(turn, n_place)
    second = cross(n_turn, place)
    third = cross(n_place, velocity)
    fourth = cross(place, n_velocity)
    force = [
        (s_place[x] - place[x] * s_one)
        + shear_damp
        * (
            (c_velocity[x] - velocity[x] * c_one)
            - (first[x] - turn_place[x] * n_one + n_turn_place[x] - second[x])
        )
        for x in range(3)
    ]
    torque = [
        shear_damp
        * radius
        * (
            (n_place_velocity[x] - third[x] - fourth[x] + place_velocity[x] * n_one)
            - (turn[x] * k_one + k_turn[x])
            + (g_place[x] - place[x] * g_one)
        )
        for x in range(3)
    ]
    return force + torque


def run_pairs(count, todo, coefs, load, scalars, add):
    def some_pairs(index, carry):
        items = [load(index * GROUP + lane) for lane in range(GROUP)]
        for lane in range(GROUP + 1):
            if lane < GROUP:
                scalars(items[lane], coefs[lane])
            if lane > 0:
                add(items[lane - 1], coefs[lane - 1])
        return carry

    lax.fori_loop(0, (count + GROUP - 1) // GROUP, some_pairs, 0)


def within(shift, size):
    return shift.astype(jnp.uint32) < jnp.uint32(size)


def list_far(count, message, heard, number, theirs, ours, ghost, blocks, todo):
    size = message.shape[0] - blocks
    for tile in range(blocks):
        for which in range(CHOICES):
            shift = heard[which, tile] - theirs
            wanted = within(shift, size)
            todo[count] = tile * 64 + blocks + shift
            count = count + wanted.astype(jnp.int32)
            shift = heard[(number + 1) * CHOICES + which, tile] - ours
            wanted = within(shift, size)
            todo[count] = (ghost + shift) * 64 + tile
            count = count + wanted.astype(jnp.int32)
    return count


def hear(messages, blocks, codes, heard, sem):
    for number, message in enumerate(messages):
        codes[number * CHOICES : (number + 1) * CHOICES, :] = message[
            blocks, 11 : 11 + CHOICES, :
        ].astype(jnp.int32)
    copy = pltpu.make_async_copy(codes, heard, sem)
    copy.start()
    return copy


def list_all(messages, places, heard, todo):
    blocks = messages[0].shape[0] - GHOST_TILES
    count = jnp.int32(0)
    ends = [count]
    for number, (message, (theirs, ours, ghost)) in enumerate(zip(messages, places)):
        count = list_far(count, message, heard, number, theirs, ours, ghost, blocks, todo)
        ends.append(count)
    return ends


def far_pairs(messages, ends, tiles, sums, spread, picked, todo, coefs):
    spare = tiles.shape[0] - 1
    count = ends[-1]
    for number, message in enumerate(messages):

        def pick(index, carry, message=message):
            picked[index] = scale(message[todo[index] % 64])
            return carry

        lax.fori_loop(ends[number], ends[number + 1], pick, 0)
    for extra in range(GROUP):
        todo[count + extra] = spare * 64
        picked[count + extra] = tiles[spare, 0:ROWS]

    def load(index):
        return todo[index] // 64, picked[index]

    def scalars(item, coef):
        mine, near = item
        pair_scalars(near, tiles[mine, 0:ROWS], tiles[mine, ROWS:], spread, coef)

    def add(item, coef):
        add_back(item[0], features(item[1]), sums, coef)

    run_pairs(count, todo, coefs, load, scalars, add)


def early_kernel(state, table, feats):
    for slot in range(table.shape[0]):
        rows = scale(state[slot])
        table[slot, 0:ROWS] = rows
        table[slot, ROWS:] = mirror(rows)
        feats[slot] = features(rows)


def slab_kernel(
    to_a, to_b, to_sub, from_a, from_b, table, early_feats, totals, tiles, feats, far_todo, new, sums, *rest
):
    spread, picked, codes, heard, todo, sem = rest[:6]
    coefs = rest[6:]
    own_tiles = to_sub.shape[0]
    size = GHOST_TILES
    blocks = own_tiles - size
    codes[7:8, :] = to_sub[blocks, 13:14, :].astype(jnp.int32)
    copy = hear([to_sub, from_a, from_b], blocks, codes, heard, sem)
    spare = tiles.shape[0] - 1

    def enter(slot, tile):
        rows = scale(tile)
        tiles[slot, 0:ROWS] = rows
        tiles[slot, ROWS:] = mirror(rows)
        return rows

    fill_spread(spread)
    copy.wait()
    shared = blocks + (2 + lax.axis_index("sub")) * size
    count = jnp.int32(0)
    for tile in range(blocks):
        for which in range(CHOICES):
            partner = heard[which, tile]
            mine = within(partner - shared, size)
            wanted = within(partner, blocks) | mine
            slot = jnp.where(mine, partner - shared + blocks, partner)
            todo[count] = tile * 64 + slot
            count = count + wanted.astype(jnp.int32)
    odd, _, _ = partners_of(lax.axis_index("slab"))
    low, high = blocks + odd * size, blocks + (1 - odd) * size
    places = [(high, low, own_tiles), (low, high, own_tiles + size)]
    ends = list_all([from_a, from_b], places, heard, far_todo)
    news = jnp.int32(0)
    for slot in range(blocks):
        new[news] = slot
        news = news + (heard[7, slot] == 0).astype(jnp.int32)
    sums[...] = jnp.zeros_like(sums)
    for slot in range(blocks):
        tiles[slot] = table[slot]
        feats[slot] = early_feats[slot]
    for tile in range(blocks, own_tiles):
        feats[tile] = features(enter(tile, to_sub[tile]))
    for tile in range(size):
        enter(own_tiles + tile, to_a[blocks + tile])
        enter(own_tiles + size + tile, to_b[blocks + tile])
    for tile in range(own_tiles + 2 * size, spare + 1):
        feats[spare] = features(enter(tile, jnp.ones((ROWS, LANES), f32)))

    def enter_new(index, carry):
        slot = new[index]
        feats[slot] = features(enter(slot, to_sub[slot]))
        return carry

    lax.fori_loop(0, news, enter_new, 0)
    for extra in range(GROUP):
        todo[count + extra] = spare * 64 + spare

    def load(index):
        return todo[index] // 64, todo[index] % 64

    def scalars(item, coef):
        first, second = item
        pair_scalars(tiles[first, 0:ROWS], tiles[second, 0:ROWS], tiles[second, ROWS:], spread, coef)

    def add(item, coef):
        first, second = item
        add_own(first, feats[second], sums, coef)
        add_back(second, feats[first], sums, coef)

    run_pairs(count, todo, coefs, load, scalars, add)
    far_pairs([from_a, from_b], ends, tiles, sums, spread, picked, far_todo, coefs)
    for group in range(tiles.shape[0] // 8):
        for row, value in enumerate(finish(group, sums, tiles)):
            totals[pl.ds(group * 64 + row, 8, stride=8), :] = value


def sub_kernel(before, tiles, state, extra, *rest):
    messages = rest[: -11 - GROUP]
    force, torque, kicked, totals, sums, spread, picked, codes, heard, todo, sem = rest[
        -11 - GROUP : -GROUP
    ]
    coefs = rest[-GROUP:]
    size = GHOST_TILES
    blocks = state.shape[0] - size
    copy = hear([state, *messages], blocks, codes, heard, sem)
    fill_spread(spread)
    copy.wait()
    sums[...] = jnp.zeros_like(sums)
    sub = lax.axis_index("sub")
    ours = blocks + (2 + sub) * size
    places = [
        (blocks + (2 + lax.bitwise_xor(sub, number + 1)) * size, ours, blocks)
        for number in range(len(messages))
    ]
    ends = list_all(messages, places, heard, todo)
    far_pairs(messages, ends, tiles, sums, spread, picked, todo, coefs)
    for group in range(tiles.shape[0] // 8):
        for row, value in enumerate(finish(group, sums, tiles)):
            part = pl.ds(group * 64 + row, 8, stride=8)
            totals[part, :] = before[part, :] + value
    settle(state, totals, extra[blocks], force, torque, kicked)


def settle(state, totals, extra, force, torque, kicked):
    odd, _, _ = partners_of(lax.axis_index("slab"))
    size = GHOST_TILES
    blocks = state.shape[0] - size
    lane_ids = lax.broadcasted_iota(jnp.int32, (LANES, LANES), 0)
    hots = []
    lefts = []
    for which in range(3):
        for tile in range(size):
            index = ghost_index(extra, which, tile, size, odd)
            hots.append(jnp.where(lane_ids == index % LANES, 1.0, 0.0).astype(bf16))
            ghost = blocks + (which + 1) % 3 * size + tile
            value = totals[ghost * 8 : ghost * 8 + 8, :]
            high = value.astype(bf16).astype(f32)
            both = jnp.concatenate([high, value - high], axis=0)
            source = jnp.broadcast_to(index // LANES, (ROWS, LANES))
            lefts.append(
                jnp.concatenate(
                    [
                        jnp.where(source == block, both, 0.0).astype(bf16)
                        for block in range(blocks)
                    ],
                    axis=0,
                )
            )
    added = dot_nt(jnp.concatenate(lefts, axis=1), jnp.concatenate(hots, axis=1))
    row_ids = lax.broadcasted_iota(jnp.int32, (8, LANES), 0)
    for block in range(blocks):
        columns = slice(block * LANES, (block + 1) * LANES)
        extra = added[block * ROWS : block * ROWS + 8] + added[block * ROWS + 8 : block * ROWS + 16]
        total = totals[block * 8 : block * 8 + 8, :] + extra
        radius = state[block, 9:10, :]
        mass = radius * radius * radius
        inertia = 0.4 * mass * radius * radius
        weight = jnp.where(row_ids < 3, time_step / mass, time_step / inertia)
        force[:, columns] = total[0:3]
        torque[:, columns] = total[3:6]
        kicked[:, columns] = state[block, 3:9, :] + (total * weight)[0:6]


def shape(*dims, dtype=f32):
    return jax.ShapeDtypeStruct(dims, dtype)


def body(positions, motion, radius, liquid, new_owner, ghost_rows, partner_tiles, live_pairs):
    per_dev = positions.shape[1]
    blocks = per_dev // LANES
    size = ghost_rows.shape[1] // LANES
    choices = partner_tiles.shape[0]
    tiles = -(-(blocks + 3 * size + 1) // 8) * 8
    slabs = lax.axis_size("slab")
    subs = lax.axis_size("sub")
    inside = [(i, i ^ 1) for i in range(slabs) if i ^ 1 < slabs]
    across = [(i, (i - 1 ^ 1) + 1) for i in range(1, slabs) if (i - 1 ^ 1) + 1 < slabs]

    state, swap_a, swap_b = pl.pallas_call(
        pack_kernel,
        out_shape=(
            shape(blocks + 1, ROWS, LANES),
            shape(CAP, ROWS, LANES),
            shape(CAP, ROWS, LANES),
        ),
        in_specs=[HBM] * 9,
        out_specs=(VMEM,) * 3,
        scratch_shapes=[
            pltpu.SMEM((blocks,), jnp.int32),
            pltpu.VMEM((3, per_dev), f32),
            pltpu.VMEM((6, per_dev), f32),
            pltpu.VMEM((blocks, LANES), f32),
            pltpu.VMEM((blocks, LANES), f32),
            pltpu.VMEM(ghost_rows.shape, jnp.int32),
            pltpu.VMEM(partner_tiles.shape, jnp.int32),
            pltpu.VMEM((1, blocks), jnp.int32),
            pltpu.VMEM((1, blocks), jnp.int32),
            pltpu.VMEM((blocks, ROWS, LANES), f32),
            pltpu.SemaphoreType.DMA((9,)),
        ],
        compiler_params=pltpu.CompilerParams(vmem_limit_bytes=60 * 1024 * 1024),
        name="pack",
    )(
        new_owner,
        positions,
        motion,
        radius.reshape(blocks, LANES),
        liquid.reshape(blocks, LANES),
        ghost_rows,
        partner_tiles,
        live_pairs.reshape(1, blocks),
        new_owner.reshape(1, blocks),
    )
    low = lax.ppermute(swap_a, "slab", inside)
    high = lax.ppermute(swap_b, "slab", across)
    early = pl.pallas_call(
        early_kernel,
        out_shape=(
            shape(blocks, 3 * ROWS, LANES),
            shape(blocks, 3 * FEATS, LANES, dtype=bf16),
        ),
        in_specs=[VMEM],
        out_specs=(VMEM, VMEM),
        compiler_params=PARAMS,
        cost_estimate=pl.CostEstimate(flops=4000000, bytes_accessed=1000000, transcendentals=0),
        name="early",
    )(state)
    to_a, to_b, to_sub = pl.pallas_call(
        place_kernel,
        out_shape=(shape(blocks + size, ROWS, LANES),) * 3,
        in_specs=[VMEM] * 3 + [pl.BlockSpec(memory_space=pl.ANY)],
        out_specs=(VMEM,) * 3,
        compiler_params=PARAMS,
        name="place",
    )(state, low, high, early[0])
    from_a = lax.ppermute(to_a, "slab", inside)
    from_b = lax.ppermute(to_b, "slab", across)
    from_sub = [
        lax.ppermute(to_sub, "sub", [(i, i ^ d) for i in range(subs)]) for d in range(1, subs)
    ]

    def work(messages):
        room = choices * blocks * (1 + messages) + GROUP
        return [
            pltpu.VMEM((tiles * MATS * FEATS, LANES), f32),
            pltpu.VMEM((6 * ROWS, len(WIDE_ROWS) * LANES), bf16),
            pltpu.VMEM((room, ROWS, LANES), f32),
            pltpu.VMEM((8, LANES), jnp.int32),
            pltpu.SMEM((8, LANES), jnp.int32),
            pltpu.SMEM((room,), jnp.int32),
            pltpu.SemaphoreType.DMA(()),
        ] + [pltpu.VMEM((MATS * LANES, 2 * LANES), bf16)] * GROUP

    totals, table = pl.pallas_call(
        slab_kernel,
        out_shape=(shape(tiles * 8, LANES), shape(tiles, 3 * ROWS, LANES)),
        in_specs=[VMEM] * 7,
        out_specs=(VMEM, VMEM),
        scratch_shapes=[
            pltpu.VMEM((tiles, 3 * FEATS, LANES), bf16),
            pltpu.SMEM((3 * choices * blocks + GROUP,), jnp.int32),
            pltpu.SMEM((blocks + 1,), jnp.int32),
        ]
        + work(2),
        compiler_params=PARAMS,
        cost_estimate=pl.CostEstimate(flops=90000000, bytes_accessed=400000, transcendentals=0),
        name="slab_pairs",
    )(to_a, to_b, to_sub, from_a, from_b, *early)
    return tuple(
        pl.pallas_call(
            sub_kernel,
            out_shape=(shape(3, per_dev), shape(3, per_dev), shape(6, per_dev)),
            in_specs=[VMEM] * (4 + len(from_sub)),
            out_specs=(VMEM,) * 3,
            scratch_shapes=[pltpu.VMEM((tiles * 8, LANES), f32)] + work(len(from_sub)),
            compiler_params=PARAMS,
            name="sub_pairs",
        )(totals, table, to_sub, state, *from_sub)
    )


def solution(mesh):
    return jax.shard_map(
        body,
        mesh=mesh,
        in_specs=(
            P(None, ("slab", "sub")),
            P(None, ("slab", "sub")),
            P(("slab", "sub")),
            P(("slab", "sub")),
            P(("slab", "sub")),
            P(None, ("slab", "sub")),
            P(None, ("slab", "sub")),
            P(("slab", "sub")),
        ),
        out_specs=(P(None, ("slab", "sub")), P(None, ("slab", "sub")), P(None, ("slab", "sub"))),
        check_vma=False,
    )
```

```python
import jax
import jax.numpy as jnp
from jax import lax
from jax.experimental import pallas as pl
from jax.experimental.pallas import tpu as pltpu
from jax.sharding import PartitionSpec as P

min_distance = 0.2
stiffness = 1.0
normal_damp = 0.5
shear_damp = 0.3
surface_tension = 2.0
rupture_scale = 1.0
time_step = 0.005

LANES = 128
ROWS = 16
CAP = 4
FEATS = 16
MATS = 5
WIDE_ROWS = (0, 1, 2, 9, 10, 11)
GROUP = 3
CHOICES = 2
GHOST_TILES = 4

f32 = jnp.float32
bf16 = jnp.bfloat16
VMEM = pl.BlockSpec(memory_space=pltpu.VMEM)
HBM = pl.BlockSpec(memory_space=pltpu.HBM)
PARAMS = pltpu.CompilerParams(vmem_limit_bytes=40 * 1024 * 1024)


def split(value, parts):
    out = []
    for _ in range(parts - 1):
        high = value.astype(bf16)
        out.append(high)
        value = value - high.astype(f32)
    out.append(value.astype(bf16))
    return out


def dot_nn(left, right):
    return lax.dot_general(left, right, (((1,), (0,)), ((), ())), preferred_element_type=f32)


def dot_nt(left, right):
    return lax.dot_general(left, right, (((1,), (1,)), ((), ())), preferred_element_type=f32)


def partners_of(here):
    odd = lax.rem(here, 2)
    return odd, here + 1 - 2 * odd, here - 1 + 2 * odd


def pack_kernel(*refs):
    sources, (state, swap_a, swap_b), (moving, sems) = refs[:9], refs[9:12], refs[-2:]
    goal, place, speed, size, wet, rows, partners, live, goals = refs[12:-2]
    copies = [
        pltpu.make_async_copy(source, target, sems.at[index])
        for index, (source, target) in enumerate(zip(sources, refs[12:-2]))
    ]
    for copy in copies:
        copy.start()
    here = lax.axis_index("slab")
    _, slab_a, slab_b = partners_of(here)
    blocks = state.shape[0] - 1
    swap_a[...] = jnp.zeros_like(swap_a)
    swap_b[...] = jnp.zeros_like(swap_b)
    for copy in copies:
        copy.wait()
    count_a = jnp.int32(0)
    count_b = jnp.int32(0)
    for block in range(blocks):
        columns = slice(block * LANES, (block + 1) * LANES)
        target = goal[block]
        moving[block, 0:3, :] = place[:, columns]
        moving[block, 3:9, :] = speed[:, columns]
        moving[block, 9:10, :] = size[block : block + 1, :]
        moving[block, 10:11, :] = wet[block : block + 1, :]
        moving[block, 11:16, :] = jnp.full((5, LANES), (target + 1).astype(f32), f32)
        slab = target // blocks
        goes_a = slab == slab_a
        goes_b = slab == slab_b

        @pl.when(slab == here)
        def _():
            state[target % blocks] = moving[block]

        @pl.when(goes_a)
        def _():
            swap_a[count_a] = moving[block]

        @pl.when(goes_b)
        def _():
            swap_b[count_b] = moving[block]

        count_a = jnp.minimum(count_a + goes_a.astype(jnp.int32), CAP - 1)
        count_b = jnp.minimum(count_b + goes_b.astype(jnp.int32), CAP - 1)
    state[blocks] = jnp.zeros((ROWS, LANES), f32)
    tiles = rows.shape[1] // LANES
    for which in range(3):
        for tile in range(tiles):
            state[blocks, which * tiles + tile : which * tiles + tile + 1, :] = rows[
                which : which + 1, tile * LANES : (tile + 1) * LANES
            ].astype(f32)
    for which in range(partners.shape[0]):
        state[blocks, 12 + which : 13 + which, 0:blocks] = jnp.where(
            live[...] > which, partners[which : which + 1, :], -1
        ).astype(f32)
    slots = lax.broadcasted_iota(jnp.int32, (LANES, blocks), 0)
    filled = jnp.where((goals[...] - here * blocks == slots) & (slots < blocks), 1.0, 0.0)
    counts = dot_nt(jnp.ones((8, blocks), bf16), filled.astype(bf16))
    state[blocks, 14:15, :] = counts[0:1, :]


def ghost_index(extra, which, tile, tiles, odd):
    rows = [extra[other * tiles + tile : other * tiles + tile + 1, :] for other in range(3)]
    row = rows[2] if which == 2 else jnp.where(odd == which, rows[1], rows[0])
    return row.astype(jnp.int32)


def place_kernel(state, low, high, _, to_a, to_b, to_sub):
    here = lax.axis_index("slab")
    odd, _, _ = partners_of(here)
    blocks = state.shape[0] - 1
    size = to_sub.shape[0] - blocks
    extra = state[blocks]
    base = (here * blocks + 1).astype(f32)
    arrived = [low[slot] for slot in range(CAP)] + [high[slot] for slot in range(CAP)]
    tags = [jnp.broadcast_to(block[11:12, :], (ROWS, LANES)) - base for block in arrived]
    for slot in range(blocks):
        current = state[slot]
        for block, tag in zip(arrived, tags):
            current = jnp.where(tag == float(slot), block, current)
        to_sub[slot] = current
        to_a[slot] = current
        to_b[slot] = current

    flat = to_sub[0:blocks].reshape(blocks * ROWS, LANES)
    left = jnp.concatenate(split(flat, 3), axis=1)
    lane_ids = lax.broadcasted_iota(jnp.int32, (LANES, LANES), 0)
    for which, message in enumerate((to_a, to_b, to_sub)):
        for tile in range(message.shape[0] - blocks):
            index = ghost_index(extra, which, tile, size, odd)
            hot = jnp.where(lane_ids == index % LANES, 1.0, 0.0).astype(bf16)
            picked = dot_nn(left, jnp.concatenate([hot, hot, hot], axis=0))
            source = jnp.broadcast_to(index // LANES, (ROWS, LANES))
            total = jnp.zeros((ROWS, LANES), f32)
            for block in range(blocks):
                total = jnp.where(source == block, picked[block * ROWS : (block + 1) * ROWS], total)
            message[blocks + tile] = total
        message[blocks, 11:14, :] = extra[12:15, :]


def cross(first, second):
    return [
        first[1] * second[2] - first[2] * second[1],
        first[2] * second[0] - first[0] * second[2],
        first[0] * second[1] - first[1] * second[0],
    ]


def recip(value):
    return pl.reciprocal(value, approx=True)


def dot_rows(first, second):
    return first[0] * second[0] + first[1] * second[1] + first[2] * second[2]


def scale(tile):
    radius, liquid = tile[9:10, :], tile[10:11, :]
    turn = radius * tile[6:9, :]
    bond = radius * jnp.sqrt(surface_tension * liquid)
    place = [tile[row : row + 1, :] for row in range(3)]
    along = dot_rows(place, [tile[row : row + 1, :] for row in range(3, 6)])
    twist = dot_rows(place, [turn[row : row + 1, :] for row in range(3)])
    one = jnp.ones((1, LANES), f32)
    return jnp.concatenate(
        [tile[0:6, :], turn, radius, rupture_scale * liquid, bond, along, one, twist, 0.0 * one],
        axis=0,
    )


def mirror(scaled):
    place, velocity, turn = scaled[0:3, :], scaled[3:6, :], scaled[6:9, :]
    along, one, twist, zero = [scaled[row : row + 1, :] for row in range(12, 16)]
    blank = jnp.broadcast_to(zero, (6, LANES))
    damp = normal_damp - shear_damp
    moving = jnp.concatenate([-velocity, -place, blank, one, along, zero, zero], axis=0)
    turning = jnp.concatenate(
        [-turn, blank[0:3], place, blank[0:3], zero, twist, -one, zero], axis=0
    )
    return jnp.concatenate([damp * moving, turning], axis=0)


def six(value, order):
    parts = split(value, 3)
    return jnp.concatenate([parts[index] for index in order], axis=0)


def features(scaled):
    rows = [scaled[row : row + 1, :] for row in range(9)]
    place, velocity, turn = rows[0:3], rows[3:6], rows[6:9]
    one = jnp.ones((1, LANES), f32)
    values = jnp.concatenate(
        place + [one] + velocity + turn + cross(turn, place) + cross(place, velocity), axis=0
    )
    return jnp.concatenate(split(values, 3), axis=0)


def fill_spread(spread):
    rows = lax.broadcasted_iota(jnp.int32, (6 * ROWS, LANES), 0)
    part = rows // ROWS
    first = (part == 0) | (part == 3) | (part == 5)
    for block, row in enumerate(WIDE_ROWS):
        hot = first & (rows % ROWS == row)
        spread[:, block * LANES : (block + 1) * LANES] = jnp.where(hot, 1.0, 0.0).astype(bf16)


def pair_columns(near, far_mirror, spread, wide):
    moving = six(far_mirror[0:ROWS], (0, 1, 2, 0, 1, 0))
    turning = six(far_mirror[ROWS:], (0, 1, 2, 0, 1, 0))
    wide[...] = lax.dot_general(
        six(near, (0, 0, 0, 1, 1, 2)),
        jnp.concatenate([spread[...], moving, turning], axis=1),
        (((0,), (0,)), ((), ())),
        preferred_element_type=f32,
    )


def pair_scalars(far, wide, coefs):
    far_rows = [far[row : row + 1, :] for row in WIDE_ROWS]
    step = 16
    for start in range(0, LANES, step):
        col = [
            wide[start : start + step, block * LANES : (block + 1) * LANES] for block in range(8)
        ]
        offset = [far_rows[row] - col[row] for row in range(3)]
        along, twist = col[6], col[7]
        square = dot_rows(offset, offset)
        root = lax.rsqrt(jnp.maximum(square, 1e-30))
        inverse = jnp.minimum(root, 1.0 / min_distance)
        gap = square * root - (far_rows[3] + col[3])
        apart = jnp.maximum(gap, 0.0)
        overlap = apart - gap
        over_radii = recip(far_rows[3] + col[3])
        inner = far_rows[3] * col[3] * over_radii * overlap
        spread_pair = inner * lax.rsqrt(jnp.maximum(inner, 1e-30))
        fill = jnp.maximum(1.0 - apart * recip(far_rows[4] + col[4]), 0.0)
        bridge = far_rows[5] * col[5] * over_radii * (fill * fill)
        inverse1 = spread_pair * inverse
        inverse2 = inverse1 * inverse
        mats = [
            (bridge - spread_pair * (overlap - along * inverse)) * inverse,
            spread_pair,
            inverse1,
            inverse2 * square,
            inverse2 * twist,
        ]
        for index, mat in enumerate(mats):
            high, low = split(mat, 2)
            coefs[index * LANES + start : index * LANES + start + step, 0:LANES] = high
            coefs[index * LANES + start : index * LANES + start + step, LANES:] = low


def add_own(first, far_feats, sums, coefs):
    own = dot_nt(jnp.concatenate([far_feats, far_feats], axis=1), coefs[...])
    own = own[0:FEATS] + own[FEATS : 2 * FEATS] + own[2 * FEATS :]
    base = pl.multiple_of(first * (MATS * FEATS), 16)
    for index in range(MATS):
        sums[pl.ds(base + index * FEATS, FEATS), :] += own[:, index * LANES : (index + 1) * LANES]


def add_back(second, near_feats, sums, coefs):
    base = pl.multiple_of(second * (MATS * FEATS), 16)
    for index in range(MATS):
        back = dot_nn(near_feats, coefs[index * LANES : (index + 1) * LANES, :])
        back = back[:, 0:LANES] + back[:, LANES:]
        back = back[0:FEATS] + back[FEATS : 2 * FEATS] + back[2 * FEATS :]
        if index == MATS - 1:
            back = -back
        sums[pl.ds(base + index * FEATS, FEATS), :] += back


def finish(group, sums, scaled):
    span = MATS * FEATS

    def total(mat, feat):
        return sums[pl.ds(group * 8 * span + mat * FEATS + feat, 8, stride=span), :]

    def own(row):
        return scaled[pl.ds(group * 8, 8), row, :]

    place = [own(row) for row in range(3)]
    velocity = [own(row) for row in range(3, 6)]
    turn = [own(row) for row in range(6, 9)]
    radius = own(9)
    s_place = [total(0, feat) for feat in range(3)]
    s_one = total(0, 3)
    c_one = total(1, 3)
    c_velocity = [total(1, feat) for feat in range(4, 7)]
    n_place = [total(2, feat) for feat in range(3)]
    n_one = total(2, 3)
    n_velocity = [total(2, feat) for feat in range(4, 7)]
    n_turn = [total(2, feat) for feat in range(7, 10)]
    n_turn_place = [total(2, feat) for feat in range(10, 13)]
    n_place_velocity = [total(2, feat) for feat in range(13, 16)]
    k_one = total(3, 3)
    k_turn = [total(3, feat) for feat in range(7, 10)]
    g_place = [total(4, feat) for feat in range(3)]
    g_one = total(4, 3)
    turn_place = cross(turn, place)
    place_velocity = cross(place, velocity)
    first = cross(turn, n_place)
    second = cross(n_turn, place)
    third = cross(n_place, velocity)
    fourth = cross(place, n_velocity)
    force = [
        (s_place[x] - place[x] * s_one)
        + shear_damp
        * (
            (c_velocity[x] - velocity[x] * c_one)
            - (first[x] - turn_place[x] * n_one + n_turn_place[x] - second[x])
        )
        for x in range(3)
    ]
    torque = [
        shear_damp
        * radius
        * (
            (n_place_velocity[x] - third[x] - fourth[x] + place_velocity[x] * n_one)
            - (turn[x] * k_one + k_turn[x])
            + (g_place[x] - place[x] * g_one)
        )
        for x in range(3)
    ]
    return force + torque


def run_pairs(count, buffers, load, columns, scalars, add):
    wides, coefs = buffers[:GROUP], buffers[GROUP:]
    groups = jnp.maximum((count + GROUP - 1) // GROUP, 1)

    def items(group):
        return [load(group * GROUP + lane) for lane in range(GROUP)]

    for item, wide in zip(items(0), wides):
        columns(item, wide)
    for item, later, wide, coef in zip(items(0), items(1), wides, coefs):
        scalars(item, wide, coef)
        columns(later, wide)

    def step(group, carry):
        for item, following, later, wide, coef in zip(
            items(group), items(group + 1), items(group + 2), wides, coefs
        ):
            add(item, coef)
            scalars(following, wide, coef)
            columns(later, wide)
        return carry

    lax.fori_loop(0, groups - 1, step, 0)
    for item, coef in zip(items(groups - 1), coefs):
        add(item, coef)


def within(shift, size):
    return shift.astype(jnp.uint32) < jnp.uint32(size)


def list_far(count, message, heard, number, theirs, ours, ghost, blocks, todo):
    size = message.shape[0] - blocks
    for tile in range(blocks):
        for which in range(CHOICES):
            shift = heard[which, tile] - theirs
            wanted = within(shift, size)
            todo[count] = tile * 64 + blocks + shift
            count = count + wanted.astype(jnp.int32)
            shift = heard[(number + 1) * CHOICES + which, tile] - ours
            wanted = within(shift, size)
            todo[count] = (ghost + shift) * 64 + tile
            count = count + wanted.astype(jnp.int32)
    return count


def hear(messages, blocks, codes, heard, sem):
    for number, message in enumerate(messages):
        codes[number * CHOICES : (number + 1) * CHOICES, :] = message[
            blocks, 11 : 11 + CHOICES, :
        ].astype(jnp.int32)
    copy = pltpu.make_async_copy(codes, heard, sem)
    copy.start()
    return copy


def list_all(messages, places, heard, todo):
    blocks = messages[0].shape[0] - GHOST_TILES
    count = jnp.int32(0)
    ends = [count]
    for number, (message, (theirs, ours, ghost)) in enumerate(zip(messages, places)):
        count = list_far(count, message, heard, number, theirs, ours, ghost, blocks, todo)
        ends.append(count)
    return ends


def far_pairs(messages, ends, tiles, sums, spread, picked, todo, buffers):
    spare = tiles.shape[0] - 1
    count = ends[-1]
    for number, message in enumerate(messages):

        def pick(index, carry, message=message):
            picked[index] = scale(message[todo[index] % 64])
            return carry

        lax.fori_loop(ends[number], ends[number + 1], pick, 0)
    for extra in range(2 * GROUP):
        todo[count + extra] = spare * 64
        picked[count + extra] = tiles[spare, 0:ROWS]

    def load(index):
        return todo[index] // 64, picked[index]

    def columns(item, wide):
        pair_columns(item[1], tiles[item[0], ROWS:], spread, wide)

    def scalars(item, wide, coef):
        pair_scalars(tiles[item[0], 0:ROWS], wide, coef)

    def add(item, coef):
        add_back(item[0], features(item[1]), sums, coef)

    run_pairs(count, buffers, load, columns, scalars, add)


def early_kernel(state, table, feats):
    for slot in range(table.shape[0]):
        rows = scale(state[slot])
        table[slot, 0:ROWS] = rows
        table[slot, ROWS:] = mirror(rows)
        feats[slot] = features(rows)


def slab_kernel(
    to_a, to_b, to_sub, from_a, from_b, table, early_feats, totals, tiles, feats, far_todo, new, sums, *rest
):
    spread, picked, codes, heard, todo, sem = rest[:6]
    buffers = rest[6:]
    own_tiles = to_sub.shape[0]
    size = GHOST_TILES
    blocks = own_tiles - size
    codes[7:8, :] = to_sub[blocks, 13:14, :].astype(jnp.int32)
    copy = hear([to_sub, from_a, from_b], blocks, codes, heard, sem)
    spare = tiles.shape[0] - 1

    def enter(slot, tile):
        rows = scale(tile)
        tiles[slot, 0:ROWS] = rows
        tiles[slot, ROWS:] = mirror(rows)
        return rows

    fill_spread(spread)
    copy.wait()
    shared = blocks + (2 + lax.axis_index("sub")) * size
    count = jnp.int32(0)
    for tile in range(blocks):
        for which in range(CHOICES):
            partner = heard[which, tile]
            mine = within(partner - shared, size)
            wanted = within(partner, blocks) | mine
            slot = jnp.where(mine, partner - shared + blocks, partner)
            todo[count] = tile * 64 + slot
            count = count + wanted.astype(jnp.int32)
    odd, _, _ = partners_of(lax.axis_index("slab"))
    low, high = blocks + odd * size, blocks + (1 - odd) * size
    places = [(high, low, own_tiles), (low, high, own_tiles + size)]
    ends = list_all([from_a, from_b], places, heard, far_todo)
    news = jnp.int32(0)
    for slot in range(blocks):
        new[news] = slot
        news = news + (heard[7, slot] == 0).astype(jnp.int32)
    sums[...] = jnp.zeros_like(sums)
    for slot in range(blocks):
        tiles[slot] = table[slot]
        feats[slot] = early_feats[slot]
    for tile in range(blocks, own_tiles):
        feats[tile] = features(enter(tile, to_sub[tile]))
    for tile in range(size):
        enter(own_tiles + tile, to_a[blocks + tile])
        enter(own_tiles + size + tile, to_b[blocks + tile])
    for tile in range(own_tiles + 2 * size, spare + 1):
        feats[spare] = features(enter(tile, jnp.ones((ROWS, LANES), f32)))

    def enter_new(index, carry):
        slot = new[index]
        feats[slot] = features(enter(slot, to_sub[slot]))
        return carry

    lax.fori_loop(0, news, enter_new, 0)
    for extra in range(2 * GROUP):
        todo[count + extra] = spare * 64 + spare

    def load(index):
        return todo[index] // 64, todo[index] % 64

    def columns(item, wide):
        pair_columns(tiles[item[0], 0:ROWS], tiles[item[1], ROWS:], spread, wide)

    def scalars(item, wide, coef):
        pair_scalars(tiles[item[1], 0:ROWS], wide, coef)

    def add(item, coef):
        first, second = item
        add_own(first, feats[second], sums, coef)
        add_back(second, feats[first], sums, coef)

    run_pairs(count, buffers, load, columns, scalars, add)
    far_pairs([from_a, from_b], ends, tiles, sums, spread, picked, far_todo, buffers)
    for group in range(tiles.shape[0] // 8):
        for row, value in enumerate(finish(group, sums, tiles)):
            totals[pl.ds(group * 64 + row, 8, stride=8), :] = value


def sub_kernel(before, tiles, state, extra, *rest):
    messages = rest[: -11 - 2 * GROUP]
    force, torque, kicked, totals, sums, spread, picked, codes, heard, todo, sem = rest[
        -11 - 2 * GROUP : -2 * GROUP
    ]
    buffers = rest[-2 * GROUP :]
    size = GHOST_TILES
    blocks = state.shape[0] - size
    copy = hear([state, *messages], blocks, codes, heard, sem)
    fill_spread(spread)
    copy.wait()
    sums[...] = jnp.zeros_like(sums)
    sub = lax.axis_index("sub")
    ours = blocks + (2 + sub) * size
    places = [
        (blocks + (2 + lax.bitwise_xor(sub, number + 1)) * size, ours, blocks)
        for number in range(len(messages))
    ]
    ends = list_all(messages, places, heard, todo)
    far_pairs(messages, ends, tiles, sums, spread, picked, todo, buffers)
    for group in range(tiles.shape[0] // 8):
        for row, value in enumerate(finish(group, sums, tiles)):
            part = pl.ds(group * 64 + row, 8, stride=8)
            totals[part, :] = before[part, :] + value
    settle(state, totals, extra[blocks], force, torque, kicked)


def settle(state, totals, extra, force, torque, kicked):
    odd, _, _ = partners_of(lax.axis_index("slab"))
    size = GHOST_TILES
    blocks = state.shape[0] - size
    lane_ids = lax.broadcasted_iota(jnp.int32, (LANES, LANES), 0)
    hots = []
    lefts = []
    for which in range(3):
        for tile in range(size):
            index = ghost_index(extra, which, tile, size, odd)
            hots.append(jnp.where(lane_ids == index % LANES, 1.0, 0.0).astype(bf16))
            ghost = blocks + (which + 1) % 3 * size + tile
            value = totals[ghost * 8 : ghost * 8 + 8, :]
            high = value.astype(bf16).astype(f32)
            both = jnp.concatenate([high, value - high], axis=0)
            source = jnp.broadcast_to(index // LANES, (ROWS, LANES))
            lefts.append(
                jnp.concatenate(
                    [
                        jnp.where(source == block, both, 0.0).astype(bf16)
                        for block in range(blocks)
                    ],
                    axis=0,
                )
            )
    added = dot_nt(jnp.concatenate(lefts, axis=1), jnp.concatenate(hots, axis=1))
    row_ids = lax.broadcasted_iota(jnp.int32, (8, LANES), 0)
    for block in range(blocks):
        columns = slice(block * LANES, (block + 1) * LANES)
        extra = added[block * ROWS : block * ROWS + 8] + added[block * ROWS + 8 : block * ROWS + 16]
        total = totals[block * 8 : block * 8 + 8, :] + extra
        radius = state[block, 9:10, :]
        mass = radius * radius * radius
        inertia = 0.4 * mass * radius * radius
        weight = jnp.where(row_ids < 3, time_step / mass, time_step / inertia)
        force[:, columns] = total[0:3]
        torque[:, columns] = total[3:6]
        kicked[:, columns] = state[block, 3:9, :] + (total * weight)[0:6]


def shape(*dims, dtype=f32):
    return jax.ShapeDtypeStruct(dims, dtype)


def body(positions, motion, radius, liquid, new_owner, ghost_rows, partner_tiles, live_pairs):
    per_dev = positions.shape[1]
    blocks = per_dev // LANES
    size = ghost_rows.shape[1] // LANES
    choices = partner_tiles.shape[0]
    tiles = -(-(blocks + 3 * size + 1) // 8) * 8
    slabs = lax.axis_size("slab")
    subs = lax.axis_size("sub")
    inside = [(i, i ^ 1) for i in range(slabs) if i ^ 1 < slabs]
    across = [(i, (i - 1 ^ 1) + 1) for i in range(1, slabs) if (i - 1 ^ 1) + 1 < slabs]

    state, swap_a, swap_b = pl.pallas_call(
        pack_kernel,
        out_shape=(
            shape(blocks + 1, ROWS, LANES),
            shape(CAP, ROWS, LANES),
            shape(CAP, ROWS, LANES),
        ),
        in_specs=[HBM] * 9,
        out_specs=(VMEM,) * 3,
        scratch_shapes=[
            pltpu.SMEM((blocks,), jnp.int32),
            pltpu.VMEM((3, per_dev), f32),
            pltpu.VMEM((6, per_dev), f32),
            pltpu.VMEM((blocks, LANES), f32),
            pltpu.VMEM((blocks, LANES), f32),
            pltpu.VMEM(ghost_rows.shape, jnp.int32),
            pltpu.VMEM(partner_tiles.shape, jnp.int32),
            pltpu.VMEM((1, blocks), jnp.int32),
            pltpu.VMEM((1, blocks), jnp.int32),
            pltpu.VMEM((blocks, ROWS, LANES), f32),
            pltpu.SemaphoreType.DMA((9,)),
        ],
        compiler_params=pltpu.CompilerParams(vmem_limit_bytes=60 * 1024 * 1024),
        name="pack",
    )(
        new_owner,
        positions,
        motion,
        radius.reshape(blocks, LANES),
        liquid.reshape(blocks, LANES),
        ghost_rows,
        partner_tiles,
        live_pairs.reshape(1, blocks),
        new_owner.reshape(1, blocks),
    )
    low = lax.ppermute(swap_a, "slab", inside)
    high = lax.ppermute(swap_b, "slab", across)
    early = pl.pallas_call(
        early_kernel,
        out_shape=(
            shape(blocks, 3 * ROWS, LANES),
            shape(blocks, 3 * FEATS, LANES, dtype=bf16),
        ),
        in_specs=[VMEM],
        out_specs=(VMEM, VMEM),
        compiler_params=PARAMS,
        cost_estimate=pl.CostEstimate(flops=4000000, bytes_accessed=1000000, transcendentals=0),
        name="early",
    )(state)
    to_a, to_b, to_sub = pl.pallas_call(
        place_kernel,
        out_shape=(shape(blocks + size, ROWS, LANES),) * 3,
        in_specs=[VMEM] * 3 + [pl.BlockSpec(memory_space=pl.ANY)],
        out_specs=(VMEM,) * 3,
        compiler_params=PARAMS,
        name="place",
    )(state, low, high, early[0])
    from_a = lax.ppermute(to_a, "slab", inside)
    from_b = lax.ppermute(to_b, "slab", across)
    from_sub = [
        lax.ppermute(to_sub, "sub", [(i, i ^ d) for i in range(subs)]) for d in range(1, subs)
    ]

    wides = [pltpu.VMEM((LANES, (len(WIDE_ROWS) + 2) * LANES), f32)] * GROUP

    def work(messages):
        room = choices * blocks * (1 + messages) + 2 * GROUP
        return [
            pltpu.VMEM((tiles * MATS * FEATS, LANES), f32),
            pltpu.VMEM((6 * ROWS, len(WIDE_ROWS) * LANES), bf16),
            pltpu.VMEM((room, ROWS, LANES), f32),
            pltpu.VMEM((8, LANES), jnp.int32),
            pltpu.SMEM((8, LANES), jnp.int32),
            pltpu.SMEM((room,), jnp.int32),
            pltpu.SemaphoreType.DMA(()),
        ] + wides + [pltpu.VMEM((MATS * LANES, 2 * LANES), bf16)] * GROUP

    totals, table = pl.pallas_call(
        slab_kernel,
        out_shape=(shape(tiles * 8, LANES), shape(tiles, 3 * ROWS, LANES)),
        in_specs=[VMEM] * 7,
        out_specs=(VMEM, VMEM),
        scratch_shapes=[
            pltpu.VMEM((tiles, 3 * FEATS, LANES), bf16),
            pltpu.SMEM((3 * choices * blocks + 2 * GROUP,), jnp.int32),
            pltpu.SMEM((blocks + 1,), jnp.int32),
        ]
        + work(2),
        compiler_params=PARAMS,
        cost_estimate=pl.CostEstimate(flops=90000000, bytes_accessed=400000, transcendentals=0),
        name="slab_pairs",
    )(to_a, to_b, to_sub, from_a, from_b, *early)
    return tuple(
        pl.pallas_call(
            sub_kernel,
            out_shape=(shape(3, per_dev), shape(3, per_dev), shape(6, per_dev)),
            in_specs=[VMEM] * (4 + len(from_sub)),
            out_specs=(VMEM,) * 3,
            scratch_shapes=[pltpu.VMEM((tiles * 8, LANES), f32)] + work(len(from_sub)),
            compiler_params=PARAMS,
            name="sub_pairs",
        )(totals, table, to_sub, state, *from_sub)
    )


def solution(mesh):
    return jax.shard_map(
        body,
        mesh=mesh,
        in_specs=(
            P(None, ("slab", "sub")),
            P(None, ("slab", "sub")),
            P(("slab", "sub")),
            P(("slab", "sub")),
            P(("slab", "sub")),
            P(None, ("slab", "sub")),
            P(None, ("slab", "sub")),
            P(("slab", "sub")),
        ),
        out_specs=(P(None, ("slab", "sub")), P(None, ("slab", "sub")), P(None, ("slab", "sub"))),
        check_vma=False,
    )
```

```python
import jax
import jax.numpy as jnp
from jax import lax
from jax.experimental import pallas as pl
from jax.experimental.pallas import tpu as pltpu
from jax.sharding import PartitionSpec as P

min_distance = 0.2
stiffness = 1.0
normal_damp = 0.5
shear_damp = 0.3
surface_tension = 2.0
rupture_scale = 1.0
time_step = 0.005

LANES = 128
ROWS = 16
CAP = 4
FEATS = 16
MATS = 5
WIDE_ROWS = (0, 1, 2, 9, 10, 11)
GROUP = 3
LEAN = 12
CHOICES = 2
GHOST_TILES = 4

f32 = jnp.float32
bf16 = jnp.bfloat16
VMEM = pl.BlockSpec(memory_space=pltpu.VMEM)
HBM = pl.BlockSpec(memory_space=pltpu.HBM)
PARAMS = pltpu.CompilerParams(vmem_limit_bytes=40 * 1024 * 1024)


def split(value, parts):
    out = []
    for _ in range(parts - 1):
        high = value.astype(bf16)
        out.append(high)
        value = value - high.astype(f32)
    out.append(value.astype(bf16))
    return out


def dot_nn(left, right):
    return lax.dot_general(left, right, (((1,), (0,)), ((), ())), preferred_element_type=f32)


def dot_nt(left, right):
    return lax.dot_general(left, right, (((1,), (1,)), ((), ())), preferred_element_type=f32)


def partners_of(here):
    odd = lax.rem(here, 2)
    return odd, here + 1 - 2 * odd, here - 1 + 2 * odd


def pack_kernel(*refs):
    sources, (state, swap_a, swap_b) = refs[:9], refs[9:12]
    moving, leave_a, leave_b, sems = refs[-4:]
    goal, place, speed, size, wet, rows, partners, live, goals = refs[12:-4]
    copies = [
        pltpu.make_async_copy(source, target, sems.at[index])
        for index, (source, target) in enumerate(zip(sources, refs[12:-4]))
    ]
    for copy in copies:
        copy.start()
    here = lax.axis_index("slab")
    _, slab_a, slab_b = partners_of(here)
    blocks = state.shape[0] - 1
    leave_a[...] = jnp.zeros_like(leave_a)
    leave_b[...] = jnp.zeros_like(leave_b)
    for copy in copies:
        copy.wait()
    count_a = jnp.int32(0)
    count_b = jnp.int32(0)
    for block in range(blocks):
        columns = slice(block * LANES, (block + 1) * LANES)
        target = goal[block]
        moving[block, 0:3, :] = place[:, columns]
        moving[block, 3:9, :] = speed[:, columns]
        moving[block, 9:10, :] = size[block : block + 1, :]
        moving[block, 10:11, :] = wet[block : block + 1, :]
        moving[block, 11:16, :] = jnp.full((5, LANES), (target + 1).astype(f32), f32)
        slab = lax.div(target, blocks)
        goes_a = slab == slab_a
        goes_b = slab == slab_b

        tile = moving[block]
        state[jnp.where(slab == here, lax.rem(target, blocks), blocks)] = tile
        leave_a[jnp.where(goes_a, count_a, CAP)] = tile
        leave_b[jnp.where(goes_b, count_b, CAP)] = tile
        count_a = jnp.minimum(count_a + goes_a.astype(jnp.int32), CAP - 1)
        count_b = jnp.minimum(count_b + goes_b.astype(jnp.int32), CAP - 1)
    swap_a[...] = leave_a[0:CAP]
    swap_b[...] = leave_b[0:CAP]
    state[blocks] = jnp.zeros((ROWS, LANES), f32)
    tiles = rows.shape[1] // LANES
    for which in range(3):
        for tile in range(tiles):
            state[blocks, which * tiles + tile : which * tiles + tile + 1, :] = rows[
                which : which + 1, tile * LANES : (tile + 1) * LANES
            ].astype(f32)
    for which in range(partners.shape[0]):
        state[blocks, 12 + which : 13 + which, 0:blocks] = jnp.where(
            live[...] > which, partners[which : which + 1, :], -1
        ).astype(f32)
    slots = lax.broadcasted_iota(jnp.int32, (LANES, blocks), 0)
    filled = jnp.where((goals[...] - here * blocks == slots) & (slots < blocks), 1.0, 0.0)
    counts = dot_nt(jnp.ones((8, blocks), bf16), filled.astype(bf16))
    state[blocks, 14:15, :] = counts[0:1, :]


def ghost_index(extra, which, tile, tiles, odd):
    rows = [extra[other * tiles + tile : other * tiles + tile + 1, :] for other in range(3)]
    row = rows[2] if which == 2 else jnp.where(odd == which, rows[1], rows[0])
    return row.astype(jnp.int32)


def place_kernel(state, low, high, _, to_a, to_b, to_sub, lean):
    here = lax.axis_index("slab")
    odd, _, _ = partners_of(here)
    blocks = state.shape[0] - 1
    size = to_sub.shape[0] - blocks
    extra = state[blocks]
    base = (here * blocks + 1).astype(f32)
    arrived = [low[slot] for slot in range(CAP)] + [high[slot] for slot in range(CAP)]
    tags = [jnp.broadcast_to(block[11:12, :], (ROWS, LANES)) - base for block in arrived]
    for slot in range(blocks):
        current = state[slot]
        for block, tag in zip(arrived, tags):
            current = jnp.where(tag == float(slot), block, current)
        to_sub[slot] = current
        to_a[slot] = current
        to_b[slot] = current
        lean[slot * LEAN : (slot + 1) * LEAN, :] = current[0:LEAN]

    flat = to_sub[0:blocks].reshape(blocks * ROWS, LANES)
    left = jnp.concatenate(split(flat, 3), axis=1)
    lane_ids = lax.broadcasted_iota(jnp.int32, (LANES, LANES), 0)
    for which, message in enumerate((to_a, to_b, to_sub)):
        for tile in range(message.shape[0] - blocks):
            index = ghost_index(extra, which, tile, size, odd)
            hot = jnp.where(lane_ids == index % LANES, 1.0, 0.0).astype(bf16)
            picked = dot_nn(left, jnp.concatenate([hot, hot, hot], axis=0))
            source = jnp.broadcast_to(index // LANES, (ROWS, LANES))
            total = jnp.zeros((ROWS, LANES), f32)
            for block in range(blocks):
                total = jnp.where(source == block, picked[block * ROWS : (block + 1) * ROWS], total)
            message[blocks + tile] = total
            if which == 2:
                start = (blocks + tile) * LEAN
                lean[start : start + LEAN, :] = total[0:LEAN]
        message[blocks, 11:14, :] = extra[12:15, :]
    lean[(blocks + size) * LEAN :, :] = extra[8:16, :]


def cross(first, second):
    return [
        first[1] * second[2] - first[2] * second[1],
        first[2] * second[0] - first[0] * second[2],
        first[0] * second[1] - first[1] * second[0],
    ]


def recip(value):
    return pl.reciprocal(value, approx=True)


def dot_rows(first, second):
    return first[0] * second[0] + first[1] * second[1] + first[2] * second[2]


def scale(tile):
    radius, liquid = tile[9:10, :], tile[10:11, :]
    turn = radius * tile[6:9, :]
    bond = radius * jnp.sqrt(surface_tension * liquid)
    place = [tile[row : row + 1, :] for row in range(3)]
    along = dot_rows(place, [tile[row : row + 1, :] for row in range(3, 6)])
    twist = dot_rows(place, [turn[row : row + 1, :] for row in range(3)])
    one = jnp.ones((1, LANES), f32)
    return jnp.concatenate(
        [tile[0:6, :], turn, radius, rupture_scale * liquid, bond, along, one, twist, 0.0 * one],
        axis=0,
    )


def mirror(scaled):
    place, velocity, turn = scaled[0:3, :], scaled[3:6, :], scaled[6:9, :]
    along, one, twist, zero = [scaled[row : row + 1, :] for row in range(12, 16)]
    blank = jnp.broadcast_to(zero, (6, LANES))
    damp = normal_damp - shear_damp
    moving = jnp.concatenate([-velocity, -place, blank, one, along, zero, zero], axis=0)
    turning = jnp.concatenate(
        [-turn, blank[0:3], place, blank[0:3], zero, twist, -one, zero], axis=0
    )
    return jnp.concatenate([damp * moving, turning], axis=0)


def six(value, order):
    parts = split(value, 3)
    return jnp.concatenate([parts[index] for index in order], axis=0)


def features(scaled):
    rows = [scaled[row : row + 1, :] for row in range(9)]
    place, velocity, turn = rows[0:3], rows[3:6], rows[6:9]
    one = jnp.ones((1, LANES), f32)
    values = jnp.concatenate(
        place + [one] + velocity + turn + cross(turn, place) + cross(place, velocity), axis=0
    )
    return jnp.concatenate(split(values, 3), axis=0)


def fill_spread(spread):
    rows = lax.broadcasted_iota(jnp.int32, (6 * ROWS, LANES), 0)
    part = rows // ROWS
    first = (part == 0) | (part == 3) | (part == 5)
    for block, row in enumerate(WIDE_ROWS):
        hot = first & (rows % ROWS == row)
        spread[:, block * LANES : (block + 1) * LANES] = jnp.where(hot, 1.0, 0.0).astype(bf16)


def pair_columns(near, far_mirror, spread, wide):
    moving = six(far_mirror[0:ROWS], (0, 1, 2, 0, 1, 0))
    turning = six(far_mirror[ROWS:], (0, 1, 2, 0, 1, 0))
    wide[...] = lax.dot_general(
        six(near, (0, 0, 0, 1, 1, 2)),
        jnp.concatenate([spread[...], moving, turning], axis=1),
        (((0,), (0,)), ((), ())),
        preferred_element_type=f32,
    )


def pair_scalars(far, wide, coefs):
    far_rows = [far[row : row + 1, :] for row in WIDE_ROWS]
    step = 16
    for start in range(0, LANES, step):
        col = [
            wide[start : start + step, block * LANES : (block + 1) * LANES] for block in range(8)
        ]
        offset = [far_rows[row] - col[row] for row in range(3)]
        along, twist = col[6], col[7]
        square = dot_rows(offset, offset)
        root = lax.rsqrt(jnp.maximum(square, 1e-30))
        inverse = jnp.minimum(root, 1.0 / min_distance)
        gap = square * root - (far_rows[3] + col[3])
        apart = jnp.maximum(gap, 0.0)
        overlap = apart - gap
        over_radii = recip(far_rows[3] + col[3])
        inner = far_rows[3] * col[3] * over_radii * overlap
        spread_pair = inner * lax.rsqrt(jnp.maximum(inner, 1e-30))
        fill = jnp.maximum(1.0 - apart * recip(far_rows[4] + col[4]), 0.0)
        bridge = far_rows[5] * col[5] * over_radii * (fill * fill)
        inverse1 = spread_pair * inverse
        inverse2 = inverse1 * inverse
        mats = [
            (bridge - spread_pair * (overlap - along * inverse)) * inverse,
            spread_pair,
            inverse1,
            inverse2 * square,
            inverse2 * twist,
        ]
        for index, mat in enumerate(mats):
            high, low = split(mat, 2)
            coefs[index * LANES + start : index * LANES + start + step, 0:LANES] = high
            coefs[index * LANES + start : index * LANES + start + step, LANES:] = low


def add_own(first, far_feats, sums, coefs):
    own = dot_nt(jnp.concatenate([far_feats, far_feats], axis=1), coefs[...])
    own = own[0:FEATS] + own[FEATS : 2 * FEATS] + own[2 * FEATS :]
    base = pl.multiple_of(first * (MATS * FEATS), 16)
    for index in range(MATS):
        sums[pl.ds(base + index * FEATS, FEATS), :] += own[:, index * LANES : (index + 1) * LANES]


def add_back(second, near_feats, sums, coefs):
    base = pl.multiple_of(second * (MATS * FEATS), 16)
    for index in range(MATS):
        back = dot_nn(near_feats, coefs[index * LANES : (index + 1) * LANES, :])
        back = back[:, 0:LANES] + back[:, LANES:]
        back = back[0:FEATS] + back[FEATS : 2 * FEATS] + back[2 * FEATS :]
        if index == MATS - 1:
            back = -back
        sums[pl.ds(base + index * FEATS, FEATS), :] += back


def finish(group, sums, scaled):
    span = MATS * FEATS

    def total(mat, feat):
        return sums[pl.ds(group * 8 * span + mat * FEATS + feat, 8, stride=span), :]

    def own(row):
        return scaled[pl.ds(group * 8, 8), row, :]

    place = [own(row) for row in range(3)]
    velocity = [own(row) for row in range(3, 6)]
    turn = [own(row) for row in range(6, 9)]
    radius = own(9)
    s_place = [total(0, feat) for feat in range(3)]
    s_one = total(0, 3)
    c_one = total(1, 3)
    c_velocity = [total(1, feat) for feat in range(4, 7)]
    n_place = [total(2, feat) for feat in range(3)]
    n_one = total(2, 3)
    n_velocity = [total(2, feat) for feat in range(4, 7)]
    n_turn = [total(2, feat) for feat in range(7, 10)]
    n_turn_place = [total(2, feat) for feat in range(10, 13)]
    n_place_velocity = [total(2, feat) for feat in range(13, 16)]
    k_one = total(3, 3)
    k_turn = [total(3, feat) for feat in range(7, 10)]
    g_place = [total(4, feat) for feat in range(3)]
    g_one = total(4, 3)
    turn_place = cross(turn, place)
    place_velocity = cross(place, velocity)
    first = cross(turn, n_place)
    second = cross(n_turn, place)
    third = cross(n_place, velocity)
    fourth = cross(place, n_velocity)
    force = [
        (s_place[x] - place[x] * s_one)
        + shear_damp
        * (
            (c_velocity[x] - velocity[x] * c_one)
            - (first[x] - turn_place[x] * n_one + n_turn_place[x] - second[x])
        )
        for x in range(3)
    ]
    torque = [
        shear_damp
        * radius
        * (
            (n_place_velocity[x] - third[x] - fourth[x] + place_velocity[x] * n_one)
            - (turn[x] * k_one + k_turn[x])
            + (g_place[x] - place[x] * g_one)
        )
        for x in range(3)
    ]
    return force + torque


def run_pairs(count, buffers, load, columns, scalars, add):
    wides, coefs = buffers[:GROUP], buffers[GROUP:]
    groups = jnp.maximum((count + GROUP - 1) // GROUP, 1)

    def items(group):
        return [load(group * GROUP + lane) for lane in range(GROUP)]

    for item, wide in zip(items(0), wides):
        columns(item, wide)
    for item, later, wide, coef in zip(items(0), items(1), wides, coefs):
        scalars(item, wide, coef)
        columns(later, wide)

    def step(group, carry):
        for item, following, later, wide, coef in zip(
            items(group), items(group + 1), items(group + 2), wides, coefs
        ):
            add(item, coef)
            scalars(following, wide, coef)
            columns(later, wide)
        return carry

    lax.fori_loop(0, groups - 1, step, 0)
    for item, coef in zip(items(groups - 1), coefs):
        add(item, coef)


def within(shift, size):
    return shift.astype(jnp.uint32) < jnp.uint32(size)


def list_far(count, heard, number, theirs, ours, ghost, blocks, todo):
    size = GHOST_TILES
    for tile in range(blocks):
        for which in range(CHOICES):
            shift = heard[which, tile] - theirs
            wanted = within(shift, size)
            todo[count] = tile * 64 + blocks + shift
            count = count + wanted.astype(jnp.int32)
            shift = heard[(number + 1) * CHOICES + which, tile] - ours
            wanted = within(shift, size)
            todo[count] = (ghost + shift) * 64 + tile
            count = count + wanted.astype(jnp.int32)
    return count


def hear(rows, codes, heard, sem):
    for number, pair in enumerate(rows):
        codes[number * CHOICES : (number + 1) * CHOICES, :] = pair.astype(jnp.int32)
    copy = pltpu.make_async_copy(codes, heard, sem)
    copy.start()
    return copy


def list_all(places, blocks, heard, todo):
    count = jnp.int32(0)
    ends = [count]
    for number, (theirs, ours, ghost) in enumerate(places):
        count = list_far(count, heard, number, theirs, ours, ghost, blocks, todo)
        ends.append(count)
    return ends


def far_pairs(messages, ends, tiles, sums, spread, picked, todo, buffers):
    spare = tiles.shape[0] - 1
    count = ends[-1]
    for number, message in enumerate(messages):

        def pick(index, carry, message=message):
            slot = lax.rem(todo[index], 64)
            if len(message.shape) == 3:
                tile = message[slot]
            else:
                tile = message[pl.ds(slot * LEAN, LEAN), :]
            picked[index] = scale(tile)
            return carry

        lax.fori_loop(ends[number], ends[number + 1], pick, 0)
    for extra in range(2 * GROUP):
        todo[count + extra] = spare * 64
        picked[count + extra] = tiles[spare, 0:ROWS]

    def load(index):
        return todo[index] // 64, picked[index]

    def columns(item, wide):
        pair_columns(item[1], tiles[item[0], ROWS:], spread, wide)

    def scalars(item, wide, coef):
        pair_scalars(tiles[item[0], 0:ROWS], wide, coef)

    def add(item, coef):
        add_back(item[0], features(item[1]), sums, coef)

    run_pairs(count, buffers, load, columns, scalars, add)


def early_kernel(state, table, feats):
    for slot in range(table.shape[0]):
        rows = scale(state[slot])
        table[slot, 0:ROWS] = rows
        table[slot, ROWS:] = mirror(rows)
        feats[slot] = features(rows)


def slab_kernel(
    to_a, to_b, to_sub, from_a, from_b, table, early_feats, totals, tiles, feats, far_todo, new, sums, *rest
):
    spread, picked, codes, heard, todo, sem = rest[:6]
    buffers = rest[6:]
    own_tiles = to_sub.shape[0]
    size = GHOST_TILES
    blocks = own_tiles - size
    codes[7:8, :] = to_sub[blocks, 13:14, :].astype(jnp.int32)
    rows = [message[blocks, 11:13, :] for message in (to_sub, from_a, from_b)]
    copy = hear(rows, codes, heard, sem)
    spare = tiles.shape[0] - 1

    def enter(slot, tile):
        rows = scale(tile)
        tiles[slot, 0:ROWS] = rows
        tiles[slot, ROWS:] = mirror(rows)
        return rows

    fill_spread(spread)
    copy.wait()
    shared = blocks + (2 + lax.axis_index("sub")) * size
    count = jnp.int32(0)
    for tile in range(blocks):
        for which in range(CHOICES):
            partner = heard[which, tile]
            mine = within(partner - shared, size)
            wanted = within(partner, blocks) | mine
            slot = jnp.where(mine, partner - shared + blocks, partner)
            todo[count] = tile * 64 + slot
            count = count + wanted.astype(jnp.int32)
    odd, _, _ = partners_of(lax.axis_index("slab"))
    low, high = blocks + odd * size, blocks + (1 - odd) * size
    places = [(high, low, own_tiles), (low, high, own_tiles + size)]
    ends = list_all(places, blocks, heard, far_todo)
    news = jnp.int32(0)
    for slot in range(blocks):
        new[news] = slot
        news = news + (heard[7, slot] == 0).astype(jnp.int32)
    sums[...] = jnp.zeros_like(sums)
    for slot in range(blocks):
        tiles[slot] = table[slot]
        feats[slot] = early_feats[slot]
    for tile in range(blocks, own_tiles):
        feats[tile] = features(enter(tile, to_sub[tile]))
    for tile in range(size):
        enter(own_tiles + tile, to_a[blocks + tile])
        enter(own_tiles + size + tile, to_b[blocks + tile])
    for tile in range(own_tiles + 2 * size, spare + 1):
        feats[spare] = features(enter(tile, jnp.ones((ROWS, LANES), f32)))

    def enter_new(index, carry):
        slot = new[index]
        feats[slot] = features(enter(slot, to_sub[slot]))
        return carry

    lax.fori_loop(0, news, enter_new, 0)
    for extra in range(2 * GROUP):
        todo[count + extra] = spare * 64 + spare

    def load(index):
        return todo[index] // 64, todo[index] % 64

    def columns(item, wide):
        pair_columns(tiles[item[0], 0:ROWS], tiles[item[1], ROWS:], spread, wide)

    def scalars(item, wide, coef):
        pair_scalars(tiles[item[1], 0:ROWS], wide, coef)

    def add(item, coef):
        first, second = item
        add_own(first, feats[second], sums, coef)
        add_back(second, feats[first], sums, coef)

    run_pairs(count, buffers, load, columns, scalars, add)
    far_pairs([from_a, from_b], ends, tiles, sums, spread, picked, far_todo, buffers)
    for group in range(tiles.shape[0] // 8):
        for row, value in enumerate(finish(group, sums, tiles)):
            totals[pl.ds(group * 64 + row, 8, stride=8), :] = value


def sub_kernel(before, tiles, state, extra, *rest):
    messages = rest[: -11 - 2 * GROUP]
    force, torque, kicked, totals, sums, spread, picked, codes, heard, todo, sem = rest[
        -11 - 2 * GROUP : -2 * GROUP
    ]
    buffers = rest[-2 * GROUP :]
    size = GHOST_TILES
    blocks = state.shape[0] - size
    last = (blocks + size) * LEAN + 4
    rows = [state[blocks, 11:13, :]] + [message[last : last + 2, :] for message in messages]
    copy = hear(rows, codes, heard, sem)
    fill_spread(spread)
    copy.wait()
    sums[...] = jnp.zeros_like(sums)
    sub = lax.axis_index("sub")
    ours = blocks + (2 + sub) * size
    places = [
        (blocks + (2 + lax.bitwise_xor(sub, len(messages) - number)) * size, ours, blocks)
        for number in range(len(messages))
    ]
    ends = list_all(places, blocks, heard, todo)
    far_pairs(messages, ends, tiles, sums, spread, picked, todo, buffers)
    for group in range(tiles.shape[0] // 8):
        for row, value in enumerate(finish(group, sums, tiles)):
            part = pl.ds(group * 64 + row, 8, stride=8)
            totals[part, :] = before[part, :] + value
    settle(state, totals, extra[blocks], force, torque, kicked)


def settle(state, totals, extra, force, torque, kicked):
    odd, _, _ = partners_of(lax.axis_index("slab"))
    size = GHOST_TILES
    blocks = state.shape[0] - size
    lane_ids = lax.broadcasted_iota(jnp.int32, (LANES, LANES), 0)
    hots = []
    lefts = []
    for which in range(3):
        for tile in range(size):
            index = ghost_index(extra, which, tile, size, odd)
            hots.append(jnp.where(lane_ids == index % LANES, 1.0, 0.0).astype(bf16))
            ghost = blocks + (which + 1) % 3 * size + tile
            value = totals[ghost * 8 : ghost * 8 + 8, :]
            high = value.astype(bf16).astype(f32)
            both = jnp.concatenate([high, value - high], axis=0)
            source = jnp.broadcast_to(index // LANES, (ROWS, LANES))
            lefts.append(
                jnp.concatenate(
                    [
                        jnp.where(source == block, both, 0.0).astype(bf16)
                        for block in range(blocks)
                    ],
                    axis=0,
                )
            )
    added = dot_nt(jnp.concatenate(lefts, axis=1), jnp.concatenate(hots, axis=1))
    row_ids = lax.broadcasted_iota(jnp.int32, (8, LANES), 0)
    for block in range(blocks):
        columns = slice(block * LANES, (block + 1) * LANES)
        extra = added[block * ROWS : block * ROWS + 8] + added[block * ROWS + 8 : block * ROWS + 16]
        total = totals[block * 8 : block * 8 + 8, :] + extra
        radius = state[block, 9:10, :]
        mass = radius * radius * radius
        inertia = 0.4 * mass * radius * radius
        weight = jnp.where(row_ids < 3, time_step / mass, time_step / inertia)
        force[:, columns] = total[0:3]
        torque[:, columns] = total[3:6]
        kicked[:, columns] = state[block, 3:9, :] + (total * weight)[0:6]


def shape(*dims, dtype=f32):
    return jax.ShapeDtypeStruct(dims, dtype)


def body(positions, motion, radius, liquid, new_owner, ghost_rows, partner_tiles, live_pairs):
    per_dev = positions.shape[1]
    blocks = per_dev // LANES
    size = ghost_rows.shape[1] // LANES
    choices = partner_tiles.shape[0]
    tiles = -(-(blocks + 3 * size + 1) // 8) * 8
    slabs = lax.axis_size("slab")
    subs = lax.axis_size("sub")
    inside = [(i, i ^ 1) for i in range(slabs) if i ^ 1 < slabs]
    across = [(i, (i - 1 ^ 1) + 1) for i in range(1, slabs) if (i - 1 ^ 1) + 1 < slabs]

    state, swap_a, swap_b = pl.pallas_call(
        pack_kernel,
        out_shape=(
            shape(blocks + 1, ROWS, LANES),
            shape(CAP, ROWS, LANES),
            shape(CAP, ROWS, LANES),
        ),
        in_specs=[HBM] * 9,
        out_specs=(VMEM,) * 3,
        scratch_shapes=[
            pltpu.SMEM((blocks,), jnp.int32),
            pltpu.VMEM((3, per_dev), f32),
            pltpu.VMEM((6, per_dev), f32),
            pltpu.VMEM((blocks, LANES), f32),
            pltpu.VMEM((blocks, LANES), f32),
            pltpu.VMEM(ghost_rows.shape, jnp.int32),
            pltpu.VMEM(partner_tiles.shape, jnp.int32),
            pltpu.VMEM((1, blocks), jnp.int32),
            pltpu.VMEM((1, blocks), jnp.int32),
            pltpu.VMEM((blocks, ROWS, LANES), f32),
            pltpu.VMEM((CAP + 1, ROWS, LANES), f32),
            pltpu.VMEM((CAP + 1, ROWS, LANES), f32),
            pltpu.SemaphoreType.DMA((9,)),
        ],
        compiler_params=pltpu.CompilerParams(vmem_limit_bytes=60 * 1024 * 1024),
        name="pack",
    )(
        new_owner,
        positions,
        motion,
        radius.reshape(blocks, LANES),
        liquid.reshape(blocks, LANES),
        ghost_rows,
        partner_tiles,
        live_pairs.reshape(1, blocks),
        new_owner.reshape(1, blocks),
    )
    low = lax.ppermute(swap_a, "slab", inside)
    high = lax.ppermute(swap_b, "slab", across)
    early = pl.pallas_call(
        early_kernel,
        out_shape=(
            shape(blocks, 3 * ROWS, LANES),
            shape(blocks, 3 * FEATS, LANES, dtype=bf16),
        ),
        in_specs=[VMEM],
        out_specs=(VMEM, VMEM),
        compiler_params=PARAMS,
        cost_estimate=pl.CostEstimate(flops=4000000, bytes_accessed=1000000, transcendentals=0),
        name="early",
    )(state)
    to_a, to_b, to_sub, lean = pl.pallas_call(
        place_kernel,
        out_shape=(shape(blocks + size, ROWS, LANES),) * 3
        + (shape((blocks + size) * LEAN + 8, LANES),),
        in_specs=[VMEM] * 3 + [pl.BlockSpec(memory_space=pl.ANY)],
        out_specs=(VMEM,) * 4,
        compiler_params=PARAMS,
        name="place",
    )(state, low, high, early[0])
    from_a = lax.ppermute(to_a, "slab", inside)
    from_b = lax.ppermute(to_b, "slab", across)
    from_sub = [
        lax.ppermute(lean, "sub", [(i, i ^ d) for i in range(subs)])
        for d in reversed(range(1, subs))
    ]

    wides = [pltpu.VMEM((LANES, (len(WIDE_ROWS) + 2) * LANES), f32)] * GROUP

    def work(messages):
        room = choices * blocks * (1 + messages) + 2 * GROUP
        return [
            pltpu.VMEM((tiles * MATS * FEATS, LANES), f32),
            pltpu.VMEM((6 * ROWS, len(WIDE_ROWS) * LANES), bf16),
            pltpu.VMEM((room, ROWS, LANES), f32),
            pltpu.VMEM((8, LANES), jnp.int32),
            pltpu.SMEM((8, LANES), jnp.int32),
            pltpu.SMEM((room,), jnp.int32),
            pltpu.SemaphoreType.DMA(()),
        ] + wides + [pltpu.VMEM((MATS * LANES, 2 * LANES), bf16)] * GROUP

    totals, table = pl.pallas_call(
        slab_kernel,
        out_shape=(shape(tiles * 8, LANES), shape(tiles, 3 * ROWS, LANES)),
        in_specs=[VMEM] * 7,
        out_specs=(VMEM, VMEM),
        scratch_shapes=[
            pltpu.VMEM((tiles, 3 * FEATS, LANES), bf16),
            pltpu.SMEM((3 * choices * blocks + 2 * GROUP,), jnp.int32),
            pltpu.SMEM((blocks + 1,), jnp.int32),
        ]
        + work(2),
        compiler_params=PARAMS,
        cost_estimate=pl.CostEstimate(flops=90000000, bytes_accessed=400000, transcendentals=0),
        name="slab_pairs",
    )(to_a, to_b, to_sub, from_a, from_b, *early)
    return tuple(
        pl.pallas_call(
            sub_kernel,
            out_shape=(shape(3, per_dev), shape(3, per_dev), shape(6, per_dev)),
            in_specs=[VMEM] * (4 + len(from_sub)),
            out_specs=(VMEM,) * 3,
            scratch_shapes=[pltpu.VMEM((tiles * 8, LANES), f32)] + work(len(from_sub)),
            compiler_params=PARAMS,
            name="sub_pairs",
        )(totals, table, to_sub, state, *from_sub)
    )


def solution(mesh):
    return jax.shard_map(
        body,
        mesh=mesh,
        in_specs=(
            P(None, ("slab", "sub")),
            P(None, ("slab", "sub")),
            P(("slab", "sub")),
            P(("slab", "sub")),
            P(("slab", "sub")),
            P(None, ("slab", "sub")),
            P(None, ("slab", "sub")),
            P(("slab", "sub")),
        ),
        out_specs=(P(None, ("slab", "sub")), P(None, ("slab", "sub")), P(None, ("slab", "sub"))),
        check_vma=False,
    )
```

```python
import jax
import jax.numpy as jnp
from jax import lax
from jax.experimental import pallas as pl
from jax.experimental.pallas import tpu as pltpu
from jax.sharding import PartitionSpec as P

min_distance = 0.2
stiffness = 1.0
normal_damp = 0.5
shear_damp = 0.3
surface_tension = 2.0
rupture_scale = 1.0
time_step = 0.005

LANES = 128
ROWS = 16
CAP = 4
FEATS = 16
MATS = 5
WIDE_ROWS = (0, 1, 2, 9, 10, 11)
GROUP = 3
LEAN = 12
CHOICES = 2
GHOST_TILES = 4

f32 = jnp.float32
bf16 = jnp.bfloat16
VMEM = pl.BlockSpec(memory_space=pltpu.VMEM)
HBM = pl.BlockSpec(memory_space=pltpu.HBM)
PARAMS = pltpu.CompilerParams(vmem_limit_bytes=40 * 1024 * 1024)


def split(value, parts):
    out = []
    for _ in range(parts - 1):
        high = value.astype(bf16)
        out.append(high)
        value = value - high.astype(f32)
    out.append(value.astype(bf16))
    return out


def dot_nn(left, right):
    return lax.dot_general(left, right, (((1,), (0,)), ((), ())), preferred_element_type=f32)


def dot_nt(left, right):
    return lax.dot_general(left, right, (((1,), (1,)), ((), ())), preferred_element_type=f32)


def partners_of(here):
    odd = lax.rem(here, 2)
    return odd, here + 1 - 2 * odd, here - 1 + 2 * odd


def pack_kernel(*refs):
    sources, (state, swap_a, swap_b) = refs[:9], refs[9:12]
    moving, leave_a, leave_b, sems = refs[-4:]
    goal, place, speed, size, wet, rows, partners, live, goals = refs[12:-4]
    copies = [
        pltpu.make_async_copy(source, target, sems.at[index])
        for index, (source, target) in enumerate(zip(sources, refs[12:-4]))
    ]
    for copy in copies:
        copy.start()
    here = lax.axis_index("slab")
    _, slab_a, slab_b = partners_of(here)
    blocks = state.shape[0] - 1
    leave_a[...] = jnp.zeros_like(leave_a)
    leave_b[...] = jnp.zeros_like(leave_b)
    for copy in copies:
        copy.wait()
    count_a = jnp.int32(0)
    count_b = jnp.int32(0)
    for block in range(blocks):
        columns = slice(block * LANES, (block + 1) * LANES)
        target = goal[block]
        moving[block, 0:3, :] = place[:, columns]
        moving[block, 3:9, :] = speed[:, columns]
        moving[block, 9:10, :] = size[block : block + 1, :]
        moving[block, 10:11, :] = wet[block : block + 1, :]
        moving[block, 11:16, :] = jnp.full((5, LANES), (target + 1).astype(f32), f32)
        slab = lax.div(target, blocks)
        goes_a = slab == slab_a
        goes_b = slab == slab_b

        tile = moving[block]
        state[jnp.where(slab == here, lax.rem(target, blocks), blocks)] = tile
        leave_a[jnp.where(goes_a, count_a, CAP)] = tile
        leave_b[jnp.where(goes_b, count_b, CAP)] = tile
        count_a = jnp.minimum(count_a + goes_a.astype(jnp.int32), CAP - 1)
        count_b = jnp.minimum(count_b + goes_b.astype(jnp.int32), CAP - 1)
    swap_a[...] = leave_a[0:CAP]
    swap_b[...] = leave_b[0:CAP]
    state[blocks] = jnp.zeros((ROWS, LANES), f32)
    tiles = rows.shape[1] // LANES
    for which in range(3):
        for tile in range(tiles):
            state[blocks, which * tiles + tile : which * tiles + tile + 1, :] = rows[
                which : which + 1, tile * LANES : (tile + 1) * LANES
            ].astype(f32)
    for which in range(partners.shape[0]):
        state[blocks, 12 + which : 13 + which, 0:blocks] = jnp.where(
            live[...] > which, partners[which : which + 1, :], -1
        ).astype(f32)
    slots = lax.broadcasted_iota(jnp.int32, (LANES, blocks), 0)
    filled = jnp.where((goals[...] - here * blocks == slots) & (slots < blocks), 1.0, 0.0)
    counts = dot_nt(jnp.ones((8, blocks), bf16), filled.astype(bf16))
    state[blocks, 14:15, :] = counts[0:1, :]


def ghost_index(extra, which, tile, tiles, odd):
    rows = [extra[other * tiles + tile : other * tiles + tile + 1, :] for other in range(3)]
    row = rows[2] if which == 2 else jnp.where(odd == which, rows[1], rows[0])
    return row.astype(jnp.int32)


def place_kernel(state, low, high, _, to_a, to_b, to_sub, lean):
    here = lax.axis_index("slab")
    odd, _, _ = partners_of(here)
    blocks = state.shape[0] - 1
    size = to_sub.shape[0] - blocks
    extra = state[blocks]
    base = (here * blocks + 1).astype(f32)
    arrived = [low[slot] for slot in range(CAP)] + [high[slot] for slot in range(CAP)]
    tags = [jnp.broadcast_to(block[11:12, :], (ROWS, LANES)) - base for block in arrived]
    for slot in range(blocks):
        current = state[slot]
        for block, tag in zip(arrived, tags):
            current = jnp.where(tag == float(slot), block, current)
        to_sub[slot] = current
        to_a[slot] = current
        to_b[slot] = current
        lean[slot * LEAN : (slot + 1) * LEAN, :] = current[0:LEAN]

    flat = to_sub[0:blocks].reshape(blocks * ROWS, LANES)
    left = jnp.concatenate(split(flat, 3), axis=1)
    lane_ids = lax.broadcasted_iota(jnp.int32, (LANES, LANES), 0)
    for which, message in enumerate((to_a, to_b, to_sub)):
        for tile in range(message.shape[0] - blocks):
            index = ghost_index(extra, which, tile, size, odd)
            hot = jnp.where(lane_ids == index % LANES, 1.0, 0.0).astype(bf16)
            picked = dot_nn(left, jnp.concatenate([hot, hot, hot], axis=0))
            source = jnp.broadcast_to(index // LANES, (ROWS, LANES))
            total = jnp.zeros((ROWS, LANES), f32)
            for block in range(blocks):
                total = jnp.where(source == block, picked[block * ROWS : (block + 1) * ROWS], total)
            message[blocks + tile] = total
            if which == 2:
                start = (blocks + tile) * LEAN
                lean[start : start + LEAN, :] = total[0:LEAN]
        message[blocks, 11:14, :] = extra[12:15, :]
    lean[(blocks + size) * LEAN :, :] = extra[8:16, :]


def cross(first, second):
    return [
        first[1] * second[2] - first[2] * second[1],
        first[2] * second[0] - first[0] * second[2],
        first[0] * second[1] - first[1] * second[0],
    ]


def recip(value):
    return pl.reciprocal(value, approx=True)


def dot_rows(first, second):
    return first[0] * second[0] + first[1] * second[1] + first[2] * second[2]


def scale(tile):
    radius, liquid = tile[9:10, :], tile[10:11, :]
    turn = radius * tile[6:9, :]
    bond = radius * jnp.sqrt(surface_tension * liquid)
    place = [tile[row : row + 1, :] for row in range(3)]
    along = dot_rows(place, [tile[row : row + 1, :] for row in range(3, 6)])
    twist = dot_rows(place, [turn[row : row + 1, :] for row in range(3)])
    one = jnp.ones((1, LANES), f32)
    return jnp.concatenate(
        [tile[0:6, :], turn, radius, rupture_scale * liquid, bond, along, one, twist, 0.0 * one],
        axis=0,
    )


def mirror(scaled):
    place, velocity, turn = scaled[0:3, :], scaled[3:6, :], scaled[6:9, :]
    along, one, twist, zero = [scaled[row : row + 1, :] for row in range(12, 16)]
    blank = jnp.broadcast_to(zero, (6, LANES))
    damp = normal_damp - shear_damp
    moving = jnp.concatenate([-velocity, -place, blank, one, along, zero, zero], axis=0)
    turning = jnp.concatenate(
        [-turn, blank[0:3], place, blank[0:3], zero, twist, -one, zero], axis=0
    )
    return jnp.concatenate([damp * moving, turning], axis=0)


def six(value, order):
    parts = split(value, 3)
    return jnp.concatenate([parts[index] for index in order], axis=0)


def features(scaled):
    rows = [scaled[row : row + 1, :] for row in range(9)]
    place, velocity, turn = rows[0:3], rows[3:6], rows[6:9]
    one = jnp.ones((1, LANES), f32)
    values = jnp.concatenate(
        place + [one] + velocity + turn + cross(turn, place) + cross(place, velocity), axis=0
    )
    return jnp.concatenate(split(values, 3), axis=0)


def fill_spread(spread):
    rows = lax.broadcasted_iota(jnp.int32, (6 * ROWS, LANES), 0)
    part = rows // ROWS
    first = (part == 0) | (part == 3) | (part == 5)
    for block, row in enumerate(WIDE_ROWS):
        hot = first & (rows % ROWS == row)
        spread[:, block * LANES : (block + 1) * LANES] = jnp.where(hot, 1.0, 0.0).astype(bf16)


def pair_columns(near, far_mirror, spread, wide):
    moving = six(far_mirror[0:ROWS], (0, 1, 2, 0, 1, 0))
    turning = six(far_mirror[ROWS:], (0, 1, 2, 0, 1, 0))
    wide[...] = lax.dot_general(
        six(near, (0, 0, 0, 1, 1, 2)),
        jnp.concatenate([spread[...], moving, turning], axis=1),
        (((0,), (0,)), ((), ())),
        preferred_element_type=f32,
    )


def pair_scalars(far, wide, coefs):
    far_rows = [far[row : row + 1, :] for row in WIDE_ROWS]
    step = 16
    for start in range(0, LANES, step):
        col = [
            wide[start : start + step, block * LANES : (block + 1) * LANES] for block in range(8)
        ]
        offset = [far_rows[row] - col[row] for row in range(3)]
        along, twist = col[6], col[7]
        square = dot_rows(offset, offset)
        root = lax.rsqrt(jnp.maximum(square, 1e-30))
        inverse = jnp.minimum(root, 1.0 / min_distance)
        gap = square * root - (far_rows[3] + col[3])
        apart = jnp.maximum(gap, 0.0)
        overlap = apart - gap
        over_radii = recip(far_rows[3] + col[3])
        inner = far_rows[3] * col[3] * over_radii * overlap
        spread_pair = inner * lax.rsqrt(jnp.maximum(inner, 1e-30))
        fill = jnp.maximum(1.0 - apart * recip(far_rows[4] + col[4]), 0.0)
        bridge = far_rows[5] * col[5] * over_radii * (fill * fill)
        inverse1 = spread_pair * inverse
        inverse2 = inverse1 * inverse
        mats = [
            (bridge - spread_pair * (overlap - along * inverse)) * inverse,
            spread_pair,
            inverse1,
            inverse2 * square,
            inverse2 * twist,
        ]
        for index, mat in enumerate(mats):
            high, low = split(mat, 2)
            coefs[index * LANES + start : index * LANES + start + step, 0:LANES] = high
            coefs[index * LANES + start : index * LANES + start + step, LANES:] = low


def add_own(first, far_feats, sums, coefs):
    own = dot_nt(jnp.concatenate([far_feats, far_feats], axis=1), coefs[...])
    own = own[0:FEATS] + own[FEATS : 2 * FEATS] + own[2 * FEATS :]
    base = pl.multiple_of(first * (MATS * FEATS), 16)
    for index in range(MATS):
        sums[pl.ds(base + index * FEATS, FEATS), :] += own[:, index * LANES : (index + 1) * LANES]


def add_back(second, near_feats, sums, coefs):
    base = pl.multiple_of(second * (MATS * FEATS), 16)
    for index in range(MATS):
        back = dot_nn(near_feats, coefs[index * LANES : (index + 1) * LANES, :])
        back = back[:, 0:LANES] + back[:, LANES:]
        back = back[0:FEATS] + back[FEATS : 2 * FEATS] + back[2 * FEATS :]
        if index == MATS - 1:
            back = -back
        sums[pl.ds(base + index * FEATS, FEATS), :] += back


def finish(group, sums, scaled):
    span = MATS * FEATS

    def total(mat, feat):
        return sums[pl.ds(group * 8 * span + mat * FEATS + feat, 8, stride=span), :]

    def own(row):
        return scaled[pl.ds(group * 8, 8), row, :]

    place = [own(row) for row in range(3)]
    velocity = [own(row) for row in range(3, 6)]
    turn = [own(row) for row in range(6, 9)]
    radius = own(9)
    s_place = [total(0, feat) for feat in range(3)]
    s_one = total(0, 3)
    c_one = total(1, 3)
    c_velocity = [total(1, feat) for feat in range(4, 7)]
    n_place = [total(2, feat) for feat in range(3)]
    n_one = total(2, 3)
    n_velocity = [total(2, feat) for feat in range(4, 7)]
    n_turn = [total(2, feat) for feat in range(7, 10)]
    n_turn_place = [total(2, feat) for feat in range(10, 13)]
    n_place_velocity = [total(2, feat) for feat in range(13, 16)]
    k_one = total(3, 3)
    k_turn = [total(3, feat) for feat in range(7, 10)]
    g_place = [total(4, feat) for feat in range(3)]
    g_one = total(4, 3)
    turn_place = cross(turn, place)
    place_velocity = cross(place, velocity)
    first = cross(turn, n_place)
    second = cross(n_turn, place)
    third = cross(n_place, velocity)
    fourth = cross(place, n_velocity)
    force = [
        (s_place[x] - place[x] * s_one)
        + shear_damp
        * (
            (c_velocity[x] - velocity[x] * c_one)
            - (first[x] - turn_place[x] * n_one + n_turn_place[x] - second[x])
        )
        for x in range(3)
    ]
    torque = [
        shear_damp
        * radius
        * (
            (n_place_velocity[x] - third[x] - fourth[x] + place_velocity[x] * n_one)
            - (turn[x] * k_one + k_turn[x])
            + (g_place[x] - place[x] * g_one)
        )
        for x in range(3)
    ]
    return force + torque


def run_pairs(count, buffers, load, columns, scalars, add):
    wides, coefs = buffers[:GROUP], buffers[GROUP:]
    groups = jnp.maximum((count + GROUP - 1) // GROUP, 1)

    def items(group):
        return [load(group * GROUP + lane) for lane in range(GROUP)]

    for item, wide in zip(items(0), wides):
        columns(item, wide)
    for item, later, wide, coef in zip(items(0), items(1), wides, coefs):
        scalars(item, wide, coef)
        columns(later, wide)

    def step(group, carry):
        for item, following, later, wide, coef in zip(
            items(group), items(group + 1), items(group + 2), wides, coefs
        ):
            add(item, coef)
            scalars(following, wide, coef)
            columns(later, wide)
        return carry

    lax.fori_loop(0, groups - 1, step, 0)
    for item, coef in zip(items(groups - 1), coefs):
        add(item, coef)


def within(shift, size):
    return shift.astype(jnp.uint32) < jnp.uint32(size)


def list_far(count, heard, number, theirs, ours, ghost, blocks, todo):
    size = GHOST_TILES
    for tile in range(blocks):
        for which in range(CHOICES):
            shift = heard[which, tile] - theirs
            wanted = within(shift, size)
            todo[count] = tile * 64 + blocks + shift
            count = count + wanted.astype(jnp.int32)
            shift = heard[(number + 1) * CHOICES + which, tile] - ours
            wanted = within(shift, size)
            todo[count] = (ghost + shift) * 64 + tile
            count = count + wanted.astype(jnp.int32)
    return count


def hear(rows, codes, heard, sem):
    for number, pair in enumerate(rows):
        codes[number * CHOICES : (number + 1) * CHOICES, :] = pair.astype(jnp.int32)
    copy = pltpu.make_async_copy(codes, heard, sem)
    copy.start()
    return copy


def list_all(places, blocks, heard, todo):
    count = jnp.int32(0)
    ends = [count]
    for number, (theirs, ours, ghost) in enumerate(places):
        count = list_far(count, heard, number, theirs, ours, ghost, blocks, todo)
        ends.append(count)
    return ends


def far_pairs(messages, ends, tiles, sums, spread, picked, todo, buffers):
    spare = tiles.shape[0] - 1
    count = ends[-1]
    for number, message in enumerate(messages):

        def pick(index, carry, message=message):
            slot = lax.rem(todo[index], 64)
            if len(message.shape) == 3:
                tile = message[slot]
            else:
                tile = message[pl.ds(slot * LEAN, LEAN), :]
            picked[index] = scale(tile)
            return carry

        lax.fori_loop(ends[number], ends[number + 1], pick, 0)
    for extra in range(2 * GROUP):
        todo[count + extra] = spare * 64
        picked[count + extra] = tiles[spare, 0:ROWS]

    def load(index):
        return todo[index] // 64, picked[index]

    def columns(item, wide):
        pair_columns(item[1], tiles[item[0], ROWS:], spread, wide)

    def scalars(item, wide, coef):
        pair_scalars(tiles[item[0], 0:ROWS], wide, coef)

    def add(item, coef):
        add_back(item[0], features(item[1]), sums, coef)

    run_pairs(count, buffers, load, columns, scalars, add)


def early_kernel(state, table, feats):
    for slot in range(table.shape[0]):
        rows = scale(state[slot])
        table[slot, 0:ROWS] = rows
        table[slot, ROWS:] = mirror(rows)
        feats[slot] = features(rows)


def slab_kernel(
    to_a, to_b, to_sub, from_a, from_b, table, early_feats, totals, tiles, feats, far_todo, new, sums, *rest
):
    spread, picked, codes, heard, todo, sem = rest[:6]
    buffers = rest[6:]
    own_tiles = to_sub.shape[0]
    size = GHOST_TILES
    blocks = own_tiles - size
    codes[7:8, :] = to_sub[blocks, 13:14, :].astype(jnp.int32)
    rows = [message[blocks, 11:13, :] for message in (to_sub, from_a, from_b)]
    copy = hear(rows, codes, heard, sem)
    spare = tiles.shape[0] - 1

    def enter(slot, tile):
        rows = scale(tile)
        tiles[slot, 0:ROWS] = rows
        tiles[slot, ROWS:] = mirror(rows)
        return rows

    fill_spread(spread)
    copy.wait()
    shared = blocks + (2 + lax.axis_index("sub")) * size
    count = jnp.int32(0)
    for tile in range(blocks):
        for which in range(CHOICES):
            partner = heard[which, tile]
            mine = within(partner - shared, size)
            wanted = within(partner, blocks) | mine
            slot = jnp.where(mine, partner - shared + blocks, partner)
            todo[count] = tile * 64 + slot
            count = count + wanted.astype(jnp.int32)
    odd, _, _ = partners_of(lax.axis_index("slab"))
    low, high = blocks + odd * size, blocks + (1 - odd) * size
    places = [(high, low, own_tiles), (low, high, own_tiles + size)]
    ends = list_all(places, blocks, heard, far_todo)
    news = jnp.int32(0)
    for slot in range(blocks):
        new[news] = slot
        news = news + (heard[7, slot] == 0).astype(jnp.int32)
    sums[...] = jnp.zeros_like(sums)
    for slot in range(blocks):
        tiles[slot] = table[slot]
        feats[slot] = early_feats[slot]
    for tile in range(blocks, own_tiles):
        feats[tile] = features(enter(tile, to_sub[tile]))
    for tile in range(size):
        enter(own_tiles + tile, to_a[blocks + tile])
        enter(own_tiles + size + tile, to_b[blocks + tile])
    for tile in range(own_tiles + 2 * size, spare + 1):
        feats[spare] = features(enter(tile, jnp.ones((ROWS, LANES), f32)))

    def enter_new(index, carry):
        slot = new[index]
        feats[slot] = features(enter(slot, to_sub[slot]))
        return carry

    lax.fori_loop(0, news, enter_new, 0)
    for extra in range(2 * GROUP):
        todo[count + extra] = spare * 64 + spare

    def load(index):
        return todo[index] // 64, todo[index] % 64

    def columns(item, wide):
        pair_columns(tiles[item[0], 0:ROWS], tiles[item[1], ROWS:], spread, wide)

    def scalars(item, wide, coef):
        pair_scalars(tiles[item[1], 0:ROWS], wide, coef)

    def add(item, coef):
        first, second = item
        add_own(first, feats[second], sums, coef)
        add_back(second, feats[first], sums, coef)

    run_pairs(count, buffers, load, columns, scalars, add)
    far_pairs([from_a, from_b], ends, tiles, sums, spread, picked, far_todo, buffers)
    for group in range(tiles.shape[0] // 8):
        for row, value in enumerate(finish(group, sums, tiles)):
            totals[pl.ds(group * 64 + row, 8, stride=8), :] = value


def sub_kernel(before, tiles, state, extra, *rest):
    messages = rest[: -11 - 2 * GROUP]
    force, torque, kicked, totals, sums, spread, picked, codes, heard, todo, sem = rest[
        -11 - 2 * GROUP : -2 * GROUP
    ]
    buffers = rest[-2 * GROUP :]
    size = GHOST_TILES
    blocks = state.shape[0] - size
    last = (blocks + size) * LEAN + 4
    rows = [state[blocks, 11:13, :]] + [message[last : last + 2, :] for message in messages]
    copy = hear(rows, codes, heard, sem)
    fill_spread(spread)
    copy.wait()
    sums[...] = jnp.zeros_like(sums)
    sub = lax.axis_index("sub")
    ours = blocks + (2 + sub) * size
    places = [
        (blocks + (2 + lax.bitwise_xor(sub, len(messages) - number)) * size, ours, blocks)
        for number in range(len(messages))
    ]
    ends = list_all(places, blocks, heard, todo)
    far_pairs(messages, ends, tiles, sums, spread, picked, todo, buffers)
    for group in range(tiles.shape[0] // 8):
        for row, value in enumerate(finish(group, sums, tiles)):
            part = pl.ds(group * 64 + row, 8, stride=8)
            totals[part, :] = before[part, :] + value
    settle(state, totals, extra[blocks], force, torque, kicked)


def settle(state, totals, extra, force, torque, kicked):
    odd, _, _ = partners_of(lax.axis_index("slab"))
    size = GHOST_TILES
    blocks = state.shape[0] - size
    lane_ids = lax.broadcasted_iota(jnp.int32, (LANES, LANES), 0)
    hots = []
    lefts = []
    for which in range(3):
        for tile in range(size):
            index = ghost_index(extra, which, tile, size, odd)
            hots.append(jnp.where(lane_ids == index % LANES, 1.0, 0.0).astype(bf16))
            ghost = blocks + (which + 1) % 3 * size + tile
            value = totals[ghost * 8 : ghost * 8 + 8, :]
            high = value.astype(bf16).astype(f32)
            both = jnp.concatenate([high, value - high], axis=0)
            source = jnp.broadcast_to(index // LANES, (ROWS, LANES))
            lefts.append(
                jnp.concatenate(
                    [
                        jnp.where(source == block, both, 0.0).astype(bf16)
                        for block in range(blocks)
                    ],
                    axis=0,
                )
            )
    added = dot_nt(jnp.concatenate(lefts, axis=1), jnp.concatenate(hots, axis=1))
    row_ids = lax.broadcasted_iota(jnp.int32, (8, LANES), 0)
    for block in range(blocks):
        columns = slice(block * LANES, (block + 1) * LANES)
        extra = added[block * ROWS : block * ROWS + 8] + added[block * ROWS + 8 : block * ROWS + 16]
        total = totals[block * 8 : block * 8 + 8, :] + extra
        radius = state[block, 9:10, :]
        mass = radius * radius * radius
        inertia = 0.4 * mass * radius * radius
        weight = jnp.where(row_ids < 3, time_step / mass, time_step / inertia)
        force[:, columns] = total[0:3]
        torque[:, columns] = total[3:6]
        kicked[:, columns] = state[block, 3:9, :] + (total * weight)[0:6]


def shape(*dims, dtype=f32):
    return jax.ShapeDtypeStruct(dims, dtype)


def body(positions, motion, radius, liquid, new_owner, ghost_rows, partner_tiles, live_pairs):
    per_dev = positions.shape[1]
    blocks = per_dev // LANES
    size = ghost_rows.shape[1] // LANES
    choices = partner_tiles.shape[0]
    tiles = -(-(blocks + 3 * size + 1) // 8) * 8
    slabs = lax.axis_size("slab")
    subs = lax.axis_size("sub")
    inside = [(i, i ^ 1) for i in range(slabs) if i ^ 1 < slabs]
    across = [(i, (i - 1 ^ 1) + 1) for i in range(1, slabs) if (i - 1 ^ 1) + 1 < slabs]

    state, swap_a, swap_b = pl.pallas_call(
        pack_kernel,
        out_shape=(
            shape(blocks + 1, ROWS, LANES),
            shape(CAP, ROWS, LANES),
            shape(CAP, ROWS, LANES),
        ),
        in_specs=[HBM] * 9,
        out_specs=(VMEM,) * 3,
        scratch_shapes=[
            pltpu.SMEM((blocks,), jnp.int32),
            pltpu.VMEM((3, per_dev), f32),
            pltpu.VMEM((6, per_dev), f32),
            pltpu.VMEM((blocks, LANES), f32),
            pltpu.VMEM((blocks, LANES), f32),
            pltpu.VMEM(ghost_rows.shape, jnp.int32),
            pltpu.VMEM(partner_tiles.shape, jnp.int32),
            pltpu.VMEM((1, blocks), jnp.int32),
            pltpu.VMEM((1, blocks), jnp.int32),
            pltpu.VMEM((blocks, ROWS, LANES), f32),
            pltpu.VMEM((CAP + 1, ROWS, LANES), f32),
            pltpu.VMEM((CAP + 1, ROWS, LANES), f32),
            pltpu.SemaphoreType.DMA((9,)),
        ],
        compiler_params=pltpu.CompilerParams(vmem_limit_bytes=60 * 1024 * 1024),
        name="pack",
    )(
        new_owner,
        positions,
        motion,
        radius.reshape(blocks, LANES),
        liquid.reshape(blocks, LANES),
        ghost_rows,
        partner_tiles,
        live_pairs.reshape(1, blocks),
        new_owner.reshape(1, blocks),
    )
    low = lax.ppermute(swap_a, "slab", inside)
    high = lax.ppermute(swap_b, "slab", across)
    early = pl.pallas_call(
        early_kernel,
        out_shape=(
            shape(blocks, 3 * ROWS, LANES),
            shape(blocks, 3 * FEATS, LANES, dtype=bf16),
        ),
        in_specs=[VMEM],
        out_specs=(VMEM, VMEM),
        compiler_params=PARAMS,
        cost_estimate=pl.CostEstimate(flops=4000000, bytes_accessed=1000000, transcendentals=0),
        name="early",
    )(state)
    to_a, to_b, to_sub, lean = pl.pallas_call(
        place_kernel,
        out_shape=(shape(blocks + size, ROWS, LANES),) * 3
        + (shape((blocks + size) * LEAN + 8, LANES),),
        in_specs=[VMEM] * 3 + [pl.BlockSpec(memory_space=pl.ANY)],
        out_specs=(VMEM,) * 4,
        compiler_params=PARAMS,
        name="place",
    )(state, high, low, early[0])
    from_a = lax.ppermute(to_a, "slab", inside)
    from_b = lax.ppermute(to_b, "slab", across)
    from_sub = [
        lax.ppermute(lean, "sub", [(i, i ^ d) for i in range(subs)])
        for d in reversed(range(1, subs))
    ]

    wides = [pltpu.VMEM((LANES, (len(WIDE_ROWS) + 2) * LANES), f32)] * GROUP

    def work(messages):
        room = choices * blocks * (1 + messages) + 2 * GROUP
        return [
            pltpu.VMEM((tiles * MATS * FEATS, LANES), f32),
            pltpu.VMEM((6 * ROWS, len(WIDE_ROWS) * LANES), bf16),
            pltpu.VMEM((room, ROWS, LANES), f32),
            pltpu.VMEM((8, LANES), jnp.int32),
            pltpu.SMEM((8, LANES), jnp.int32),
            pltpu.SMEM((room,), jnp.int32),
            pltpu.SemaphoreType.DMA(()),
        ] + wides + [pltpu.VMEM((MATS * LANES, 2 * LANES), bf16)] * GROUP

    totals, table = pl.pallas_call(
        slab_kernel,
        out_shape=(shape(tiles * 8, LANES), shape(tiles, 3 * ROWS, LANES)),
        in_specs=[VMEM] * 7,
        out_specs=(VMEM, VMEM),
        scratch_shapes=[
            pltpu.VMEM((tiles, 3 * FEATS, LANES), bf16),
            pltpu.SMEM((3 * choices * blocks + 2 * GROUP,), jnp.int32),
            pltpu.SMEM((blocks + 1,), jnp.int32),
        ]
        + work(2),
        compiler_params=PARAMS,
        cost_estimate=pl.CostEstimate(flops=90000000, bytes_accessed=400000, transcendentals=0),
        name="slab_pairs",
    )(to_a, to_b, to_sub, from_a, from_b, *early)
    return tuple(
        pl.pallas_call(
            sub_kernel,
            out_shape=(shape(3, per_dev), shape(3, per_dev), shape(6, per_dev)),
            in_specs=[VMEM] * (4 + len(from_sub)),
            out_specs=(VMEM,) * 3,
            scratch_shapes=[pltpu.VMEM((tiles * 8, LANES), f32)] + work(len(from_sub)),
            compiler_params=PARAMS,
            name="sub_pairs",
        )(totals, table, to_sub, state, *from_sub)
    )


def solution(mesh):
    return jax.shard_map(
        body,
        mesh=mesh,
        in_specs=(
            P(None, ("slab", "sub")),
            P(None, ("slab", "sub")),
            P(("slab", "sub")),
            P(("slab", "sub")),
            P(("slab", "sub")),
            P(None, ("slab", "sub")),
            P(None, ("slab", "sub")),
            P(("slab", "sub")),
        ),
        out_specs=(P(None, ("slab", "sub")), P(None, ("slab", "sub")), P(None, ("slab", "sub"))),
        check_vma=False,
    )
```
